128 devices in a mesh: gx: 8 (over z, core), gy: 16 (over y, x).
Axes of the slice: x: 4, y: 4, z: 4, core: 2. Of those that a mesh axis runs over, the one named last changes fastest.
Arguments:
- state_path: float32 [2, 128, 256, 256], P(None, 'gx', 'gy'), may hold values from -6 to 6
- velocity: float32 [3, 128, 256, 256], P(None, 'gx', 'gy'), may hold values from -6 to 6
- weights: bfloat16 [2, 4, 128, 256, 256], P(None, None, 'gx', 'gy'), may hold values from -0.25 to 0.75
- owners: int32 [2, 8, 16, 256, 1], P(None, 'gx', 'gy'), may hold values from 0 to 127; in each aligned block of 256 rows (0 to 255, 256 to 511, ..., all dimensions but the last counted through in order) at most 6 rows name the same one
- sources: int32 [2, 8, 16, 256], P(None, 'gx', 'gy'), may hold values from 0 to 255
Outputs:
- hessian_action: float32 [3, 128, 256, 256], P(None, 'gx', 'gy')
The draws below stay inside these ranges and needn't reach their ends.
Inputs may be any that keep to these rules, and one draw needn't show every extreme that they name: `owners`: in each step, of the 256 columns of one device at most 6 name any one owner, and in every draw some device's columns name one owner exactly 6 times.
All inputs are finite; a program needn't handle non-finite values.
Results may differ from the reference program's by a relative error of at most 0.0003.
Values sent between devices are 32-bit elements; how exact they have to be, the bound alone decides.
No kernel may reach another device: no remote copies, remote signals or barrier semaphores. Data moves between devices by JAX's collectives and lax.ppermute only.
A program may use at most 64 MiB of HBM per device.

```python
import math
import jax
import jax.numpy as jnp
import numpy as np

CX = 16
CY = 16
NZ = 256
STEPS = 2
XGROUPS = 8
YGROUPS = 16
C = 256
CAP = 6
NX = 128
NY = 256
DEVICES = 128


def plant(entries, own_key, smallest, largest):
    longest = entries.shape.index(max(entries.shape))
    spots = []
    for shift in (0, 1):
        where = [jax.random.randint(jax.random.fold_in(own_key, axis), (), 0, length) for axis, length in enumerate(entries.shape)]
        where[longest] = (where[longest] + shift) % entries.shape[longest]
        spots.append(tuple(where))
    return entries.at[spots[0]].set(smallest).at[spots[1]].set(largest)


def shard_levels(stream_key, extent, pieces, smallest, largest):
    factor_of = 1.0
    for position, parts in pieces:
        heights = jax.random.uniform(jax.random.fold_in(jax.random.fold_in(stream_key, 6), position), (parts,), jnp.float32, smallest / len(pieces), largest / len(pieces))
        factor_of = factor_of * jnp.repeat(jnp.exp(heights), extent[position] // parts).reshape((-1,) + (1,) * (len(extent) - 1 - position))
    return factor_of


def shared_out(stream_key, own, number, rows, count, top, limit, lean):
    sequence = jax.random.permutation(stream_key, count)
    packed, usual = portions_of(count, rows * top, limit, lean, True), portions_of(count, rows * top, limit, lean, False)
    places = jnp.arange(count)

    def named(lengths, turn):
        used = int((lengths > 0).sum())
        fixed = max(1, used // 4)
        passed = fixed + (places - fixed + turn * (used - fixed)) % max(1, count - fixed)
        return jnp.zeros((count,), jnp.int32).at[sequence[jnp.where(places < fixed, places, passed)]].set(jnp.asarray(lengths, jnp.int32))

    lengths = jnp.where(number % 4 == 0, named(packed, number // 4), named(usual, number - number // 4 - 1))
    mixed = jax.random.permutation(jax.random.fold_in(own, 3), count)
    giver, sink = mixed[0:count // 2 * 2:2], mixed[1:count // 2 * 2:2]
    room = jnp.minimum(lengths[giver] - 1, limit - lengths[sink]) // 2
    room = jnp.where((giver == sequence[0]) | (sink == sequence[0]) | (lengths[sink] == 0), 0, jnp.maximum(room, 0))
    passed = jax.random.randint(jax.random.fold_in(own, 4), (count // 2,), 0, 1 << 20) % (room + 1)
    lengths = lengths.at[giver].add(-passed).at[sink].add(passed)
    items = jnp.searchsorted(jnp.cumsum(lengths), jnp.arange(rows * top), side="right").astype(jnp.int32)
    table = items.reshape(top, rows).T
    table = table[jax.random.permutation(jax.random.fold_in(own, 1), rows)]
    turn = jax.random.randint(jax.random.fold_in(own, 2), (rows, 1), 0, top)
    return jnp.take_along_axis(table, (jnp.arange(top)[None, :] + turn) % top, axis=1)


def portions_of(amount, total, most, skew, full):
    weights = [(1 << 20) // math.isqrt(grade ** skew) + 1 for grade in range(1, amount + 1)]
    largest = most if full else min(most, max(-(-total // amount), total * weights[0] // sum(weights)))
    least = 1 if total - largest >= amount - 1 else 0
    counts, surplus = [largest] + [least] * (amount - 1), total - largest - least * (amount - 1)
    while surplus > 0:
        candidates = [i for i in range(1, amount) if counts[i] < largest] or [i for i in range(1, amount) if counts[i] < most]
        mass, remaining = sum([weights[i] for i in candidates]), surplus
        for i in candidates:
            more = min(most - counts[i], max(1, remaining * weights[i] // mass), surplus)
            counts[i] = counts[i] + more
            surplus = surplus - more
    return np.array(counts)


def gaussian(stream_key, dims, deviation, bound, pieces=(), kind=jnp.bfloat16):
    entries = deviation * jax.random.normal(stream_key, dims, jnp.float32)
    if pieces:
        entries = entries * shard_levels(stream_key, dims, pieces, -0.22, 0.18)
    return jnp.clip(entries, -bound, bound).astype(kind)


def setup_inputs(seed: int = 0) -> dict:
    streams_of = jax.random.split(jax.random.key(seed), 6)
    state_path = gaussian(streams_of[0], (STEPS, NX, NY, NZ), 1.0, 6.0, ((1, 8), (2, 16)), jnp.float32)
    velocity = gaussian(streams_of[1], (3, NX, NY, NZ), 1.0, 6.0, ((1, 8), (2, 16)), jnp.float32)
    weights = jnp.clip(-0.25 + 1.0 * jax.random.uniform(streams_of[2], (STEPS, 4, NX, NY, NZ), jnp.float32) ** shard_levels(streams_of[2], (STEPS, 4, NX, NY, NZ), ((2, 8), (3, 16)), -0.2, 0.2), -0.25, 0.75).astype(jnp.bfloat16)
    owners_keys = jax.random.split(jax.random.fold_in(streams_of[3], 1), STEPS * XGROUPS * YGROUPS * C // C)
    owners_turns = jax.random.permutation(jax.random.fold_in(streams_of[3], 3), STEPS * XGROUPS * YGROUPS * C // C)
    owners = jax.vmap(lambda own, number: shared_out(jax.random.fold_in(streams_of[3], 2), own, number, C, DEVICES, 1, CAP, 2))(owners_keys, owners_turns).reshape((STEPS, XGROUPS, YGROUPS, C, 1))
    sources = plant(jax.random.randint(streams_of[4], (STEPS, XGROUPS, YGROUPS, C), 0, C), jax.random.fold_in(streams_of[4], 1), 0, C - 1).astype(jnp.int32)
    return {"state_path": state_path, "velocity": velocity, "weights": weights, "owners": owners, "sources": sources}


FIRST = (0.8, -0.2, 4.0 / 105.0, -1.0 / 280.0)
SECOND = (-205.0 / 72.0, 1.6, -0.2, 8.0 / 315.0, -1.0 / 560.0)
BETA = 0.05


def derive(field, axis):
    out = jnp.zeros_like(field)
    for k in range(4):
        out = out + FIRST[k] * (jnp.roll(field, -(k + 1), axis) - jnp.roll(field, k + 1, axis))
    return out


def laplace(field):
    out = 3.0 * SECOND[0] * field
    for axis in range(3):
        for k in range(4):
            out = out + SECOND[k + 1] * (jnp.roll(field, -(k + 1), axis) + jnp.roll(field, k + 1, axis))
    return out


def to_cols(field):
    blocks = field.reshape(XGROUPS, CX, YGROUPS, CY, NZ).transpose(0, 2, 1, 3, 4)
    return blocks.reshape(XGROUPS * YGROUPS * C, NZ)


def from_cols(cols):
    blocks = cols.reshape(XGROUPS, YGROUPS, CX, CY, NZ).transpose(0, 2, 1, 3, 4)
    return blocks.reshape(NX, NY, NZ)


def reference(state_path, velocity, weights, owners, sources):
    step_len = 1.0 / STEPS
    slopes = []
    flats = []
    moved = jnp.zeros((XGROUPS * YGROUPS * C, NZ), jnp.float32)
    for j in range(STEPS):
        state = state_path[j]
        slope = [derive(state, 0), derive(state, 1), derive(state, 2)]
        slopes.append(slope)
        flat = (owners[j, :, :, :, 0].reshape(-1) * C + sources[j].reshape(-1)).astype(jnp.int32)
        flats.append(flat)
        source_term = -(velocity[0] * slope[0] + velocity[1] * slope[1] + velocity[2] * slope[2])
        before = moved + step_len * to_cols(source_term)
        pulled = before[flat]
        total = jnp.zeros_like(pulled)
        for k in range(4):
            total = total + to_cols(weights[j, k].astype(jnp.float32)) * jnp.roll(pulled, 1 - k, axis=1)
        moved = total
    adjoint = moved
    hess = [BETA * (-laplace(velocity[c])) for c in range(3)]
    for j in range(STEPS - 1, -1, -1):
        spread = jnp.zeros_like(adjoint)
        for k in range(4):
            spread = spread + jnp.roll(to_cols(weights[j, k].astype(jnp.float32)) * adjoint, k - 1, axis=1)
        adjoint = jnp.zeros_like(adjoint).at[flats[j]].add(spread)
        field = from_cols(adjoint)
        hess = [hess[c] - step_len * field * slopes[j][c] for c in range(3)]
    return jnp.stack(hess, axis=0)
```

```python
import jax
import jax.numpy as jnp
from jax import lax
from jax.experimental import pallas as pl
from jax.experimental.pallas import tpu as pltpu
from jax.sharding import PartitionSpec as P

FIRST = (0.8, -0.2, 4.0 / 105.0, -1.0 / 280.0)
SECOND = (-205.0 / 72.0, 1.6, -0.2, 8.0 / 315.0, -1.0 / 560.0)
BETA = 0.05
AXES = ("gx", "gy")
CAP = 6
DEV = 128
COLS = 256
NZ = 256
F32 = jnp.float32
BF16 = jnp.bfloat16
W_ROWS = CAP * 8
A_ROWS = W_ROWS + 1
V_ROWS = CAP * 2


def params(mib):
    return pltpu.CompilerParams(vmem_limit_bytes=mib * 1024 * 1024)


def call(kernel, out_shape, mib, micros, **kw):
    return pl.pallas_call(
        kernel,
        out_shape=out_shape,
        compiler_params=params(mib),
        cost_estimate=pl.CostEstimate(
            flops=int(micros * 1e8), bytes_accessed=int(micros * 2e6), transcendentals=0
        ),
        **kw,
    )


def iota(shape, dim):
    return lax.broadcasted_iota(jnp.int32, shape, dim)


def split3(x):
    hi = x.astype(BF16)
    rest = x - hi.astype(F32)
    mid = rest.astype(BF16)
    low = (rest - mid.astype(F32)).astype(BF16)
    return hi, mid, low


def select(onehot, x):
    return sum(jnp.dot(onehot, part, preferred_element_type=F32) for part in split3(x))


def slots_row(owner_col, owner_row):
    earlier = (owner_col == owner_row) & (iota((COLS, COLS), 0) < iota((COLS, COLS), 1))
    return jnp.sum(earlier.astype(jnp.int32), axis=0, keepdims=True)


def slots_col(owner_col, owner_row):
    earlier = (owner_col == owner_row) & (iota((COLS, COLS), 1) < iota((COLS, COLS), 0))
    return jnp.sum(earlier.astype(jnp.int32), axis=1, keepdims=True)


def place_mask(owner_row, slot_row, s):
    return (iota((DEV, COLS), 0) == owner_row) & (slot_row == s)


def request_kernel(oc_ref, or_ref, sr_ref, w_ref, out_ref):
    lane = iota((DEV, 128), 1)
    wanted = jnp.zeros((DEV, 128), F32)
    for j in range(2):
        owner_row = or_ref[j : j + 1, :]
        slot_row = slots_row(oc_ref[j], owner_row)
        source_row = sr_ref[j : j + 1, :].astype(F32)
        masks = [place_mask(owner_row, slot_row, s) for s in range(CAP)]
        for s in range(CAP):
            column = jnp.sum(jnp.where(masks[s], source_row, 0.0), axis=1, keepdims=True)
            wanted = jnp.where(lane == 8 * j + s, column, wanted)
        if j == 1:
            onehot = jnp.concatenate([m.astype(BF16) for m in masks], axis=0)
            for k in range(4):
                weight = w_ref[0, k].reshape(COLS, NZ)
                placed = jnp.dot(onehot, weight, preferred_element_type=F32)
                for s in range(CAP):
                    for half in range(2):
                        row = s * 8 + k * 2 + half
                        out_ref[pl.ds(row, DEV, stride=A_ROWS), :] = placed[
                            s * DEV : (s + 1) * DEV, half * 128 : half * 128 + 128
                        ]
    out_ref[pl.ds(W_ROWS, DEV, stride=A_ROWS), :] = wanted


def stencil_kernel(st_ref, ve_ref, xlo_ref, xhi_ref, ylo_ref, yhi_ref, g_ref, b_ref, h_ref, xpad, ypad):
    step_len = 0.5
    for field in range(5):
        source = st_ref.at[field] if field < 2 else ve_ref.at[field - 2]
        xpad[0:4] = xlo_ref[field]
        xpad[4:20] = source[...]
        xpad[20:24] = xhi_ref[field]
        ypad[:, 4:8] = ylo_ref[field]
        ypad[:, 8:24] = source[...]
        ypad[:, 24:28] = yhi_ref[field]

        def row(x, carry, field=field):
            centre = xpad[x + 4]
            sign = -1.0 if field < 2 else 1.0
            parts = [jnp.zeros_like(centre) for _ in range(3)]
            coeffs = FIRST if field < 2 else SECOND[1:]
            for k in range(4):
                d = k + 1
                parts[0] += coeffs[k] * (xpad[x + 4 + d] + sign * xpad[x + 4 - d])
                parts[1] += coeffs[k] * (ypad[x, 8 + d : 24 + d, :] + sign * ypad[x, 8 - d : 24 - d, :])
                parts[2] += coeffs[k] * (
                    pltpu.roll(centre, NZ - d, 1) + sign * pltpu.roll(centre, d, 1)
                )
            if field < 2:
                for c in range(3):
                    g_ref[field, c, x] = parts[c]
                dot = ve_ref[0, x] * parts[0] + ve_ref[1, x] * parts[1] + ve_ref[2, x] * parts[2]
                b_ref[field, x] = -step_len * dot
            else:
                total = 3.0 * SECOND[0] * centre + parts[0] + parts[1] + parts[2]
                h_ref[field - 2, x] = -BETA * total
            return carry

        lax.fori_loop(0, 16, row, 0)


def supply_kernel(idx_ref, b_ref, out_ref):
    wanted = idx_ref[:, 0, 0, :]
    place = iota((DEV, COLS), 1).astype(F32)
    onehot = jnp.concatenate(
        [(wanted[:, s : s + 1] == place).astype(BF16) for s in range(CAP)], axis=0
    )
    values = select(onehot, b_ref[0])
    for s in range(CAP):
        for half in range(2):
            out_ref[pl.ds(s * 2 + half, DEV, stride=V_ROWS), :] = values[
                s * DEV : (s + 1) * DEV, half * 128 : half * 128 + 128
            ]


def gathered_rows(wanted_t, first):
    place = iota((COLS, DEV), 0).astype(F32)
    return jnp.concatenate(
        [(place == wanted_t[first + s : first + s + 1, :]).astype(BF16) for s in range(CAP)], axis=1
    )


def normal_kernel(a_ref, d_ref, wt_ref, w_scr):
    wanted_t = a_ref[pl.ds(W_ROWS, DEV, stride=A_ROWS), :].T
    wt_ref[...] = wanted_t[:16]
    onehot_t = gathered_rows(wanted_t, 8)
    for k in range(4):
        for s in range(CAP):
            for half in range(2):
                w_scr[k, s * DEV : (s + 1) * DEV, half * 128 : half * 128 + 128] = a_ref[
                    pl.ds(s * 8 + k * 2 + half, DEV, stride=A_ROWS), :
                ]
    for m in range(4):
        total = None
        for k in range(4 - m):
            product = w_scr[k] * w_scr[k + m]
            high = product.astype(BF16)
            low = (product - high.astype(F32)).astype(BF16)
            part = jnp.dot(onehot_t, high, preferred_element_type=F32) + jnp.dot(
                onehot_t, low, preferred_element_type=F32
            )
            if k != 1:
                part = pltpu.roll(part, (k - 1) % NZ, 1)
            total = part if total is None else total + part
        d_ref[m] = total


def read_slots(ref):
    return jnp.concatenate(
        [
            jnp.concatenate(
                [ref[pl.ds(s * 2 + half, DEV, stride=V_ROWS), :] for half in range(2)], axis=1
            )
            for s in range(CAP)
        ],
        axis=0,
    )


def middle_kernel(arr_ref, oc_ref, or_ref, w_ref, b_ref, d_ref, lam_ref, out_ref):
    owner_col = oc_ref[0]
    owner_row = or_ref[0:1, :]
    slot_col = slots_col(owner_col, owner_row)
    slot_row = slots_row(owner_col, owner_row)
    lane = iota((COLS, DEV), 1)
    taken = jnp.concatenate(
        [((lane == owner_col) & (slot_col == s)).astype(BF16) for s in range(CAP)], axis=1
    )
    mine = select(taken, read_slots(arr_ref))
    weights = [w_ref[0, k].reshape(COLS, NZ).astype(F32) for k in range(4)]
    field = b_ref[0]
    for k in range(4):
        field += weights[k] * (mine if k == 1 else pltpu.roll(mine, (1 - k) % NZ, 1))
    lam = d_ref[0] * field
    for m in range(1, 4):
        lam += d_ref[m] * pltpu.roll(field, NZ - m, 1) + pltpu.roll(d_ref[m] * field, m, 1)
    lam_ref[...] = lam
    spread = weights[1] * lam
    for k in (0, 2, 3):
        spread += pltpu.roll(weights[k] * lam, (k - 1) % NZ, 1)
    onehot = jnp.concatenate(
        [place_mask(owner_row, slot_row, s).astype(BF16) for s in range(CAP)], axis=0
    )
    values = select(onehot, spread)
    for s in range(CAP):
        for half in range(2):
            out_ref[pl.ds(s * 2 + half, DEV, stride=V_ROWS), :] = values[
                s * DEV : (s + 1) * DEV, half * 128 : half * 128 + 128
            ]


def final_kernel(arr_ref, wt_ref, h_ref, g_ref, out_ref):
    onehot_t = gathered_rows(wt_ref[...], 0)
    lam = select(onehot_t, read_slots(arr_ref))
    for c in range(3):
        out_ref[c] = h_ref[c] - 0.5 * (lam * g_ref[0, c])


def exchange(value):
    return lax.all_to_all(value, AXES, split_axis=0, concat_axis=0, tiled=True)


def neighbours(first, last, axis):
    count = lax.axis_size(axis)
    up = [(i, (i + 1) % count) for i in range(count)]
    down = [(j, i) for i, j in up]
    return lax.ppermute(last, axis, up), lax.ppermute(first, axis, down)


def per_device(state_path, velocity, weights, owners, sources):
    owner_col = owners.reshape(2, COLS, 1)
    owner_row = owners.reshape(2, COLS)
    source_row = sources.reshape(2, COLS)
    whole = lambda *shape: pl.BlockSpec(shape, lambda i: (0,) * len(shape))
    weight_spec = lambda j: pl.BlockSpec((1, 4, 16, 16, NZ), lambda i: (j, 0, 0, 0, 0))
    struct = lambda *shape: jax.ShapeDtypeStruct(shape, F32)

    request = call(
        request_kernel,
        struct(DEV * A_ROWS, 128),
        20,
        3,
        grid=(1,),
        in_specs=[whole(2, COLS, 1), whole(2, COLS), whole(2, COLS), weight_spec(1)],
        out_specs=whole(DEV * A_ROWS, 128),
    )(owner_col, owner_row, source_row, weights)
    asked = exchange(request.reshape(DEV, A_ROWS, 1, 128))

    faces = lambda lo, hi, dim: jnp.concatenate(
        [lax.slice_in_dim(v, lo, hi, axis=dim) for v in (state_path, velocity)], axis=0
    )
    xlo, xhi = neighbours(faces(0, 4, 1), faces(12, 16, 1), "gx")
    ylo, yhi = neighbours(faces(0, 4, 2), faces(12, 16, 2), "gy")
    slopes, before, hess = call(
        stencil_kernel,
        (struct(2, 3, 16, 16, NZ), struct(2, 16, 16, NZ), struct(3, 16, 16, NZ)),
        20,
        6,
        scratch_shapes=[pltpu.VMEM((24, 16, NZ), F32), pltpu.VMEM((16, 32, NZ), F32)],
    )(state_path, velocity, xlo, xhi, ylo, yhi)
    slopes = slopes.reshape(2, 3, COLS, NZ)
    before = before.reshape(2, COLS, NZ)
    hess = hess.reshape(3, COLS, NZ)

    step_field = lambda j: pl.BlockSpec((1, COLS, NZ), lambda i: (j, 0, 0))
    supply = call(
        supply_kernel,
        struct(DEV * V_ROWS, 128),
        20,
        1,
        grid=(1,),
        in_specs=[pl.BlockSpec((DEV, 1, 1, 128), lambda i: (0, W_ROWS, 0, 0)), step_field(0)],
        out_specs=whole(DEV * V_ROWS, 128),
    )(asked, before)
    arrived = exchange(supply.reshape(DEV, CAP, 2, 128))

    normal, wanted_t = call(
        normal_kernel,
        (struct(4, COLS, NZ), struct(16, 128)),
        24,
        4,
        scratch_shapes=[pltpu.VMEM((4, CAP * DEV, NZ), F32)],
    )(asked.reshape(DEV * A_ROWS, 128))

    lam, push = call(
        middle_kernel,
        (struct(COLS, NZ), struct(DEV * V_ROWS, 128)),
        24,
        3,
        grid=(1,),
        in_specs=[
            whole(DEV * V_ROWS, 128),
            whole(2, COLS, 1),
            whole(2, COLS),
            weight_spec(0),
            step_field(1),
            whole(4, COLS, NZ),
        ],
        out_specs=(whole(COLS, NZ), whole(DEV * V_ROWS, 128)),
    )(arrived.reshape(DEV * V_ROWS, 128), owner_col, owner_row, weights, before, normal)
    returned = exchange(push.reshape(DEV, CAP, 2, 128))

    hess = hess - 0.5 * (lam[None] * slopes[1])
    out = call(
        final_kernel,
        struct(3, COLS, NZ),
        20,
        2,
        grid=(1,),
        in_specs=[
            whole(DEV * V_ROWS, 128),
            whole(16, 128),
            whole(3, COLS, NZ),
            pl.BlockSpec((1, 3, COLS, NZ), lambda i: (0, 0, 0, 0)),
        ],
        out_specs=whole(3, COLS, NZ),
    )(returned.reshape(DEV * V_ROWS, 128), wanted_t, hess, slopes)
    return out.reshape(3, 16, 16, NZ)


def solution(mesh):
    return jax.shard_map(
        per_device,
        mesh=mesh,
        in_specs=(
            P(None, "gx", "gy", None),
            P(None, "gx", "gy", None),
            P(None, None, "gx", "gy", None),
            P(None, "gx", "gy", None, None),
            P(None, "gx", "gy", None),
        ),
        out_specs=P(None, "gx", "gy", None),
        check_vma=False,
    )
```

```python
import jax
import jax.numpy as jnp
from jax import lax
from jax.experimental import pallas as pl
from jax.experimental.pallas import tpu as pltpu
from jax.sharding import PartitionSpec as P

FIRST = (0.8, -0.2, 4.0 / 105.0, -1.0 / 280.0)
SECOND = (-205.0 / 72.0, 1.6, -0.2, 8.0 / 315.0, -1.0 / 560.0)
BETA = 0.05
AXES = ("gx", "gy")
CAP = 6
DEV = 128
COLS = 256
NZ = 256
F32 = jnp.float32
BF16 = jnp.bfloat16
W_ROWS = CAP * 8
A_ROWS = W_ROWS + 1
V_ROWS = CAP * 2
PART = 32


def call(kernel, out_shape, mib, micros, **kw):
    return pl.pallas_call(
        kernel,
        out_shape=out_shape,
        compiler_params=pltpu.CompilerParams(vmem_limit_bytes=mib * 1024 * 1024),
        cost_estimate=pl.CostEstimate(
            flops=int(micros * 1e8), bytes_accessed=int(micros * 2e6), transcendentals=0
        ),
        **kw,
    )


def iota(shape, dim):
    return lax.broadcasted_iota(jnp.int32, shape, dim)


def dot(a, b):
    return jnp.dot(a, b, preferred_element_type=F32)


def split3(x):
    hi = x.astype(BF16)
    rest = x - hi.astype(F32)
    mid = rest.astype(BF16)
    low = (rest - mid.astype(F32)).astype(BF16)
    return hi, mid, low


def select(onehot, parts):
    return sum(dot(onehot, part) for part in parts)


def ones(mask):
    return jnp.where(mask, 1.0, 0.0).astype(BF16)


def masks_by_owner(owner_row, first, count):
    match = iota((count, COLS), 0) + first == owner_row
    before = ones(iota((COLS, COLS), 0) < iota((COLS, COLS), 1))
    slot = dot(ones(match), before)
    return [match & (slot == float(s)) for s in range(CAP)]


def masks_by_column(owner_row):
    spread = jnp.broadcast_to(owner_row.astype(F32), (DEV, COLS)).T
    match = iota((COLS, DEV), 1).astype(F32) == spread
    before = ones(iota((COLS, COLS), 1) < iota((COLS, COLS), 0))
    slot = dot(before, ones(match))
    return [match & (slot == float(s)) for s in range(CAP)]


def put_slots(out_ref, start, values, count):
    for s in range(CAP):
        for half in range(2):
            out_ref[pl.ds(start + s * 2 + half, count, stride=V_ROWS), :] = values[
                s * count : (s + 1) * count, half * 128 : half * 128 + 128
            ]


def request_kernel(or_ref, sr_ref, w_ref, out_ref):
    first = pl.program_id(0) * PART
    lane = iota((PART, 128), 1)
    wanted = jnp.zeros((PART, 128), F32)
    for j in range(2):
        masks = masks_by_owner(or_ref[j], first, PART)
        source_row = sr_ref[j].astype(F32)
        for s in range(CAP):
            column = jnp.sum(jnp.where(masks[s], source_row, 0.0), axis=1, keepdims=True)
            wanted = jnp.where(lane == 8 * j + s, column, wanted)
    onehot = jnp.concatenate([ones(m) for m in masks], axis=0)
    for k in range(4):
        placed = dot(onehot, w_ref[0, k].reshape(COLS, NZ))
        for s in range(CAP):
            for half in range(2):
                out_ref[pl.ds(s * 8 + k * 2 + half, PART, stride=A_ROWS), :] = placed[
                    s * PART : (s + 1) * PART, half * 128 : half * 128 + 128
                ]
    out_ref[pl.ds(W_ROWS, PART, stride=A_ROWS), :] = wanted


def stencil_kernel(st_ref, ve_ref, xlo_ref, xhi_ref, ylo_ref, yhi_ref, g_ref, b_ref, h_ref, xpad, ypad):
    step_len = 0.5
    for field in range(5):
        source = st_ref.at[field] if field < 2 else ve_ref.at[field - 2]
        xpad[0:4] = xlo_ref[field]
        xpad[4:20] = source[...]
        xpad[20:24] = xhi_ref[field]
        ypad[:, 4:8] = ylo_ref[field]
        ypad[:, 8:24] = source[...]
        ypad[:, 24:28] = yhi_ref[field]

        def row(x, carry, field=field):
            centre = xpad[x + 4]
            sign = -1.0 if field < 2 else 1.0
            parts = [jnp.zeros_like(centre) for _ in range(3)]
            coeffs = FIRST if field < 2 else SECOND[1:]
            for k in range(4):
                d = k + 1
                parts[0] += coeffs[k] * (xpad[x + 4 + d] + sign * xpad[x + 4 - d])
                parts[1] += coeffs[k] * (ypad[x, 8 + d : 24 + d, :] + sign * ypad[x, 8 - d : 24 - d, :])
                parts[2] += coeffs[k] * (
                    pltpu.roll(centre, NZ - d, 1) + sign * pltpu.roll(centre, d, 1)
                )
            if field < 2:
                for c in range(3):
                    g_ref[field, c, x] = parts[c]
                dot = ve_ref[0, x] * parts[0] + ve_ref[1, x] * parts[1] + ve_ref[2, x] * parts[2]
                b_ref[field, x] = -step_len * dot
            else:
                total = 3.0 * SECOND[0] * centre + parts[0] + parts[1] + parts[2]
                h_ref[field - 2, x] = -BETA * total
            return carry

        lax.fori_loop(0, 16, row, 0)


def supply_kernel(idx_ref, b_ref, out_ref):
    wanted = idx_ref[:, 0, 0, :]
    place = iota((PART, COLS), 1).astype(F32)
    onehot = jnp.concatenate([ones(wanted[:, s : s + 1] == place) for s in range(CAP)], axis=0)
    put_slots(out_ref, 0, select(onehot, split3(b_ref[0])), PART)


def gathered_rows(wanted_t, first):
    place = iota((COLS, DEV), 0).astype(F32)
    return jnp.concatenate(
        [ones(place == wanted_t[first + s : first + s + 1, :]) for s in range(CAP)], axis=1
    )


def normal_kernel(a_ref, d_ref, wt_ref, w_scr):
    wanted_t = a_ref[pl.ds(W_ROWS, DEV, stride=A_ROWS), :].T
    wt_ref[...] = wanted_t[:16]
    onehot_t = gathered_rows(wanted_t, 8)
    for k in range(4):
        for s in range(CAP):
            for half in range(2):
                w_scr[k, s * DEV : (s + 1) * DEV, half * 128 : half * 128 + 128] = a_ref[
                    pl.ds(s * 8 + k * 2 + half, DEV, stride=A_ROWS), :
                ]
    for m in range(4):
        total = None
        for k in range(4 - m):
            product = w_scr[k] * w_scr[k + m]
            high = product.astype(BF16)
            low = (product - high.astype(F32)).astype(BF16)
            part = dot(onehot_t, high) + dot(onehot_t, low)
            if k != 1:
                part = pltpu.roll(part, (k - 1) % NZ, 1)
            total = part if total is None else total + part
        d_ref[m] = total


def read_slots(ref):
    return jnp.concatenate(
        [
            jnp.concatenate(
                [ref[pl.ds(s * 2 + half, DEV, stride=V_ROWS), :] for half in range(2)], axis=1
            )
            for s in range(CAP)
        ],
        axis=0,
    )


def middle_kernel(arr_hbm, own_hbm, w_hbm, b_hbm, d_hbm, lam_hbm, out_hbm, arr, own, w, b, d, lam_scr, out, parts, sems):
    copies = [
        pltpu.make_async_copy(source, target, sems.at[i])
        for i, (source, target) in enumerate(
            ((own_hbm.at[0], own), (arr_hbm, arr), (w_hbm.at[0], w), (b_hbm.at[1], b), (d_hbm, d))
        )
    ]
    for copy in copies:
        copy.start()
    copies[0].wait()
    owner_row = own[...]
    taken = jnp.concatenate([ones(m) for m in masks_by_column(owner_row)], axis=1)
    masks = masks_by_owner(owner_row, 0, DEV)
    copies[1].wait()
    mine_all = select(taken, split3(read_slots(arr)))
    for copy in copies[2:]:
        copy.wait()
    rows = 64
    for start in range(0, COLS, rows):
        here = slice(start, start + rows)
        mine = mine_all[here]
        weights = [
            w[k, start // 16 : (start + rows) // 16].reshape(rows, NZ).astype(F32) for k in range(4)
        ]
        field = b[here]
        for k in range(4):
            field += weights[k] * (mine if k == 1 else pltpu.roll(mine, (1 - k) % NZ, 1))
        lam = d[0, here] * field
        for m in range(1, 4):
            lam += d[m, here] * pltpu.roll(field, NZ - m, 1) + pltpu.roll(d[m, here] * field, m, 1)
        lam_scr[here] = lam
        spread = weights[1] * lam
        for k in (0, 2, 3):
            spread += pltpu.roll(weights[k] * lam, (k - 1) % NZ, 1)
        for i, part in enumerate(split3(spread)):
            parts[i, here] = part
    lam_copy = pltpu.make_async_copy(lam_scr, lam_hbm, sems.at[0])
    lam_copy.start()
    sent = []
    for i, first in enumerate(range(0, DEV, PART)):
        onehot = jnp.concatenate([ones(m[first : first + PART]) for m in masks], axis=0)
        values = select(onehot, [parts[p] for p in range(3)])
        put_slots(out, first * V_ROWS, values, PART)
        block = pl.ds(first * V_ROWS, PART * V_ROWS)
        copy = pltpu.make_async_copy(out.at[block], out_hbm.at[block], sems.at[1 + i])
        copy.start()
        sent.append(copy)
    lam_copy.wait()
    for copy in sent:
        copy.wait()


def final_kernel(arr_hbm, wt_hbm, h_hbm, g_hbm, out_hbm, arr, wt, h, g, out, sems):
    copies = [
        pltpu.make_async_copy(source, target, sems.at[i])
        for i, (source, target) in enumerate(
            ((wt_hbm, wt), (arr_hbm, arr), (h_hbm, h), (g_hbm.at[0], g))
        )
    ]
    for copy in copies:
        copy.start()
    copies[0].wait()
    onehot_t = gathered_rows(wt[...], 0)
    copies[1].wait()
    lam = select(onehot_t, split3(read_slots(arr)))
    copies[2].wait()
    copies[3].wait()
    sent = []
    for c in range(3):
        out[c] = h[c] - 0.5 * (lam * g[c])
        copy = pltpu.make_async_copy(out.at[c], out_hbm.at[c], sems.at[c])
        copy.start()
        sent.append(copy)
    for copy in sent:
        copy.wait()


def exchange(value):
    return lax.all_to_all(value, AXES, split_axis=0, concat_axis=0, tiled=True)


def neighbours(first, last, axis):
    count = lax.axis_size(axis)
    up = [(i, (i + 1) % count) for i in range(count)]
    down = [(j, i) for i, j in up]
    return lax.ppermute(last, axis, up), lax.ppermute(first, axis, down)


def per_device(state_path, velocity, weights, owners, sources):
    owner_row = owners.reshape(2, 1, COLS)
    source_row = sources.reshape(2, 1, COLS)
    whole = lambda *shape: pl.BlockSpec(shape, lambda i: (0,) * len(shape))
    blocks = lambda *shape: pl.BlockSpec(shape, lambda i: (i,) + (0,) * (len(shape) - 1))
    hbm = pl.BlockSpec(memory_space=pltpu.HBM)
    struct = lambda *shape: jax.ShapeDtypeStruct(shape, F32)

    faces = lambda lo, hi, dim: jnp.concatenate(
        [lax.slice_in_dim(v, lo, hi, axis=dim) for v in (state_path, velocity)], axis=0
    )
    xlo, xhi = neighbours(faces(0, 4, 1), faces(12, 16, 1), "gx")
    ylo, yhi = neighbours(faces(0, 4, 2), faces(12, 16, 2), "gy")

    request = call(
        request_kernel,
        struct(DEV * A_ROWS, 128),
        60,
        3,
        grid=(DEV // PART,),
        in_specs=[
            whole(2, 1, COLS),
            whole(2, 1, COLS),
            pl.BlockSpec((1, 4, 16, 16, NZ), lambda i: (1, 0, 0, 0, 0)),
        ],
        out_specs=blocks(PART * A_ROWS, 128),
    )(owner_row, source_row, weights)
    request, xlo, xhi, ylo, yhi = lax.optimization_barrier((request, xlo, xhi, ylo, yhi))
    asked = exchange(request.reshape(DEV, A_ROWS, 1, 128))

    slopes, before, hess = call(
        stencil_kernel,
        (struct(2, 3, 16, 16, NZ), struct(2, 16, 16, NZ), struct(3, 16, 16, NZ)),
        24,
        9,
        scratch_shapes=[pltpu.VMEM((24, 16, NZ), F32), pltpu.VMEM((16, 32, NZ), F32)],
    )(state_path, velocity, xlo, xhi, ylo, yhi)
    slopes = slopes.reshape(2, 3, COLS, NZ)
    before = before.reshape(2, COLS, NZ)
    hess = hess.reshape(3, COLS, NZ)

    supply = call(
        supply_kernel,
        struct(DEV * V_ROWS, 128),
        60,
        2,
        grid=(DEV // PART,),
        in_specs=[
            pl.BlockSpec((PART, 1, 1, 128), lambda i: (i, W_ROWS, 0, 0)),
            pl.BlockSpec((1, COLS, NZ), lambda i: (0, 0, 0)),
        ],
        out_specs=blocks(PART * V_ROWS, 128),
    )(asked, before)
    arrived = exchange(supply.reshape(DEV, CAP, 2, 128))

    normal, wanted_t = call(
        normal_kernel,
        (struct(4, COLS, NZ), struct(16, 128)),
        60,
        4,
        grid=(1,),
        in_specs=[whole(DEV * A_ROWS, 128)],
        out_specs=(whole(4, COLS, NZ), whole(16, 128)),
        scratch_shapes=[pltpu.VMEM((4, CAP * DEV, NZ), F32)],
    )(asked.reshape(DEV * A_ROWS, 128))

    lam, push = call(
        middle_kernel,
        (struct(COLS, NZ), struct(DEV * V_ROWS, 128)),
        60,
        4,
        in_specs=[hbm] * 5,
        out_specs=(hbm, hbm),
        scratch_shapes=[
            pltpu.VMEM((DEV * V_ROWS, 128), F32),
            pltpu.VMEM((1, COLS), jnp.int32),
            pltpu.VMEM((4, 16, 16, NZ), BF16),
            pltpu.VMEM((COLS, NZ), F32),
            pltpu.VMEM((4, COLS, NZ), F32),
            pltpu.VMEM((COLS, NZ), F32),
            pltpu.VMEM((DEV * V_ROWS, 128), F32),
            pltpu.VMEM((3, COLS, NZ), BF16),
            pltpu.SemaphoreType.DMA((5,)),
        ],
    )(arrived.reshape(DEV * V_ROWS, 128), owner_row, weights, before, normal)
    returned = exchange(push.reshape(DEV, CAP, 2, 128))

    hess = hess - 0.5 * (lam[None] * slopes[1])
    out = call(
        final_kernel,
        struct(3, COLS, NZ),
        60,
        2,
        in_specs=[hbm] * 4,
        out_specs=hbm,
        scratch_shapes=[
            pltpu.VMEM((DEV * V_ROWS, 128), F32),
            pltpu.VMEM((16, 128), F32),
            pltpu.VMEM((3, COLS, NZ), F32),
            pltpu.VMEM((3, COLS, NZ), F32),
            pltpu.VMEM((3, COLS, NZ), F32),
            pltpu.SemaphoreType.DMA((4,)),
        ],
    )(returned.reshape(DEV * V_ROWS, 128), wanted_t, hess, slopes)
    return out.reshape(3, 16, 16, NZ)


def solution(mesh):
    return jax.shard_map(
        per_device,
        mesh=mesh,
        in_specs=(
            P(None, "gx", "gy", None),
            P(None, "gx", "gy", None),
            P(None, None, "gx", "gy", None),
            P(None, "gx", "gy", None, None),
            P(None, "gx", "gy", None),
        ),
        out_specs=P(None, "gx", "gy", None),
        check_vma=False,
    )
```

```python
import functools

import jax
import jax.numpy as jnp
from jax import lax
from jax.experimental import pallas as pl
from jax.experimental.pallas import tpu as pltpu
from jax.sharding import PartitionSpec as P

FIRST = (0.8, -0.2, 4.0 / 105.0, -1.0 / 280.0)
SECOND = (-205.0 / 72.0, 1.6, -0.2, 8.0 / 315.0, -1.0 / 560.0)
BETA = 0.05
AXES = ("gx", "gy")
CAP = 6
DEV = 128
COLS = 256
NZ = 256
F32 = jnp.float32
BF16 = jnp.bfloat16
W_ROWS = CAP * 8
A_ROWS = W_ROWS + 1
V_ROWS = CAP * 2
PART = 32


def call(kernel, out_shape, mib, micros, in_specs, **kw):
    run = pl.pallas_call(
        kernel,
        out_shape=out_shape,
        in_specs=in_specs,
        compiler_params=pltpu.CompilerParams(vmem_limit_bytes=mib * 1024 * 1024),
        cost_estimate=pl.CostEstimate(
            flops=int(micros * 1e8), bytes_accessed=int(micros * 2e6), transcendentals=0
        ),
        **kw,
    )

    def placed(*args):
        return run(
            *(
                pltpu.with_memory_space_constraint(x, pltpu.HBM) if spec.memory_space == pltpu.HBM else x
                for spec, x in zip(in_specs, args)
            )
        )

    return placed


def iota(shape, dim):
    return lax.broadcasted_iota(jnp.int32, shape, dim)


def dot(a, b):
    return jnp.dot(a, b, preferred_element_type=F32)


def split3(x):
    hi = x.astype(BF16)
    rest = x - hi.astype(F32)
    mid = rest.astype(BF16)
    low = (rest - mid.astype(F32)).astype(BF16)
    return hi, mid, low


def select(onehot, parts):
    return sum(dot(onehot, part) for part in parts)


def ones(mask):
    return jnp.where(mask, 1.0, 0.0).astype(BF16)


def masks_by_owner(owner_row, first, count):
    match = iota((count, COLS), 0) + first == owner_row
    before = ones(iota((COLS, COLS), 0) < iota((COLS, COLS), 1))
    slot = dot(ones(match), before)
    return [match & (slot == float(s)) for s in range(CAP)]


def masks_by_column(owner_row):
    spread = jnp.broadcast_to(owner_row.astype(F32), (DEV, COLS)).T
    match = iota((COLS, DEV), 1).astype(F32) == spread
    before = ones(iota((COLS, COLS), 1) < iota((COLS, COLS), 0))
    slot = dot(before, ones(match))
    return [match & (slot == float(s)) for s in range(CAP)]


def put_slots(out_ref, start, values, count):
    for s in range(CAP):
        for half in range(2):
            out_ref[pl.ds(start + s * 2 + half, count, stride=V_ROWS), :] = values[
                s * count : (s + 1) * count, half * 128 : half * 128 + 128
            ]


def start_all(pairs, sems, first=0):
    copies = [
        pltpu.make_async_copy(source, target, sems.at[first + i])
        for i, (source, target) in enumerate(pairs)
    ]
    for copy in copies:
        copy.start()
    return copies


def wait_all(copies):
    for copy in copies:
        copy.wait()


def request_kernel(own_hbm, src_hbm, w_hbm, out_hbm, own, src, w, out, sems):
    copies = start_all(((own_hbm, own), (src_hbm, src), (w_hbm.at[1], w)), sems)
    wait_all(copies[:2])
    lane = iota((DEV, 128), 1)
    wanted = jnp.zeros((DEV, 128), F32)
    for j in range(2):
        masks = masks_by_owner(own[j], 0, DEV)
        source_row = src[j].astype(F32)
        for s in range(CAP):
            column = jnp.sum(jnp.where(masks[s], source_row, 0.0), axis=1, keepdims=True)
            wanted = jnp.where(lane == 8 * j + s, column, wanted)
    out[pl.ds(W_ROWS, DEV, stride=A_ROWS), :] = wanted
    copies[2].wait()
    sent = []
    for i, first in enumerate(range(0, DEV, PART)):
        onehot = jnp.concatenate([ones(m[first : first + PART]) for m in masks], axis=0)
        for k in range(4):
            placed = dot(onehot, w[k].reshape(COLS, NZ))
            for s in range(CAP):
                for half in range(2):
                    row = first * A_ROWS + s * 8 + k * 2 + half
                    out[pl.ds(row, PART, stride=A_ROWS), :] = placed[
                        s * PART : (s + 1) * PART, half * 128 : half * 128 + 128
                    ]
        block = pl.ds(first * A_ROWS, PART * A_ROWS)
        sent += start_all(((out.at[block], out_hbm.at[block]),), sems, 3 + i)
    wait_all(sent)


def stencil_kernel(step, lap, st_hbm, ve_hbm, xlo, xhi, ylo, yhi, *refs):
    if lap:
        refs = refs[1:]
    outs, refs = refs[: 2 + lap], refs[2 + lap :]
    xpad, ypad, ve = refs[:3]
    results, sems = refs[3 : 5 + lap], refs[-1]
    sources = [st_hbm.at[step]] + [ve_hbm.at[c] for c in range(3)] * lap
    pairs = [(source, xpad.at[i, pl.ds(4, 16)]) for i, source in enumerate(sources)]
    pairs += [(source, ypad.at[i, :, pl.ds(8, 16)]) for i, source in enumerate(sources)]
    copies = start_all(pairs + [(ve_hbm, ve)] * (not lap), sems)
    for i in range(len(sources)):
        xpad[i, 0:4] = xlo[i]
        xpad[i, 20:24] = xhi[i]
        ypad[i, :, 4:8] = ylo[i]
        ypad[i, :, 24:28] = yhi[i]
    wait_all(copies)
    rows = 4

    def block(x):
        here = pl.ds(x, rows)

        def differences(i, coeffs, sign):
            centre = xpad[i, pl.ds(x + 4, rows)]
            parts = [None, None, None]
            for k in range(4):
                d = k + 1
                terms = (
                    xpad[i, pl.ds(x + 4 + d, rows)] + sign * xpad[i, pl.ds(x + 4 - d, rows)],
                    ypad[i, here, 8 + d : 24 + d, :] + sign * ypad[i, here, 8 - d : 24 - d, :],
                    pltpu.roll(centre, NZ - d, 2) + sign * pltpu.roll(centre, d, 2),
                )
                for c in range(3):
                    term = coeffs[k] * terms[c]
                    parts[c] = term if parts[c] is None else parts[c] + term
            return centre, parts

        slope = differences(0, FIRST, -1.0)[1]
        total = None
        for c in range(3):
            results[0][c, here] = slope[c]
            along = xpad[1 + c, pl.ds(x + 4, rows)] if lap else ve[c, here]
            total = along * slope[c] if total is None else total + along * slope[c]
        results[1][here] = -0.5 * total
        for c in range(3 * lap):
            centre, parts = differences(1 + c, SECOND[1:], 1.0)
            results[2][c, here] = -BETA * (3.0 * SECOND[0] * centre + parts[0] + parts[1] + parts[2])

    sent = []
    for first in (0, 8):
        pl.loop(first, first + 8, step=rows)(block)
        half = pl.ds(first, 8)
        pairs = [(results[0].at[:, half], outs[0].at[:, half]), (results[1].at[half], outs[1].at[half])]
        if lap:
            pairs.append((results[2].at[:, half], outs[2].at[:, half]))
        sent += start_all(pairs, sems, len(sent))
    wait_all(sent)


def supply_kernel(asked, b_hbm, out_hbm, b, out, sems):
    copies = start_all(((b_hbm, b),), sems)
    wanted = asked[pl.ds(W_ROWS, DEV, stride=A_ROWS), :]
    place = iota((PART, COLS), 1).astype(F32)
    onehots = [
        jnp.concatenate(
            [ones(wanted[first : first + PART, s : s + 1] == place) for s in range(CAP)], axis=0
        )
        for first in range(0, DEV, PART)
    ]
    wait_all(copies)
    parts = split3(b[...])
    sent = []
    for i, first in enumerate(range(0, DEV, PART)):
        put_slots(out, first * V_ROWS, select(onehots[i], parts), PART)
        here = pl.ds(first * V_ROWS, PART * V_ROWS)
        sent += start_all(((out.at[here], out_hbm.at[here]),), sems, 1 + i)
    wait_all(sent)


def gathered_rows(wanted_t, first):
    place = iota((COLS, DEV), 0).astype(F32)
    return jnp.concatenate(
        [ones(place == wanted_t[first + s : first + s + 1, :]) for s in range(CAP)], axis=1
    )


def normal_kernel(asked, d_hbm, wt_hbm, w, d, wt, sems):
    wanted_t = asked[pl.ds(W_ROWS, DEV, stride=A_ROWS), :].T
    wt[...] = wanted_t[:16]
    sent = start_all(((wt, wt_hbm),), sems)
    onehot_t = gathered_rows(wanted_t, 8)
    for k in range(4):
        for s in range(CAP):
            for half in range(2):
                w[k, s * DEV : (s + 1) * DEV, half * 128 : half * 128 + 128] = asked[
                    pl.ds(s * 8 + k * 2 + half, DEV, stride=A_ROWS), :
                ]
    for m in range(4):
        total = None
        for k in range(4 - m):
            product = w[k] * w[k + m]
            high = product.astype(BF16)
            low = (product - high.astype(F32)).astype(BF16)
            part = dot(onehot_t, high) + dot(onehot_t, low)
            if k != 1:
                part = pltpu.roll(part, (k - 1) % NZ, 1)
            total = part if total is None else total + part
        d[m] = total
        sent += start_all(((d.at[m], d_hbm.at[m]),), sems, 1 + m)
    wait_all(sent)


def read_slots(ref):
    return jnp.concatenate(
        [
            jnp.concatenate(
                [ref[pl.ds(s * 2 + half, DEV, stride=V_ROWS), :] for half in range(2)], axis=1
            )
            for s in range(CAP)
        ],
        axis=0,
    )


def middle_kernel(arr, own_hbm, w_hbm, b_hbm, d_hbm, lam_hbm, out_hbm, own, w, b, d, lam_scr, out, parts, sems):
    copies = start_all(((own_hbm.at[0], own), (w_hbm.at[0], w), (b_hbm, b), (d_hbm, d)), sems)
    copies[0].wait()
    owner_row = own[...]
    taken = jnp.concatenate([ones(m) for m in masks_by_column(owner_row)], axis=1)
    masks = masks_by_owner(owner_row, 0, DEV)
    mine_all = select(taken, split3(read_slots(arr)))
    wait_all(copies[1:])
    rows = 64
    for start in range(0, COLS, rows):
        here = slice(start, start + rows)
        mine = mine_all[here]
        weights = [
            w[k, start // 16 : (start + rows) // 16].reshape(rows, NZ).astype(F32) for k in range(4)
        ]
        field = b[here]
        for k in range(4):
            field += weights[k] * (mine if k == 1 else pltpu.roll(mine, (1 - k) % NZ, 1))
        lam = d[0, here] * field
        for m in range(1, 4):
            lam += d[m, here] * pltpu.roll(field, NZ - m, 1) + pltpu.roll(d[m, here] * field, m, 1)
        lam_scr[here] = lam
        spread = weights[1] * lam
        for k in (0, 2, 3):
            spread += pltpu.roll(weights[k] * lam, (k - 1) % NZ, 1)
        for i, part in enumerate(split3(spread)):
            parts[i, here] = part
    sent = start_all(((lam_scr, lam_hbm),), sems)
    for i, first in enumerate(range(0, DEV, PART)):
        onehot = jnp.concatenate([ones(m[first : first + PART]) for m in masks], axis=0)
        put_slots(out, first * V_ROWS, select(onehot, [parts[p] for p in range(3)]), PART)
        here = pl.ds(first * V_ROWS, PART * V_ROWS)
        sent += start_all(((out.at[here], out_hbm.at[here]),), sems, 1 + i)
    wait_all(sent)


def final_kernel(arr, wt_hbm, h_hbm, g_hbm, out_hbm, wt, h, g, out, sems):
    copies = start_all(((wt_hbm, wt), (h_hbm, h), (g_hbm, g)), sems)
    copies[0].wait()
    onehot_t = gathered_rows(wt[...], 0)
    lam = select(onehot_t, split3(read_slots(arr)))
    wait_all(copies[1:])
    sent = []
    for c in range(3):
        out[c] = h[c] - 0.5 * (lam * g[c])
        sent += start_all(((out.at[c], out_hbm.at[c]),), sems, c)
    wait_all(sent)


def exchange(value):
    return lax.all_to_all(value, AXES, split_axis=0, concat_axis=0, tiled=True)


def neighbours(first, last, axis):
    count = lax.axis_size(axis)
    up = [(i, (i + 1) % count) for i in range(count)]
    down = [(j, i) for i, j in up]
    return lax.ppermute(last, axis, up), lax.ppermute(first, axis, down)


def per_device(state_path, velocity, weights, owners, sources):
    owner_row = owners.reshape(2, 1, COLS)
    source_row = sources.reshape(2, 1, COLS)
    hbm = pl.BlockSpec(memory_space=pltpu.HBM)
    near = pl.BlockSpec(memory_space=pltpu.VMEM)
    struct = lambda *shape: pltpu.HBM(shape, F32)
    scratch = lambda *shape: pltpu.VMEM(shape, F32)
    sems = lambda count: pltpu.SemaphoreType.DMA((count,))
    per_field = lambda count: struct(count, 16, 16, NZ)

    request = call(
        request_kernel,
        struct(DEV * A_ROWS, 128),
        16,
        3,
        in_specs=[hbm] * 3,
        out_specs=hbm,
        scratch_shapes=[
            pltpu.VMEM((2, 1, COLS), jnp.int32),
            pltpu.VMEM((2, 1, COLS), jnp.int32),
            pltpu.VMEM((4, 16, 16, NZ), BF16),
            scratch(DEV * A_ROWS, 128),
            sems(7),
        ],
    )(owner_row, source_row, weights)
    asked = exchange(request.reshape(DEV, A_ROWS, 1, 128)).reshape(DEV * A_ROWS, 128)

    def halo(fields):
        xlo, xhi = neighbours(fields(slice(0, 4), slice(None)), fields(slice(12, 16), slice(None)), "gx")
        ylo, yhi = neighbours(fields(slice(None), slice(0, 4)), fields(slice(None), slice(12, 16)), "gy")
        return xlo, xhi, ylo, yhi

    slope0, before0 = call(
        functools.partial(stencil_kernel, 0, False),
        (per_field(3), struct(16, 16, NZ)),
        10,
        3,
        in_specs=[hbm] * 2 + [near] * 4,
        out_specs=(hbm, hbm),
        scratch_shapes=[
            scratch(1, 24, 16, NZ),
            scratch(1, 16, 32, NZ),
            scratch(3, 16, 16, NZ),
            scratch(3, 16, 16, NZ),
            scratch(16, 16, NZ),
            sems(4),
        ],
    )(state_path, velocity, *halo(lambda x, y: state_path[:1, x, y]))

    supply = call(
        supply_kernel,
        struct(DEV * V_ROWS, 128),
        8,
        2,
        in_specs=[near, hbm],
        out_specs=hbm,
        scratch_shapes=[scratch(COLS, NZ), scratch(DEV * V_ROWS, 128), sems(5)],
    )(asked, before0.reshape(COLS, NZ))
    arrived = exchange(supply.reshape(DEV, CAP, 2, 128)).reshape(DEV * V_ROWS, 128)

    later = halo(lambda x, y: jnp.concatenate([state_path[1:, x, y], velocity[:, x, y]], axis=0))
    slope1, before1, hess = call(
        functools.partial(stencil_kernel, 1, True),
        (per_field(3), struct(16, 16, NZ), per_field(3)),
        16,
        7,
        in_specs=[hbm] * 2 + [near] * 4 + [hbm],
        out_specs=(hbm, hbm, hbm),
        scratch_shapes=[
            scratch(4, 24, 16, NZ),
            scratch(4, 16, 32, NZ),
            scratch(8, 128),
            scratch(3, 16, 16, NZ),
            scratch(16, 16, NZ),
            scratch(3, 16, 16, NZ),
            sems(8),
        ],
    )(state_path, velocity, *later, supply)

    normal, wanted_t = call(
        normal_kernel,
        (struct(4, COLS, NZ), struct(16, 128)),
        20,
        4,
        in_specs=[near],
        out_specs=(hbm, hbm),
        scratch_shapes=[scratch(4, CAP * DEV, NZ), scratch(4, COLS, NZ), scratch(16, 128), sems(5)],
    )(asked)

    lam, push = call(
        middle_kernel,
        (struct(COLS, NZ), struct(DEV * V_ROWS, 128)),
        14,
        4,
        in_specs=[near] + [hbm] * 4,
        out_specs=(hbm, hbm),
        scratch_shapes=[
            pltpu.VMEM((1, COLS), jnp.int32),
            pltpu.VMEM((4, 16, 16, NZ), BF16),
            scratch(COLS, NZ),
            scratch(4, COLS, NZ),
            scratch(COLS, NZ),
            scratch(DEV * V_ROWS, 128),
            pltpu.VMEM((3, COLS, NZ), BF16),
            sems(5),
        ],
    )(arrived, owner_row, weights, before1.reshape(COLS, NZ), normal)
    returned = exchange(push.reshape(DEV, CAP, 2, 128)).reshape(DEV * V_ROWS, 128)

    hess = hess - 0.5 * (lam.reshape(1, 16, 16, NZ) * slope1)
    out = call(
        final_kernel,
        struct(3, COLS, NZ),
        14,
        2,
        in_specs=[near] + [hbm] * 3,
        out_specs=hbm,
        scratch_shapes=[
            scratch(16, 128),
            scratch(3, COLS, NZ),
            scratch(3, COLS, NZ),
            scratch(3, COLS, NZ),
            sems(3),
        ],
    )(returned, wanted_t, hess.reshape(3, COLS, NZ), slope0.reshape(3, COLS, NZ))
    return out.reshape(3, 16, 16, NZ)


def solution(mesh):
    return jax.shard_map(
        per_device,
        mesh=mesh,
        in_specs=(
            P(None, "gx", "gy", None),
            P(None, "gx", "gy", None),
            P(None, None, "gx", "gy", None),
            P(None, "gx", "gy", None, None),
            P(None, "gx", "gy", None),
        ),
        out_specs=P(None, "gx", "gy", None),
        check_vma=False,
    )
```

```python
import functools

import jax
import jax.numpy as jnp
from jax import lax
from jax.experimental import pallas as pl
from jax.experimental.pallas import tpu as pltpu
from jax.sharding import PartitionSpec as P

FIRST = (0.8, -0.2, 4.0 / 105.0, -1.0 / 280.0)
SECOND = (-205.0 / 72.0, 1.6, -0.2, 8.0 / 315.0, -1.0 / 560.0)
BETA = 0.05
AXES = ("gx", "gy")
CAP = 6
DEV = 128
COLS = 256
NZ = 256
F32 = jnp.float32
BF16 = jnp.bfloat16
W_ROWS = CAP * 8
A_ROWS = W_ROWS + 1
V_ROWS = CAP * 2
PART = 32


def call(kernel, out_shape, mib, micros, in_specs, **kw):
    run = pl.pallas_call(
        kernel,
        out_shape=out_shape,
        in_specs=in_specs,
        compiler_params=pltpu.CompilerParams(vmem_limit_bytes=mib * 1024 * 1024),
        cost_estimate=pl.CostEstimate(
            flops=int(micros * 1e8), bytes_accessed=int(micros * 2e6), transcendentals=0
        ),
        **kw,
    )

    def placed(*args):
        return run(
            *(
                pltpu.with_memory_space_constraint(x, pltpu.HBM) if spec.memory_space == pltpu.HBM else x
                for spec, x in zip(in_specs, args)
            )
        )

    return placed


def iota(shape, dim):
    return lax.broadcasted_iota(jnp.int32, shape, dim)


def dot(a, b):
    return jnp.dot(a, b, preferred_element_type=F32)


def split(x):
    hi = x.astype(BF16)
    return hi, (x - hi.astype(F32)).astype(BF16)


def select(onehot, parts):
    return sum(dot(onehot, part) for part in parts)


def ones(mask):
    return jnp.where(mask, 1.0, 0.0).astype(BF16)


def masks_by_owner(owner_row, first, count):
    match = iota((count, COLS), 0) + first == owner_row
    before = ones(iota((COLS, COLS), 0) < iota((COLS, COLS), 1))
    slot = dot(ones(match), before)
    return [match & (slot == float(s)) for s in range(CAP)]


def masks_by_column(owner_row):
    spread = jnp.broadcast_to(owner_row.astype(F32), (DEV, COLS)).T
    match = iota((COLS, DEV), 1).astype(F32) == spread
    before = ones(iota((COLS, COLS), 1) < iota((COLS, COLS), 0))
    slot = dot(before, ones(match))
    return [match & (slot == float(s)) for s in range(CAP)]


def put_slots(out_ref, start, values, count):
    for s in range(CAP):
        for half in range(2):
            out_ref[pl.ds(start + s * 2 + half, count, stride=V_ROWS), :] = values[
                s * count : (s + 1) * count, half * 128 : half * 128 + 128
            ]


def start_all(pairs, sems, first=0):
    copies = [
        pltpu.make_async_copy(source, target, sems.at[first + i])
        for i, (source, target) in enumerate(pairs)
    ]
    for copy in copies:
        copy.start()
    return copies


def wait_all(copies):
    for copy in copies:
        copy.wait()


def request_kernel(own_hbm, src_hbm, w_hbm, out_hbm, own, src, w, out, sems):
    copies = start_all(((own_hbm, own), (src_hbm, src), (w_hbm.at[1], w)), sems)
    wait_all(copies[:2])
    lane = iota((DEV, 128), 1)
    wanted = jnp.zeros((DEV, 128), F32)
    for j in range(2):
        masks = masks_by_owner(own[j], 0, DEV)
        source_row = src[j].astype(F32)
        for s in range(CAP):
            column = jnp.sum(jnp.where(masks[s], source_row, 0.0), axis=1, keepdims=True)
            wanted = jnp.where(lane == 8 * j + s, column, wanted)
    out[pl.ds(W_ROWS, DEV, stride=A_ROWS), :] = wanted
    copies[2].wait()
    sent = []
    for i, first in enumerate(range(0, DEV, PART)):
        onehot = jnp.concatenate([ones(m[first : first + PART]) for m in masks], axis=0)
        for k in range(4):
            placed = dot(onehot, w[k].reshape(COLS, NZ))
            for s in range(CAP):
                for half in range(2):
                    row = first * A_ROWS + s * 8 + k * 2 + half
                    out[pl.ds(row, PART, stride=A_ROWS), :] = placed[
                        s * PART : (s + 1) * PART, half * 128 : half * 128 + 128
                    ]
        block = pl.ds(first * A_ROWS, PART * A_ROWS)
        sent += start_all(((out.at[block], out_hbm.at[block]),), sems, 3 + i)
    wait_all(sent)


def fill(sources, halos, xpad, ypad, sems, extra=()):
    xlo, xhi, ylo, yhi = halos
    pairs = list(extra)
    for i, source in enumerate(sources):
        pairs += [(source, xpad.at[i, pl.ds(4, 16)]), (source, ypad.at[i, :, pl.ds(8, 16)])]
    copies = start_all(pairs, sems)
    for i in range(len(sources)):
        xpad[i, 0:4] = xlo[i]
        xpad[i, 20:24] = xhi[i]
        ypad[i, :, 4:8] = ylo[i]
        ypad[i, :, 24:28] = yhi[i]
    return copies


def differences(xpad, ypad, i, x, rows, coeffs, sign):
    centre = xpad[i, pl.ds(x + 4, rows)]
    parts = [None, None, None]
    for k in range(4):
        d = k + 1
        terms = (
            xpad[i, pl.ds(x + 4 + d, rows)] + sign * xpad[i, pl.ds(x + 4 - d, rows)],
            ypad[i, pl.ds(x, rows), 8 + d : 24 + d, :] + sign * ypad[i, pl.ds(x, rows), 8 - d : 24 - d, :],
            pltpu.roll(centre, NZ - d, 2) + sign * pltpu.roll(centre, d, 2),
        )
        for c in range(3):
            term = coeffs[k] * terms[c]
            parts[c] = term if parts[c] is None else parts[c] + term
    return centre, parts


ROWS = 4


def slope_kernel(step, st_hbm, ve_hbm, *refs):
    g_hbm, b_hbm, xpad, ypad, ve, g, b, sems = refs[-8:]
    wait_all(fill([st_hbm.at[step]], refs[:4], xpad, ypad, sems, [(ve_hbm, ve)]))

    def block(x):
        here = pl.ds(x, ROWS)
        slope = differences(xpad, ypad, 0, x, ROWS, FIRST, -1.0)[1]
        total = None
        for c in range(3):
            g[c, here] = slope[c]
            term = ve[c, here] * slope[c]
            total = term if total is None else total + term
        b[here] = -0.5 * total

    sent = []
    for first in (0, 8):
        pl.loop(first, first + 8, step=ROWS)(block)
        half = pl.ds(first, 8)
        pairs = ((b.at[half], b_hbm.at[half]), (g.at[:, half], g_hbm.at[:, half]))
        sent += start_all(pairs, sems, len(sent))
    wait_all(sent)


def curve_kernel(ve_hbm, xlo, xhi, ylo, yhi, lam_hbm, g_hbm, h_hbm, xpad, ypad, lam, g, h, sems):
    sources = [ve_hbm.at[c] for c in range(3)]
    extra = [(lam_hbm, lam), (g_hbm, g)]
    wait_all(fill(sources, (xlo, xhi, ylo, yhi), xpad, ypad, sems, extra))

    def block(x):
        here = pl.ds(x, ROWS)
        for c in range(3):
            centre, parts = differences(xpad, ypad, c, x, ROWS, SECOND[1:], 1.0)
            total = 3.0 * SECOND[0] * centre + parts[0] + parts[1] + parts[2]
            h[c, here] = -BETA * total - 0.5 * (lam[here] * g[c, here])

    pl.loop(0, 16, step=ROWS)(block)
    wait_all(start_all(((h, h_hbm),), sems))


def supply_kernel(asked, b_hbm, *refs):
    out_hbm, b, out, sems = refs[-4:]
    copies = start_all(((b_hbm, b),), sems)
    wanted = asked[pl.ds(W_ROWS, DEV, stride=A_ROWS), :]
    place = iota((PART, COLS), 1).astype(F32)
    onehots = [
        jnp.concatenate(
            [ones(wanted[first : first + PART, s : s + 1] == place) for s in range(CAP)], axis=0
        )
        for first in range(0, DEV, PART)
    ]
    wait_all(copies)
    parts = split(b[...])
    sent = []
    for i, first in enumerate(range(0, DEV, PART)):
        put_slots(out, first * V_ROWS, select(onehots[i], parts), PART)
        here = pl.ds(first * V_ROWS, PART * V_ROWS)
        sent += start_all(((out.at[here], out_hbm.at[here]),), sems, 1 + i)
    wait_all(sent)


def gathered_rows(wanted_t, first):
    place = iota((COLS, DEV), 0).astype(F32)
    return jnp.concatenate(
        [ones(place == wanted_t[first + s : first + s + 1, :]) for s in range(CAP)], axis=1
    )


def normal_kernel(asked, d_hbm, wt_hbm, w, d, wt, sems):
    wanted_t = asked[pl.ds(W_ROWS, DEV, stride=A_ROWS), :].T
    wt[...] = wanted_t[:16]
    sent = start_all(((wt, wt_hbm),), sems)
    onehot_t = gathered_rows(wanted_t, 8)
    for k in range(4):
        for s in range(CAP):
            for half in range(2):
                w[k, s * DEV : (s + 1) * DEV, half * 128 : half * 128 + 128] = asked[
                    pl.ds(s * 8 + k * 2 + half, DEV, stride=A_ROWS), :
                ]
    for m in range(4):
        total = None
        for k in range(4 - m):
            product = w[k] * w[k + m]
            high = product.astype(BF16)
            low = (product - high.astype(F32)).astype(BF16)
            part = dot(onehot_t, high) + dot(onehot_t, low)
            if k != 1:
                part = pltpu.roll(part, (k - 1) % NZ, 1)
            total = part if total is None else total + part
        d[m] = total
        sent += start_all(((d.at[m], d_hbm.at[m]),), sems, 1 + m)
    wait_all(sent)


def read_slots(ref):
    return jnp.concatenate(
        [
            jnp.concatenate(
                [ref[pl.ds(s * 2 + half, DEV, stride=V_ROWS), :] for half in range(2)], axis=1
            )
            for s in range(CAP)
        ],
        axis=0,
    )


def middle_kernel(arr, own_hbm, w_hbm, b_hbm, d_hbm, *refs):
    lam_hbm, out_hbm, own, w, b, d, lam_scr, out, parts, sems = refs[-10:]
    copies = start_all(((own_hbm.at[0], own), (w_hbm.at[0], w), (b_hbm, b), (d_hbm, d)), sems)
    copies[0].wait()
    owner_row = own[...]
    taken = jnp.concatenate([ones(m) for m in masks_by_column(owner_row)], axis=1)
    masks = masks_by_owner(owner_row, 0, DEV)
    mine_all = select(taken, split(read_slots(arr)))
    wait_all(copies[1:])
    rows = 64
    for start in range(0, COLS, rows):
        here = slice(start, start + rows)
        mine = mine_all[here]
        weights = [
            w[k, start // 16 : (start + rows) // 16].reshape(rows, NZ).astype(F32) for k in range(4)
        ]
        field = b[here]
        for k in range(4):
            field += weights[k] * (mine if k == 1 else pltpu.roll(mine, (1 - k) % NZ, 1))
        lam = d[0, here] * field
        for m in range(1, 4):
            lam += d[m, here] * pltpu.roll(field, NZ - m, 1) + pltpu.roll(d[m, here] * field, m, 1)
        lam_scr[here] = lam
        spread = weights[1] * lam
        for k in (0, 2, 3):
            spread += pltpu.roll(weights[k] * lam, (k - 1) % NZ, 1)
        for i, part in enumerate(split(spread)):
            parts[i, here] = part
    sent = start_all(((lam_scr, lam_hbm),), sems)
    for i, first in enumerate(range(0, DEV, PART)):
        onehot = jnp.concatenate([ones(m[first : first + PART]) for m in masks], axis=0)
        put_slots(out, first * V_ROWS, select(onehot, [parts[p] for p in range(2)]), PART)
        here = pl.ds(first * V_ROWS, PART * V_ROWS)
        sent += start_all(((out.at[here], out_hbm.at[here]),), sems, 1 + i)
    wait_all(sent)


def final_kernel(arr, wt_hbm, h_hbm, g_hbm, out_hbm, wt, h, g, out, sems):
    copies = start_all(((wt_hbm, wt), (h_hbm, h), (g_hbm, g)), sems)
    copies[0].wait()
    onehot_t = gathered_rows(wt[...], 0)
    lam = select(onehot_t, split(read_slots(arr)))
    wait_all(copies[1:])
    sent = []
    for c in range(3):
        out[c] = h[c] - 0.5 * (lam * g[c])
        sent += start_all(((out.at[c], out_hbm.at[c]),), sems, c)
    wait_all(sent)


def exchange(value):
    return lax.all_to_all(value, AXES, split_axis=0, concat_axis=0, tiled=True)


def neighbours(first, last, axis):
    count = lax.axis_size(axis)
    up = [(i, (i + 1) % count) for i in range(count)]
    down = [(j, i) for i, j in up]
    return lax.ppermute(last, axis, up), lax.ppermute(first, axis, down)


def per_device(state_path, velocity, weights, owners, sources):
    owner_row = owners.reshape(2, 1, COLS)
    source_row = sources.reshape(2, 1, COLS)
    hbm = pl.BlockSpec(memory_space=pltpu.HBM)
    near = pl.BlockSpec(memory_space=pltpu.VMEM)
    struct = lambda *shape: pltpu.HBM(shape, F32)
    scratch = lambda *shape: pltpu.VMEM(shape, F32)
    sems = lambda count: pltpu.SemaphoreType.DMA((count,))
    per_field = lambda count: struct(count, 16, 16, NZ)

    request = call(
        request_kernel,
        struct(DEV * A_ROWS, 128),
        16,
        3,
        in_specs=[hbm] * 3,
        out_specs=hbm,
        scratch_shapes=[
            pltpu.VMEM((2, 1, COLS), jnp.int32),
            pltpu.VMEM((2, 1, COLS), jnp.int32),
            pltpu.VMEM((4, 16, 16, NZ), BF16),
            scratch(DEV * A_ROWS, 128),
            sems(7),
        ],
    )(owner_row, source_row, weights)
    asked = exchange(request.reshape(DEV, A_ROWS, 1, 128)).reshape(DEV * A_ROWS, 128)

    def halo(fields):
        xlo, xhi = neighbours(fields(slice(0, 4), slice(None)), fields(slice(12, 16), slice(None)), "gx")
        ylo, yhi = neighbours(fields(slice(None), slice(0, 4)), fields(slice(None), slice(12, 16)), "gy")
        return xlo, xhi, ylo, yhi

    tie = pl.BlockSpec(memory_space=pl.ANY)

    def slopes(step, faces, *after):
        return call(
            functools.partial(slope_kernel, step),
            (per_field(3), struct(16, 16, NZ)),
            10,
            3,
            in_specs=[hbm] * 2 + [near] * 4 + [hbm] * len(after),
            out_specs=(hbm, hbm),
            scratch_shapes=[
                scratch(1, 24, 16, NZ),
                scratch(1, 16, 32, NZ),
                scratch(3, 16, 16, NZ),
                scratch(3, 16, 16, NZ),
                scratch(16, 16, NZ),
                sems(4),
            ],
        )(state_path, velocity, *faces, *after)

    slope0, before0 = slopes(0, halo(lambda x, y: state_path[:1, x, y]))
    faces1 = halo(lambda x, y: state_path[1:, x, y])

    supply = call(
        supply_kernel,
        struct(DEV * V_ROWS, 128),
        8,
        2,
        in_specs=[near, hbm] + [tie] * 4,
        out_specs=hbm,
        scratch_shapes=[scratch(COLS, NZ), scratch(DEV * V_ROWS, 128), sems(5)],
    )(asked, before0.reshape(COLS, NZ), *faces1)
    arrived = exchange(supply.reshape(DEV, CAP, 2, 128)).reshape(DEV * V_ROWS, 128)

    slope1, before1 = slopes(1, faces1, supply)
    faces = halo(lambda x, y: velocity[:, x, y])

    normal, wanted_t = call(
        normal_kernel,
        (struct(4, COLS, NZ), struct(16, 128)),
        20,
        4,
        in_specs=[near],
        out_specs=(hbm, hbm),
        scratch_shapes=[scratch(4, CAP * DEV, NZ), scratch(4, COLS, NZ), scratch(16, 128), sems(5)],
    )(asked)

    lam, push = call(
        middle_kernel,
        (struct(COLS, NZ), struct(DEV * V_ROWS, 128)),
        14,
        4,
        in_specs=[near] + [hbm] * 4 + [tie] * 4,
        out_specs=(hbm, hbm),
        scratch_shapes=[
            pltpu.VMEM((1, COLS), jnp.int32),
            pltpu.VMEM((4, 16, 16, NZ), BF16),
            scratch(COLS, NZ),
            scratch(4, COLS, NZ),
            scratch(COLS, NZ),
            scratch(DEV * V_ROWS, 128),
            pltpu.VMEM((2, COLS, NZ), BF16),
            sems(5),
        ],
    )(arrived, owner_row, weights, before1.reshape(COLS, NZ), normal, *faces)
    returned = exchange(push.reshape(DEV, CAP, 2, 128)).reshape(DEV * V_ROWS, 128)

    hess = call(
        curve_kernel,
        per_field(3),
        14,
        5,
        in_specs=[hbm] + [near] * 4 + [hbm] * 2,
        out_specs=hbm,
        scratch_shapes=[
            scratch(3, 24, 16, NZ),
            scratch(3, 16, 32, NZ),
            scratch(16, 16, NZ),
            scratch(3, 16, 16, NZ),
            scratch(3, 16, 16, NZ),
            sems(8),
        ],
    )(velocity, *faces, lam.reshape(16, 16, NZ), slope1)
    out = call(
        final_kernel,
        struct(3, COLS, NZ),
        14,
        2,
        in_specs=[near] + [hbm] * 3,
        out_specs=hbm,
        scratch_shapes=[
            scratch(16, 128),
            scratch(3, COLS, NZ),
            scratch(3, COLS, NZ),
            scratch(3, COLS, NZ),
            sems(3),
        ],
    )(returned, wanted_t, hess.reshape(3, COLS, NZ), slope0.reshape(3, COLS, NZ))
    return out.reshape(3, 16, 16, NZ)


def solution(mesh):
    return jax.shard_map(
        per_device,
        mesh=mesh,
        in_specs=(
            P(None, "gx", "gy", None),
            P(None, "gx", "gy", None),
            P(None, None, "gx", "gy", None),
            P(None, "gx", "gy", None, None),
            P(None, "gx", "gy", None),
        ),
        out_specs=P(None, "gx", "gy", None),
        check_vma=False,
    )
```

```python
import functools

import jax
import jax.numpy as jnp
from jax import lax
from jax.experimental import pallas as pl
from jax.experimental.pallas import tpu as pltpu
from jax.sharding import PartitionSpec as P

FIRST = (0.8, -0.2, 4.0 / 105.0, -1.0 / 280.0)
SECOND = (-205.0 / 72.0, 1.6, -0.2, 8.0 / 315.0, -1.0 / 560.0)
BETA = 0.05
AXES = ("gx", "gy")
CAP = 6
DEV = 128
COLS = 256
NZ = 256
F32 = jnp.float32
BF16 = jnp.bfloat16
W_ROWS = CAP * 8
A_ROWS = W_ROWS + 1
V_ROWS = CAP * 2
PART = 32


def call(kernel, out_shape, mib, micros, in_specs, **kw):
    run = pl.pallas_call(
        kernel,
        out_shape=out_shape,
        in_specs=in_specs,
        compiler_params=pltpu.CompilerParams(vmem_limit_bytes=mib * 1024 * 1024),
        cost_estimate=pl.CostEstimate(
            flops=int(micros * 1e8), bytes_accessed=int(micros * 2e6), transcendentals=0
        ),
        **kw,
    )

    def placed(*args):
        return run(
            *(
                pltpu.with_memory_space_constraint(x, pltpu.HBM) if spec.memory_space == pltpu.HBM else x
                for spec, x in zip(in_specs, args)
            )
        )

    return placed


def iota(shape, dim):
    return lax.broadcasted_iota(jnp.int32, shape, dim)


def dot(a, b):
    return jnp.dot(a, b, preferred_element_type=F32)


def split(x):
    hi = x.astype(BF16)
    return hi, (x - hi.astype(F32)).astype(BF16)


def select(onehot, parts):
    return sum(dot(onehot, part) for part in parts)


def ones(mask):
    return jnp.where(mask, 1.0, 0.0).astype(BF16)


def masks_by_owner(owner_row, first, count):
    match = iota((count, COLS), 0) + first == owner_row
    before = ones(iota((COLS, COLS), 0) < iota((COLS, COLS), 1))
    slot = dot(ones(match), before)
    return [match & (slot == float(s)) for s in range(CAP)]


def masks_by_column(owner_row):
    spread = jnp.broadcast_to(owner_row.astype(F32), (DEV, COLS)).T
    match = iota((COLS, DEV), 1).astype(F32) == spread
    before = ones(iota((COLS, COLS), 1) < iota((COLS, COLS), 0))
    slot = dot(before, ones(match))
    return [match & (slot == float(s)) for s in range(CAP)]


def put_slots(out_ref, start, values, count):
    for s in range(CAP):
        for half in range(2):
            out_ref[pl.ds(start + s * 2 + half, count, stride=V_ROWS), :] = values[
                s * count : (s + 1) * count, half * 128 : half * 128 + 128
            ]


def start_all(pairs, sems, first=0):
    copies = [
        pltpu.make_async_copy(source, target, sems.at[first + i])
        for i, (source, target) in enumerate(pairs)
    ]
    for copy in copies:
        copy.start()
    return copies


def wait_all(copies):
    for copy in copies:
        copy.wait()


def request_kernel(own_hbm, src_hbm, w_hbm, out_hbm, own, src, w, out, sems):
    copies = start_all(((own_hbm, own), (src_hbm, src), (w_hbm.at[1], w)), sems)
    wait_all(copies[:2])
    lane = iota((DEV, 128), 1)
    wanted = jnp.zeros((DEV, 128), F32)
    for j in range(2):
        masks = masks_by_owner(own[j], 0, DEV)
        source_row = src[j].astype(F32)
        for s in range(CAP):
            column = jnp.sum(jnp.where(masks[s], source_row, 0.0), axis=1, keepdims=True)
            wanted = jnp.where(lane == 8 * j + s, column, wanted)
    out[pl.ds(W_ROWS, DEV, stride=A_ROWS), :] = wanted
    copies[2].wait()
    sent = []
    for i, first in enumerate(range(0, DEV, PART)):
        onehot = jnp.concatenate([ones(m[first : first + PART]) for m in masks], axis=0)
        for k in range(4):
            placed = dot(onehot, w[k].reshape(COLS, NZ))
            for s in range(CAP):
                for half in range(2):
                    row = first * A_ROWS + s * 8 + k * 2 + half
                    out[pl.ds(row, PART, stride=A_ROWS), :] = placed[
                        s * PART : (s + 1) * PART, half * 128 : half * 128 + 128
                    ]
        block = pl.ds(first * A_ROWS, PART * A_ROWS)
        sent += start_all(((out.at[block], out_hbm.at[block]),), sems, 3 + i)
    wait_all(sent)


def fill(sources, halos, xpad, ypad, ylo, yhi, sems, extra=()):
    pairs = list(extra) + [(halos[2], ylo), (halos[3], yhi)]
    pairs += [(halos[0], xpad.at[:, pl.ds(0, 4)]), (halos[1], xpad.at[:, pl.ds(20, 4)])]
    for i, source in enumerate(sources):
        pairs += [(source, xpad.at[i, pl.ds(4, 16)]), (source, ypad.at[i, :, pl.ds(8, 16)])]
    wait_all(start_all(pairs, sems))
    ypad[:, :, 4:8] = ylo[...]
    ypad[:, :, 24:28] = yhi[...]


def differences(xpad, ypad, i, x, rows, coeffs, sign):
    centre = xpad[i, pl.ds(x + 4, rows)]
    parts = [None, None, None]
    for k in range(4):
        d = k + 1
        terms = (
            xpad[i, pl.ds(x + 4 + d, rows)] + sign * xpad[i, pl.ds(x + 4 - d, rows)],
            ypad[i, pl.ds(x, rows), 8 + d : 24 + d, :] + sign * ypad[i, pl.ds(x, rows), 8 - d : 24 - d, :],
            pltpu.roll(centre, NZ - d, 2) + sign * pltpu.roll(centre, d, 2),
        )
        for c in range(3):
            term = coeffs[k] * terms[c]
            parts[c] = term if parts[c] is None else parts[c] + term
    return centre, parts


ROWS = 4


def faces_kernel(st_hbm, ve_hbm, xlo, xhi, ylo, yhi, edges, sems):
    pairs = []
    for out, y_out, first, y_first in ((xlo, 0, 0, 0), (xhi, 1, 12, 8)):
        for source, place in ((st_hbm, pl.ds(0, 2)), (ve_hbm, pl.ds(2, 3))):
            pairs.append((source.at[:, pl.ds(first, 4)], out.at[place]))
            pairs.append((source.at[:, :, pl.ds(y_first, 8)], edges.at[y_out, place]))
    wait_all(start_all(pairs, sems))
    ylo[...] = edges[0, :, :, 0:4]
    yhi[...] = edges[1, :, :, 4:8]


def stencil_kernel(st_hbm, ve_hbm, xlo, xhi, ylo, yhi, g_hbm, b_hbm, h_hbm, xpad, ypad, ylo_scr, yhi_scr, g, b, h, sems):
    sources = [st_hbm.at[j] for j in range(2)] + [ve_hbm.at[c] for c in range(3)]
    fill(sources, (xlo, xhi, ylo, yhi), xpad, ypad, ylo_scr, yhi_scr, sems)
    sent = []
    for j in range(2):

        @pl.loop(0, 16, step=ROWS)
        def slope_rows(x):
            here = pl.ds(x, ROWS)
            slope = differences(xpad, ypad, j, x, ROWS, FIRST, -1.0)[1]
            total = None
            for c in range(3):
                g[j, c, here] = slope[c]
                term = xpad[2 + c, pl.ds(x + 4, ROWS)] * slope[c]
                total = term if total is None else total + term
            b[j, here] = -0.5 * total

        sent += start_all(((b.at[j], b_hbm.at[j]), (g.at[j], g_hbm.at[j])), sems, len(sent))

    @pl.loop(0, 16, step=ROWS)
    def curve_rows(x):
        for c in range(3):
            centre, parts = differences(xpad, ypad, 2 + c, x, ROWS, SECOND[1:], 1.0)
            total = 3.0 * SECOND[0] * centre + parts[0] + parts[1] + parts[2]
            h[c, pl.ds(x, ROWS)] = -BETA * total

    sent += start_all(((h, h_hbm),), sems, len(sent))
    wait_all(sent)


def supply_kernel(asked, b_hbm, out_hbm, b, out, sems):
    copies = start_all(((b_hbm.at[0], b),), sems)
    wanted = asked[pl.ds(W_ROWS, DEV, stride=A_ROWS), :]
    place = iota((PART, COLS), 1).astype(F32)
    onehots = [
        jnp.concatenate(
            [ones(wanted[first : first + PART, s : s + 1] == place) for s in range(CAP)], axis=0
        )
        for first in range(0, DEV, PART)
    ]
    wait_all(copies)
    parts = split(b[...])
    sent = []
    for i, first in enumerate(range(0, DEV, PART)):
        put_slots(out, first * V_ROWS, select(onehots[i], parts), PART)
        here = pl.ds(first * V_ROWS, PART * V_ROWS)
        sent += start_all(((out.at[here], out_hbm.at[here]),), sems, 1 + i)
    wait_all(sent)


def gathered_rows(wanted_t, first):
    place = iota((COLS, DEV), 0).astype(F32)
    return jnp.concatenate(
        [ones(place == wanted_t[first + s : first + s + 1, :]) for s in range(CAP)], axis=1
    )


def normal_kernel(asked, *refs):
    d_hbm, wt_hbm, w, d, wt, sems = refs[-6:]
    wanted_t = asked[pl.ds(W_ROWS, DEV, stride=A_ROWS), :].T
    wt[...] = wanted_t[:16]
    sent = start_all(((wt, wt_hbm),), sems)
    onehot_t = gathered_rows(wanted_t, 8)
    for k in range(4):
        for s in range(CAP):
            for half in range(2):
                w[k, s * DEV : (s + 1) * DEV, half * 128 : half * 128 + 128] = asked[
                    pl.ds(s * 8 + k * 2 + half, DEV, stride=A_ROWS), :
                ]
    for m in range(4):
        total = None
        for k in range(4 - m):
            product = w[k] * w[k + m]
            high = product.astype(BF16)
            low = (product - high.astype(F32)).astype(BF16)
            part = dot(onehot_t, high) + dot(onehot_t, low)
            if k != 1:
                part = pltpu.roll(part, (k - 1) % NZ, 1)
            total = part if total is None else total + part
        d[m] = total
        sent += start_all(((d.at[m], d_hbm.at[m]),), sems, 1 + m)
    wait_all(sent)


def read_slots(ref):
    return jnp.concatenate(
        [
            jnp.concatenate(
                [ref[pl.ds(s * 2 + half, DEV, stride=V_ROWS), :] for half in range(2)], axis=1
            )
            for s in range(CAP)
        ],
        axis=0,
    )


def middle_kernel(arr, own_hbm, w_hbm, b_hbm, d_hbm, *refs):
    lam_hbm, out_hbm, own, w, b, d, lam_scr, out, parts, sems = refs[-10:]
    copies = start_all(((own_hbm.at[0], own), (w_hbm.at[0], w), (b_hbm.at[1], b), (d_hbm, d)), sems)
    copies[0].wait()
    owner_row = own[...]
    taken = jnp.concatenate([ones(m) for m in masks_by_column(owner_row)], axis=1)
    masks = masks_by_owner(owner_row, 0, DEV)
    mine_all = select(taken, split(read_slots(arr)))
    wait_all(copies[1:])
    rows = 64
    for start in range(0, COLS, rows):
        here = slice(start, start + rows)
        mine = mine_all[here]
        weights = [
            w[k, start // 16 : (start + rows) // 16].reshape(rows, NZ).astype(F32) for k in range(4)
        ]
        field = b[here]
        for k in range(4):
            field += weights[k] * (mine if k == 1 else pltpu.roll(mine, (1 - k) % NZ, 1))
        lam = d[0, here] * field
        for m in range(1, 4):
            lam += d[m, here] * pltpu.roll(field, NZ - m, 1) + pltpu.roll(d[m, here] * field, m, 1)
        lam_scr[here] = lam
        spread = weights[1] * lam
        for k in (0, 2, 3):
            spread += pltpu.roll(weights[k] * lam, (k - 1) % NZ, 1)
        for i, part in enumerate(split(spread)):
            parts[i, here] = part
    sent = start_all(((lam_scr, lam_hbm),), sems)
    for i, first in enumerate(range(0, DEV, PART)):
        onehot = jnp.concatenate([ones(m[first : first + PART]) for m in masks], axis=0)
        put_slots(out, first * V_ROWS, select(onehot, [parts[p] for p in range(2)]), PART)
        here = pl.ds(first * V_ROWS, PART * V_ROWS)
        sent += start_all(((out.at[here], out_hbm.at[here]),), sems, 1 + i)
    wait_all(sent)


def final_kernel(arr, wt_hbm, h_hbm, g_hbm, out_hbm, wt, h, g, out, sems):
    copies = start_all(((wt_hbm, wt), (h_hbm, h), (g_hbm.at[0], g)), sems)
    copies[0].wait()
    onehot_t = gathered_rows(wt[...], 0)
    lam = select(onehot_t, split(read_slots(arr)))
    wait_all(copies[1:])
    sent = []
    for c in range(3):
        out[c] = h[c] - 0.5 * (lam * g[c])
        sent += start_all(((out.at[c], out_hbm.at[c]),), sems, c)
    wait_all(sent)


def exchange(value):
    return lax.all_to_all(value, AXES, split_axis=0, concat_axis=0, tiled=True)


def neighbours(first, last, axis):
    count = lax.axis_size(axis)
    up = [(i, (i + 1) % count) for i in range(count)]
    down = [(j, i) for i, j in up]
    return lax.ppermute(last, axis, up), lax.ppermute(first, axis, down)


def per_device(state_path, velocity, weights, owners, sources):
    owner_row = owners.reshape(2, 1, COLS)
    source_row = sources.reshape(2, 1, COLS)
    hbm = pl.BlockSpec(memory_space=pltpu.HBM)
    near = pl.BlockSpec(memory_space=pltpu.VMEM)
    struct = lambda *shape: pltpu.HBM(shape, F32)
    scratch = lambda *shape: pltpu.VMEM(shape, F32)
    sems = lambda count: pltpu.SemaphoreType.DMA((count,))
    per_field = lambda count: struct(count, 16, 16, NZ)

    request = call(
        request_kernel,
        struct(DEV * A_ROWS, 128),
        16,
        3,
        in_specs=[hbm] * 3,
        out_specs=hbm,
        scratch_shapes=[
            pltpu.VMEM((2, 1, COLS), jnp.int32),
            pltpu.VMEM((2, 1, COLS), jnp.int32),
            pltpu.VMEM((4, 16, 16, NZ), BF16),
            scratch(DEV * A_ROWS, 128),
            sems(7),
        ],
    )(owner_row, source_row, weights)
    asked = exchange(request.reshape(DEV, A_ROWS, 1, 128)).reshape(DEV * A_ROWS, 128)

    edge = pltpu.VMEM((5, 4, 16, NZ), F32), pltpu.VMEM((5, 16, 4, NZ), F32)
    first_x, last_x, first_y, last_y = call(
        faces_kernel,
        (edge[0], edge[0], edge[1], edge[1]),
        10,
        1,
        in_specs=[hbm] * 2,
        out_specs=(near,) * 4,
        scratch_shapes=[scratch(2, 5, 16, 8, NZ), sems(8)],
    )(state_path, velocity)
    halos = neighbours(first_x, last_x, "gx") + neighbours(first_y, last_y, "gy")
    slopes, before, hess = call(
        stencil_kernel,
        (struct(2, 3, 16, 16, NZ), struct(2, 16, 16, NZ), per_field(3)),
        24,
        1000,
        in_specs=[hbm] * 6,
        out_specs=(hbm,) * 3,
        scratch_shapes=[
            scratch(5, 24, 16, NZ),
            scratch(5, 16, 32, NZ),
            scratch(5, 16, 4, NZ),
            scratch(5, 16, 4, NZ),
            scratch(2, 3, 16, 16, NZ),
            scratch(2, 16, 16, NZ),
            scratch(3, 16, 16, NZ),
            sems(14),
        ],
    )(state_path, velocity, *halos)
    before = before.reshape(2, COLS, NZ)

    supply = call(
        supply_kernel,
        struct(DEV * V_ROWS, 128),
        8,
        2,
        in_specs=[near, hbm],
        out_specs=hbm,
        scratch_shapes=[scratch(COLS, NZ), scratch(DEV * V_ROWS, 128), sems(5)],
    )(asked, before)
    arrived = exchange(supply.reshape(DEV, CAP, 2, 128)).reshape(DEV * V_ROWS, 128)

    normal, wanted_t = call(
        normal_kernel,
        (struct(4, COLS, NZ), struct(16, 128)),
        20,
        4,
        in_specs=[near],
        out_specs=(hbm, hbm),
        scratch_shapes=[scratch(4, CAP * DEV, NZ), scratch(4, COLS, NZ), scratch(16, 128), sems(5)],
    )(asked)

    lam, push = call(
        middle_kernel,
        (struct(COLS, NZ), struct(DEV * V_ROWS, 128)),
        14,
        4,
        in_specs=[near] + [hbm] * 4,
        out_specs=(hbm, hbm),
        scratch_shapes=[
            pltpu.VMEM((1, COLS), jnp.int32),
            pltpu.VMEM((4, 16, 16, NZ), BF16),
            scratch(COLS, NZ),
            scratch(4, COLS, NZ),
            scratch(COLS, NZ),
            scratch(DEV * V_ROWS, 128),
            pltpu.VMEM((2, COLS, NZ), BF16),
            sems(5),
        ],
    )(arrived, owner_row, weights, before, normal)
    returned = exchange(push.reshape(DEV, CAP, 2, 128)).reshape(DEV * V_ROWS, 128)

    hess = hess - 0.5 * (lam.reshape(1, 16, 16, NZ) * slopes[1])
    out = call(
        final_kernel,
        struct(3, COLS, NZ),
        14,
        2,
        in_specs=[near] + [hbm] * 3,
        out_specs=hbm,
        scratch_shapes=[
            scratch(16, 128),
            scratch(3, COLS, NZ),
            scratch(3, COLS, NZ),
            scratch(3, COLS, NZ),
            sems(3),
        ],
    )(returned, wanted_t, hess.reshape(3, COLS, NZ), slopes.reshape(2, 3, COLS, NZ))
    return out.reshape(3, 16, 16, NZ)


def solution(mesh):
    return jax.shard_map(
        per_device,
        mesh=mesh,
        in_specs=(
            P(None, "gx", "gy", None),
            P(None, "gx", "gy", None),
            P(None, None, "gx", "gy", None),
            P(None, "gx", "gy", None, None),
            P(None, "gx", "gy", None),
        ),
        out_specs=P(None, "gx", "gy", None),
        check_vma=False,
    )
```

```python
import functools

import jax
import jax.numpy as jnp
from jax import lax
from jax.experimental import pallas as pl
from jax.experimental.pallas import tpu as pltpu
from jax.sharding import PartitionSpec as P

FIRST = (0.8, -0.2, 4.0 / 105.0, -1.0 / 280.0)
SECOND = (-205.0 / 72.0, 1.6, -0.2, 8.0 / 315.0, -1.0 / 560.0)
BETA = 0.05
AXES = ("gx", "gy")
CAP = 6
DEV = 128
COLS = 256
NZ = 256
F32 = jnp.float32
BF16 = jnp.bfloat16
W_ROWS = CAP * 8
A_ROWS = W_ROWS + 1
V_ROWS = CAP * 2
PART = 32


def call(kernel, out_shape, mib, micros, in_specs, **kw):
    run = pl.pallas_call(
        kernel,
        out_shape=out_shape,
        in_specs=in_specs,
        compiler_params=pltpu.CompilerParams(vmem_limit_bytes=mib * 1024 * 1024),
        cost_estimate=pl.CostEstimate(
            flops=int(micros * 1e8), bytes_accessed=int(micros * 2e6), transcendentals=0
        ),
        **kw,
    )

    def placed(*args):
        return run(
            *(
                pltpu.with_memory_space_constraint(x, pltpu.HBM) if spec.memory_space == pltpu.HBM else x
                for spec, x in zip(in_specs, args)
            )
        )

    return placed


def iota(shape, dim):
    return lax.broadcasted_iota(jnp.int32, shape, dim)


def dot(a, b):
    return jnp.dot(a, b, preferred_element_type=F32)


def split(x):
    hi = x.astype(BF16)
    return hi, (x - hi.astype(F32)).astype(BF16)


def select(onehot, parts):
    return sum(dot(onehot, part) for part in parts)


def ones(mask):
    return jnp.where(mask, 1.0, 0.0).astype(BF16)


def masks_by_owner(owner_row, first, count):
    match = iota((count, COLS), 0) + first == owner_row
    before = ones(iota((COLS, COLS), 0) < iota((COLS, COLS), 1))
    slot = dot(ones(match), before)
    return [match & (slot == float(s)) for s in range(CAP)]


def masks_by_column(owner_row):
    spread = jnp.broadcast_to(owner_row.astype(F32), (DEV, COLS)).T
    match = iota((COLS, DEV), 1).astype(F32) == spread
    before = ones(iota((COLS, COLS), 1) < iota((COLS, COLS), 0))
    slot = dot(before, ones(match))
    return [match & (slot == float(s)) for s in range(CAP)]


def put_slots(out_ref, start, values, count):
    for s in range(CAP):
        for half in range(2):
            out_ref[pl.ds(start + s * 2 + half, count, stride=V_ROWS), :] = values[
                s * count : (s + 1) * count, half * 128 : half * 128 + 128
            ]


def start_all(pairs, sems, first=0):
    copies = [
        pltpu.make_async_copy(source, target, sems.at[first + i])
        for i, (source, target) in enumerate(pairs)
    ]
    for copy in copies:
        copy.start()
    return copies


def under_way(tile):
    @pl.loop(0, 2)
    def touch(i):
        tile[pl.ds(i * 8, 8), :] = jnp.zeros((8, 128), F32)


def wait_all(copies):
    for copy in copies:
        copy.wait()


def request_kernel(
    own_hbm, src_hbm, w_hbm, st_hbm, ve_hbm, out_hbm, xlo, xhi, ylo, yhi, own, src, w, out, edges, tile, sems
):
    pairs = [(own_hbm, own), (src_hbm, src), (w_hbm.at[1], w)]
    for x_out, y_out, first, y_first in ((xlo, 0, 0, 0), (xhi, 1, 12, 8)):
        for source, place in ((st_hbm, pl.ds(0, 2)), (ve_hbm, pl.ds(2, 3))):
            pairs.append((source.at[:, pl.ds(first, 4)], x_out.at[place]))
            pairs.append((source.at[:, :, pl.ds(y_first, 8)], edges.at[y_out, place]))
    copies = start_all(pairs, sems)
    under_way(tile)
    wait_all(copies[:2])
    lane = iota((DEV, 128), 1)
    wanted = jnp.zeros((DEV, 128), F32)
    for j in range(2):
        masks = masks_by_owner(own[j], 0, DEV)
        source_row = src[j].astype(F32)
        for s in range(CAP):
            column = jnp.sum(jnp.where(masks[s], source_row, 0.0), axis=1, keepdims=True)
            wanted = jnp.where(lane == 8 * j + s, column, wanted)
    out[pl.ds(W_ROWS, DEV, stride=A_ROWS), :] = wanted
    copies[2].wait()
    sent = []
    for i, first in enumerate(range(0, DEV, PART)):
        onehot = jnp.concatenate([ones(m[first : first + PART]) for m in masks], axis=0)
        for k in range(4):
            placed = dot(onehot, w[k].reshape(COLS, NZ))
            for s in range(CAP):
                for half in range(2):
                    row = first * A_ROWS + s * 8 + k * 2 + half
                    out[pl.ds(row, PART, stride=A_ROWS), :] = placed[
                        s * PART : (s + 1) * PART, half * 128 : half * 128 + 128
                    ]
        block = pl.ds(first * A_ROWS, PART * A_ROWS)
        sent += start_all(((out.at[block], out_hbm.at[block]),), sems, 11 + i)
    wait_all(copies[3:])
    ylo[...] = edges[0, :, :, 0:4]
    yhi[...] = edges[1, :, :, 4:8]
    wait_all(sent)


def fill(sources, halos, xpad, ypad, ylo, yhi, sems, extra=()):
    pairs = list(extra) + [(halos[2], ylo), (halos[3], yhi)]
    pairs += [(halos[0], xpad.at[:, pl.ds(0, 4)]), (halos[1], xpad.at[:, pl.ds(20, 4)])]
    for i, source in enumerate(sources):
        pairs += [(source, xpad.at[i, pl.ds(4, 16)]), (source, ypad.at[i, :, pl.ds(8, 16)])]
    wait_all(start_all(pairs, sems))
    ypad[:, :, 4:8] = ylo[...]
    ypad[:, :, 24:28] = yhi[...]


def differences(xpad, ypad, i, x, rows, coeffs, sign):
    centre = xpad[i, pl.ds(x + 4, rows)]
    parts = [None, None, None]
    for k in range(4):
        d = k + 1
        terms = (
            xpad[i, pl.ds(x + 4 + d, rows)] + sign * xpad[i, pl.ds(x + 4 - d, rows)],
            ypad[i, pl.ds(x, rows), 8 + d : 24 + d, :] + sign * ypad[i, pl.ds(x, rows), 8 - d : 24 - d, :],
            pltpu.roll(centre, NZ - d, 2) + sign * pltpu.roll(centre, d, 2),
        )
        for c in range(3):
            term = coeffs[k] * terms[c]
            parts[c] = term if parts[c] is None else parts[c] + term
    return centre, parts


ROWS = 4


def stencil_kernel(
    st_hbm, ve_hbm, xlo, xhi, ylo, yhi, g_hbm, b_hbm, h_hbm, first_parts, xpad, ypad, ylo_scr, yhi_scr, g, b, h, sems
):
    sources = [st_hbm.at[j] for j in range(2)] + [ve_hbm.at[c] for c in range(3)]
    fill(sources, (xlo, xhi, ylo, yhi), xpad, ypad, ylo_scr, yhi_scr, sems)
    sent = []
    for j in range(2):

        @pl.loop(0, 16, step=ROWS)
        def slope_rows(x):
            here = pl.ds(x, ROWS)
            slope = differences(xpad, ypad, j, x, ROWS, FIRST, -1.0)[1]
            total = None
            for c in range(3):
                g[j, c, here] = slope[c]
                term = xpad[2 + c, pl.ds(x + 4, ROWS)] * slope[c]
                total = term if total is None else total + term
            b[j, here] = -0.5 * total

        sent += start_all(((g.at[j], g_hbm.at[j]),), sems, len(sent))
    for p, part in enumerate(split(b[0].reshape(COLS, NZ))):
        first_parts[p] = part
    sent += start_all(((b.at[1], b_hbm),), sems, len(sent))

    @pl.loop(0, 16, step=ROWS)
    def curve_rows(x):
        for c in range(3):
            centre, parts = differences(xpad, ypad, 2 + c, x, ROWS, SECOND[1:], 1.0)
            total = 3.0 * SECOND[0] * centre + parts[0] + parts[1] + parts[2]
            h[c, pl.ds(x, ROWS)] = -BETA * total

    sent += start_all(((h, h_hbm),), sems, len(sent))
    wait_all(sent)


def supply_kernel(asked_hbm, parts, out_hbm, asked, out, sems):
    count = DEV // 8
    groups = [pl.ds(first, count) for first in range(0, DEV, count)]
    wait_all(start_all([(asked_hbm.at[here, W_ROWS], asked.at[here]) for here in groups], sems))
    wanted = asked[:, 0, :]
    place = iota((PART, COLS), 1).astype(F32)
    sent = []
    for i, first in enumerate(range(0, DEV, PART)):
        onehot = jnp.concatenate(
            [ones(wanted[first : first + PART, s : s + 1] == place) for s in range(CAP)], axis=0
        )
        put_slots(out, first * V_ROWS, select(onehot, [parts[p] for p in range(2)]), PART)
        here = pl.ds(first * V_ROWS, PART * V_ROWS)
        sent += start_all(((out.at[here], out_hbm.at[here]),), sems, i)
    wait_all(sent)


def gathered_rows(wanted_t, first):
    place = iota((COLS, DEV), 0).astype(F32)
    return jnp.concatenate(
        [ones(place == wanted_t[first + s : first + s + 1, :]) for s in range(CAP)], axis=1
    )


def normal_kernel(asked_hbm, own_hbm, w_hbm, b_hbm, d, taken, w0, b, placed_hbm, wt_hbm, asked, w, own, wt, placed, sems):
    copies = start_all(((own_hbm.at[0], own), (w_hbm.at[0], w0), (b_hbm, b)), sems)
    wait_all(start_all(((asked_hbm, asked),), sems, 3))
    wanted_t = asked[pl.ds(W_ROWS, DEV, stride=A_ROWS), :].T
    wt[...] = wanted_t[:16]
    sent = start_all(((wt, wt_hbm),), sems, 3)
    onehot_t = gathered_rows(wanted_t, 8)
    for k in range(4):
        for s in range(CAP):
            for half in range(2):
                w[k, s * DEV : (s + 1) * DEV, half * 128 : half * 128 + 128] = asked[
                    pl.ds(s * 8 + k * 2 + half, DEV, stride=A_ROWS), :
                ]
    for m in range(4):
        total = None
        for k in range(4 - m):
            product = w[k] * w[k + m]
            high = product.astype(BF16)
            low = (product - high.astype(F32)).astype(BF16)
            part = dot(onehot_t, high) + dot(onehot_t, low)
            if k != 1:
                part = pltpu.roll(part, (k - 1) % NZ, 1)
            total = part if total is None else total + part
        d[m] = total
    wait_all(copies)
    owner_row = own[...]
    for s, mask in enumerate(masks_by_column(owner_row)):
        taken[:, s * DEV : (s + 1) * DEV] = ones(mask)
    for s, mask in enumerate(masks_by_owner(owner_row, 0, DEV)):
        for i in range(DEV // PART):
            row = i * CAP * PART + s * PART
            placed[row : row + PART] = ones(mask[i * PART : (i + 1) * PART])
    wait_all(sent + start_all(((placed, placed_hbm),), sems, 4))


def read_slots(ref):
    return jnp.concatenate(
        [
            jnp.concatenate(
                [ref[pl.ds(s * 2 + half, DEV, stride=V_ROWS), :] for half in range(2)], axis=1
            )
            for s in range(CAP)
        ],
        axis=0,
    )


def middle_kernel(arr, d, taken, w, b, placed_hbm, lam_out, out_hbm, placed, out, parts, tile, sems):
    copies = start_all(((placed_hbm, placed),), sems)
    under_way(tile)
    mine_all = select(taken[...], split(read_slots(arr)))
    rows = 128
    for start in range(0, COLS, rows):
        here = slice(start, start + rows)
        mine = mine_all[here]
        weights = [
            w[k, start // 16 : (start + rows) // 16].reshape(rows, NZ).astype(F32) for k in range(4)
        ]
        field = b[here]
        for k in range(4):
            field += weights[k] * (mine if k == 1 else pltpu.roll(mine, (1 - k) % NZ, 1))
        lam = d[0, here] * field
        for m in range(1, 4):
            lam += d[m, here] * pltpu.roll(field, NZ - m, 1) + pltpu.roll(d[m, here] * field, m, 1)
        lam_out[here] = lam
        spread = weights[1] * lam
        for k in (0, 2, 3):
            spread += pltpu.roll(weights[k] * lam, (k - 1) % NZ, 1)
        for i, part in enumerate(split(spread)):
            parts[i, here] = part
    wait_all(copies)
    sent = []
    for i, first in enumerate(range(0, DEV, PART)):
        onehot = placed[i * CAP * PART : (i + 1) * CAP * PART]
        put_slots(out, first * V_ROWS, select(onehot, [parts[p] for p in range(2)]), PART)
        here = pl.ds(first * V_ROWS, PART * V_ROWS)
        sent += start_all(((out.at[here], out_hbm.at[here]),), sems, i)
    wait_all(sent)


def blend_kernel(lam, wt_hbm, h_hbm, g_hbm, h, g, onehot, wt, g1, sems):
    copies = start_all(((wt_hbm, wt), (h_hbm, h), (g_hbm.at[0], g), (g_hbm.at[1], g1)), sems)
    copies[0].wait()
    onehot[...] = gathered_rows(wt[...], 0)
    wait_all(copies[1:])
    for c in range(3):
        h[c] = h[c] - 0.5 * (lam[...] * g1[c])


def final_kernel(arr, onehot, h, g, out_hbm, out, sems):
    lam = select(onehot[...], split(read_slots(arr)))
    sent = []
    for c in range(3):
        out[c] = h[c] - 0.5 * (lam * g[c])
        sent += start_all(((out.at[c], out_hbm.at[c]),), sems, c)
    wait_all(sent)


def exchange(value):
    return lax.all_to_all(value, AXES, split_axis=0, concat_axis=0, tiled=True)


def neighbours(first, last, axis):
    count = lax.axis_size(axis)
    up = [(i, (i + 1) % count) for i in range(count)]
    down = [(j, i) for i, j in up]
    return lax.ppermute(last, axis, up), lax.ppermute(first, axis, down)


def per_device(state_path, velocity, weights, owners, sources):
    owner_row = owners.reshape(2, 1, COLS)
    source_row = sources.reshape(2, 1, COLS)
    hbm = pl.BlockSpec(memory_space=pltpu.HBM)
    near = pl.BlockSpec(memory_space=pltpu.VMEM)
    struct = lambda *shape: pltpu.HBM(shape, F32)
    scratch = lambda *shape: pltpu.VMEM(shape, F32)
    sems = lambda count: pltpu.SemaphoreType.DMA((count,))
    per_field = lambda count: struct(count, 16, 16, NZ)

    edge_x, edge_y = pltpu.VMEM((5, 4, 16, NZ), F32), pltpu.VMEM((5, 16, 4, NZ), F32)
    request, first_x, last_x, first_y, last_y = call(
        request_kernel,
        (struct(DEV * A_ROWS, 128), edge_x, edge_x, edge_y, edge_y),
        16,
        3,
        in_specs=[hbm] * 5,
        out_specs=(hbm,) + (near,) * 4,
        scratch_shapes=[
            pltpu.VMEM((2, 1, COLS), jnp.int32),
            pltpu.VMEM((2, 1, COLS), jnp.int32),
            pltpu.VMEM((4, 16, 16, NZ), BF16),
            scratch(DEV * A_ROWS, 128),
            scratch(2, 5, 16, 8, NZ),
            scratch(16, 128),
            sems(15),
        ],
    )(owner_row, source_row, weights, state_path, velocity)
    asked = exchange(request.reshape(DEV, A_ROWS, 1, 128))

    halos = neighbours(first_x, last_x, "gx") + neighbours(first_y, last_y, "gy")
    slopes, before, hess, before_parts = call(
        stencil_kernel,
        (struct(2, 3, 16, 16, NZ), struct(16, 16, NZ), per_field(3), pltpu.VMEM((2, COLS, NZ), BF16)),
        24,
        1000,
        in_specs=[hbm] * 6,
        out_specs=(hbm,) * 3 + (near,),
        scratch_shapes=[
            scratch(5, 24, 16, NZ),
            scratch(5, 16, 32, NZ),
            scratch(5, 16, 4, NZ),
            scratch(5, 16, 4, NZ),
            scratch(2, 3, 16, 16, NZ),
            scratch(2, 16, 16, NZ),
            scratch(3, 16, 16, NZ),
            sems(14),
        ],
    )(state_path, velocity, *halos)

    supply = call(
        supply_kernel,
        struct(DEV * V_ROWS, 128),
        8,
        2,
        in_specs=[hbm, near],
        out_specs=hbm,
        scratch_shapes=[scratch(DEV, 1, 128), scratch(DEV * V_ROWS, 128), sems(8)],
    )(asked, before_parts)
    arrived = exchange(supply.reshape(DEV, CAP, 2, 128)).reshape(DEV * V_ROWS, 128)

    normal, taken, weight0, before1, placed, wanted_t = call(
        normal_kernel,
        (
            scratch(4, COLS, NZ),
            pltpu.VMEM((COLS, CAP * DEV), BF16),
            pltpu.VMEM((4, 16, 16, NZ), BF16),
            scratch(COLS, NZ),
            pltpu.HBM((CAP * DEV, COLS), BF16),
            struct(16, 128),
        ),
        20,
        4,
        in_specs=[hbm] * 4,
        out_specs=(near,) * 4 + (hbm,) * 2,
        scratch_shapes=[
            scratch(DEV * A_ROWS, 128),
            scratch(4, CAP * DEV, NZ),
            pltpu.VMEM((1, COLS), jnp.int32),
            scratch(16, 128),
            pltpu.VMEM((CAP * DEV, COLS), BF16),
            sems(5),
        ],
    )(asked.reshape(DEV * A_ROWS, 128), owner_row, weights, before.reshape(COLS, NZ))

    lam, push = call(
        middle_kernel,
        (scratch(COLS, NZ), struct(DEV * V_ROWS, 128)),
        8,
        4,
        in_specs=[near] * 5 + [hbm],
        out_specs=(near, hbm),
        scratch_shapes=[
            pltpu.VMEM((CAP * DEV, COLS), BF16),
            scratch(DEV * V_ROWS, 128),
            pltpu.VMEM((2, COLS, NZ), BF16),
            scratch(16, 128),
            sems(4),
        ],
    )(arrived, normal, taken, weight0, before1, placed)
    returned = exchange(push.reshape(DEV, CAP, 2, 128)).reshape(DEV * V_ROWS, 128)

    hess, slope0, onehot = call(
        blend_kernel,
        (scratch(3, COLS, NZ), scratch(3, COLS, NZ), pltpu.VMEM((COLS, CAP * DEV), BF16)),
        8,
        3,
        in_specs=[near] + [hbm] * 3,
        out_specs=(near,) * 3,
        scratch_shapes=[scratch(16, 128), scratch(3, COLS, NZ), sems(4)],
    )(lam, wanted_t, hess.reshape(3, COLS, NZ), slopes.reshape(2, 3, COLS, NZ))
    out = call(
        final_kernel,
        struct(3, COLS, NZ),
        8,
        2,
        in_specs=[near] * 4,
        out_specs=hbm,
        scratch_shapes=[scratch(3, COLS, NZ), sems(3)],
    )(returned, onehot, hess, slope0)
    return out.reshape(3, 16, 16, NZ)


def solution(mesh):
    return jax.shard_map(
        per_device,
        mesh=mesh,
        in_specs=(
            P(None, "gx", "gy", None),
            P(None, "gx", "gy", None),
            P(None, None, "gx", "gy", None),
            P(None, "gx", "gy", None, None),
            P(None, "gx", "gy", None),
        ),
        out_specs=P(None, "gx", "gy", None),
        check_vma=False,
    )
```

```python
import functools

import jax
import jax.numpy as jnp
from jax import lax
from jax.experimental import pallas as pl
from jax.experimental.pallas import tpu as pltpu
from jax.sharding import PartitionSpec as P

FIRST = (0.8, -0.2, 4.0 / 105.0, -1.0 / 280.0)
SECOND = (-205.0 / 72.0, 1.6, -0.2, 8.0 / 315.0, -1.0 / 560.0)
BETA = 0.05
AXES = ("gx", "gy")
CAP = 6
DEV = 128
COLS = 256
NZ = 256
F32 = jnp.float32
BF16 = jnp.bfloat16
W_ROWS = CAP * 8
A_ROWS = W_ROWS + 1
V_ROWS = CAP * 2
PART = 32


def call(kernel, out_shape, mib, micros, in_specs, **kw):
    run = pl.pallas_call(
        kernel,
        out_shape=out_shape,
        in_specs=in_specs,
        compiler_params=pltpu.CompilerParams(vmem_limit_bytes=mib * 1024 * 1024),
        cost_estimate=pl.CostEstimate(
            flops=int(micros * 1e8), bytes_accessed=int(micros * 2e6), transcendentals=0
        ),
        **kw,
    )

    def placed(*args):
        return run(
            *(
                pltpu.with_memory_space_constraint(x, pltpu.HBM) if spec.memory_space == pltpu.HBM else x
                for spec, x in zip(in_specs, args)
            )
        )

    return placed


def iota(shape, dim):
    return lax.broadcasted_iota(jnp.int32, shape, dim)


def dot(a, b):
    return jnp.dot(a, b, preferred_element_type=F32)


def split(x):
    hi = x.astype(BF16)
    return hi, (x - hi.astype(F32)).astype(BF16)


def select(onehot, parts):
    return sum(dot(onehot, part) for part in parts)


def ones(mask):
    return jnp.where(mask, 1.0, 0.0).astype(BF16)


def masks_by_owner(owner_row, first, count):
    match = iota((count, COLS), 0) + first == owner_row
    before = ones(iota((COLS, COLS), 0) < iota((COLS, COLS), 1))
    slot = dot(ones(match), before)
    return [match & (slot == float(s)) for s in range(CAP)]


def masks_by_column(owner_row):
    spread = jnp.broadcast_to(owner_row.astype(F32), (DEV, COLS)).T
    match = iota((COLS, DEV), 1).astype(F32) == spread
    before = ones(iota((COLS, COLS), 1) < iota((COLS, COLS), 0))
    slot = dot(before, ones(match))
    return [match & (slot == float(s)) for s in range(CAP)]


def put_slots(out_ref, start, values, count):
    for s in range(CAP):
        for half in range(2):
            out_ref[pl.ds(start + s * 2 + half, count, stride=V_ROWS), :] = values[
                s * count : (s + 1) * count, half * 128 : half * 128 + 128
            ]


def start_all(pairs, sems, first=0):
    copies = [
        pltpu.make_async_copy(source, target, sems.at[first + i])
        for i, (source, target) in enumerate(pairs)
    ]
    for copy in copies:
        copy.start()
    return copies


def under_way(tile):
    @pl.loop(0, 2)
    def touch(i):
        tile[pl.ds(i * 8, 8), :] = jnp.zeros((8, 128), F32)


def wait_all(copies):
    for copy in copies:
        copy.wait()


def request_kernel(
    own_hbm, src_hbm, w_hbm, st_hbm, ve_hbm, out_hbm, xlo, xhi, ylo, yhi, own, src, w, out, edges, tile, sems
):
    pairs = [(own_hbm, own), (src_hbm, src), (w_hbm.at[1], w)]
    for x_out, y_out, first, y_first in ((xlo, 0, 0, 0), (xhi, 1, 12, 8)):
        for source, place in ((st_hbm, pl.ds(0, 2)), (ve_hbm, pl.ds(2, 3))):
            pairs.append((source.at[:, pl.ds(first, 4)], x_out.at[place]))
            pairs.append((source.at[:, :, pl.ds(y_first, 8)], edges.at[y_out, place]))
    copies = start_all(pairs, sems)
    under_way(tile)
    wait_all(copies[:2])
    lane = iota((DEV, 128), 1)
    wanted = jnp.zeros((DEV, 128), F32)
    for j in range(2):
        masks = masks_by_owner(own[j], 0, DEV)
        source_row = src[j].astype(F32)
        for s in range(CAP):
            column = jnp.sum(jnp.where(masks[s], source_row, 0.0), axis=1, keepdims=True)
            wanted = jnp.where(lane == 8 * j + s, column, wanted)
    out[pl.ds(W_ROWS, DEV, stride=A_ROWS), :] = wanted
    copies[2].wait()
    sent = []
    for i, first in enumerate(range(0, DEV, PART)):
        onehot = jnp.concatenate([ones(m[first : first + PART]) for m in masks], axis=0)
        for k in range(4):
            placed = dot(onehot, w[k].reshape(COLS, NZ))
            for s in range(CAP):
                for half in range(2):
                    row = first * A_ROWS + s * 8 + k * 2 + half
                    out[pl.ds(row, PART, stride=A_ROWS), :] = placed[
                        s * PART : (s + 1) * PART, half * 128 : half * 128 + 128
                    ]
        block = pl.ds(first * A_ROWS, PART * A_ROWS)
        sent += start_all(((out.at[block], out_hbm.at[block]),), sems, 11 + i)
    wait_all(copies[3:])
    ylo[...] = edges[0, :, :, 0:4]
    yhi[...] = edges[1, :, :, 4:8]
    wait_all(sent)


def fill(sources, halos, xpad, ypad, ylo, yhi, sems, extra=()):
    pairs = list(extra) + [(halos[2], ylo), (halos[3], yhi)]
    pairs += [(halos[0], xpad.at[:, pl.ds(0, 4)]), (halos[1], xpad.at[:, pl.ds(20, 4)])]
    for i, source in enumerate(sources):
        pairs += [(source, xpad.at[i, pl.ds(4, 16)]), (source, ypad.at[i, :, pl.ds(8, 16)])]
    wait_all(start_all(pairs, sems))
    ypad[:, :, 4:8] = ylo[...]
    ypad[:, :, 24:28] = yhi[...]


def differences(xpad, ypad, i, x, rows, coeffs, sign):
    centre = xpad[i, pl.ds(x + 4, rows)]
    parts = [None, None, None]
    for k in range(4):
        d = k + 1
        terms = (
            xpad[i, pl.ds(x + 4 + d, rows)] + sign * xpad[i, pl.ds(x + 4 - d, rows)],
            ypad[i, pl.ds(x, rows), 8 + d : 24 + d, :] + sign * ypad[i, pl.ds(x, rows), 8 - d : 24 - d, :],
            pltpu.roll(centre, NZ - d, 2) + sign * pltpu.roll(centre, d, 2),
        )
        for c in range(3):
            term = coeffs[k] * terms[c]
            parts[c] = term if parts[c] is None else parts[c] + term
    return centre, parts


ROWS = 4


def stencil_kernel(
    st_hbm, ve_hbm, xlo, xhi, ylo, yhi, g_hbm, b_hbm, h_hbm, first_parts, xpad, ypad, ylo_scr, yhi_scr, g, b, h, sems
):
    sources = [st_hbm.at[j] for j in range(2)] + [ve_hbm.at[c] for c in range(3)]
    fill(sources, (xlo, xhi, ylo, yhi), xpad, ypad, ylo_scr, yhi_scr, sems)
    sent = []
    for j in range(2):

        @pl.loop(0, 16, step=ROWS)
        def slope_rows(x):
            here = pl.ds(x, ROWS)
            slope = differences(xpad, ypad, j, x, ROWS, FIRST, -1.0)[1]
            total = None
            for c in range(3):
                g[j, c, here] = slope[c]
                term = xpad[2 + c, pl.ds(x + 4, ROWS)] * slope[c]
                total = term if total is None else total + term
            b[j, here] = -0.5 * total

        sent += start_all(((g.at[j], g_hbm.at[j]),), sems, len(sent))
    for p, part in enumerate(split(b[0].reshape(COLS, NZ))):
        first_parts[p] = part
    sent += start_all(((b.at[1], b_hbm),), sems, len(sent))

    @pl.loop(0, 16, step=ROWS)
    def curve_rows(x):
        for c in range(3):
            centre, parts = differences(xpad, ypad, 2 + c, x, ROWS, SECOND[1:], 1.0)
            total = 3.0 * SECOND[0] * centre + parts[0] + parts[1] + parts[2]
            h[c, pl.ds(x, ROWS)] = -BETA * total

    sent += start_all(((h, h_hbm),), sems, len(sent))
    wait_all(sent)


def supply_kernel(asked_hbm, parts, out_hbm, asked, out, sems):
    wait_all(start_all(((asked_hbm.at[:, W_ROWS, 0], asked),), sems))
    wanted = asked[...]
    place = iota((PART, COLS), 1).astype(F32)
    sent = []
    for i, first in enumerate(range(0, DEV, PART)):
        onehot = jnp.concatenate(
            [ones(wanted[first : first + PART, s : s + 1] == place) for s in range(CAP)], axis=0
        )
        put_slots(out, first * V_ROWS, select(onehot, [parts[p] for p in range(2)]), PART)
        here = pl.ds(first * V_ROWS, PART * V_ROWS)
        sent += start_all(((out.at[here], out_hbm.at[here]),), sems, i)
    wait_all(sent)


def gathered_rows(wanted_t, first):
    place = iota((COLS, DEV), 0).astype(F32)
    return jnp.concatenate(
        [ones(place == wanted_t[first + s : first + s + 1, :]) for s in range(CAP)], axis=1
    )


def normal_kernel(asked_hbm, own_hbm, w_hbm, b_hbm, d, taken, w0, b, placed_hbm, wt_hbm, asked, w, own, wt, placed, sems):
    copies = start_all(((own_hbm.at[0], own), (w_hbm.at[0], w0), (b_hbm, b)), sems)
    wait_all(start_all(((asked_hbm, asked),), sems, 3))
    wanted_t = asked[pl.ds(W_ROWS, DEV, stride=A_ROWS), :].T
    wt[...] = wanted_t[:16]
    sent = start_all(((wt, wt_hbm),), sems, 3)
    onehot_t = gathered_rows(wanted_t, 8)
    for k in range(4):
        for s in range(CAP):
            for half in range(2):
                w[k, s * DEV : (s + 1) * DEV, half * 128 : half * 128 + 128] = asked[
                    pl.ds(s * 8 + k * 2 + half, DEV, stride=A_ROWS), :
                ]
    for m in range(4):
        total = None
        for k in range(4 - m):
            product = w[k] * w[k + m]
            high = product.astype(BF16)
            low = (product - high.astype(F32)).astype(BF16)
            part = dot(onehot_t, high) + dot(onehot_t, low)
            if k != 1:
                part = pltpu.roll(part, (k - 1) % NZ, 1)
            total = part if total is None else total + part
        d[m] = total
    wait_all(copies)
    owner_row = own[...]
    for s, mask in enumerate(masks_by_column(owner_row)):
        taken[:, s * DEV : (s + 1) * DEV] = ones(mask)
    for s, mask in enumerate(masks_by_owner(owner_row, 0, DEV)):
        for i in range(DEV // PART):
            row = i * CAP * PART + s * PART
            placed[row : row + PART] = ones(mask[i * PART : (i + 1) * PART])
    wait_all(sent + start_all(((placed, placed_hbm),), sems, 4))


def read_slots(ref):
    return jnp.concatenate(
        [
            jnp.concatenate(
                [ref[pl.ds(s * 2 + half, DEV, stride=V_ROWS), :] for half in range(2)], axis=1
            )
            for s in range(CAP)
        ],
        axis=0,
    )


def middle_kernel(arr, d, taken, w, b, placed_hbm, lam_out, out_hbm, placed, out, parts, tile, sems):
    copies = start_all(((placed_hbm, placed),), sems)
    under_way(tile)
    mine_all = select(taken[...], split(read_slots(arr)))
    rows = 128
    for start in range(0, COLS, rows):
        here = slice(start, start + rows)
        mine = mine_all[here]
        weights = [
            w[k, start // 16 : (start + rows) // 16].reshape(rows, NZ).astype(F32) for k in range(4)
        ]
        field = b[here]
        for k in range(4):
            field += weights[k] * (mine if k == 1 else pltpu.roll(mine, (1 - k) % NZ, 1))
        lam = d[0, here] * field
        for m in range(1, 4):
            lam += d[m, here] * pltpu.roll(field, NZ - m, 1) + pltpu.roll(d[m, here] * field, m, 1)
        lam_out[here] = lam
        spread = weights[1] * lam
        for k in (0, 2, 3):
            spread += pltpu.roll(weights[k] * lam, (k - 1) % NZ, 1)
        for i, part in enumerate(split(spread)):
            parts[i, here] = part
    wait_all(copies)
    sent = []
    for i, first in enumerate(range(0, DEV, PART)):
        onehot = placed[i * CAP * PART : (i + 1) * CAP * PART]
        put_slots(out, first * V_ROWS, select(onehot, [parts[p] for p in range(2)]), PART)
        here = pl.ds(first * V_ROWS, PART * V_ROWS)
        sent += start_all(((out.at[here], out_hbm.at[here]),), sems, i)
    wait_all(sent)


def blend_kernel(lam, wt_hbm, h_hbm, g_hbm, h, g, onehot, wt, g1, sems):
    copies = start_all(((wt_hbm, wt), (h_hbm, h), (g_hbm.at[0], g), (g_hbm.at[1], g1)), sems)
    copies[0].wait()
    onehot[...] = gathered_rows(wt[...], 0)
    wait_all(copies[1:])
    for c in range(3):
        h[c] = h[c] - 0.5 * (lam[...] * g1[c])


def final_kernel(arr, onehot, h, g, out_hbm, out, sems):
    lam = select(onehot[...], split(read_slots(arr)))
    sent = []
    for c in range(3):
        out[c] = h[c] - 0.5 * (lam * g[c])
        sent += start_all(((out.at[c], out_hbm.at[c]),), sems, c)
    wait_all(sent)


def exchange(value):
    return lax.all_to_all(value, AXES, split_axis=0, concat_axis=0, tiled=True)


def neighbours(first, last, axis):
    count = lax.axis_size(axis)
    up = [(i, (i + 1) % count) for i in range(count)]
    down = [(j, i) for i, j in up]
    return lax.ppermute(last, axis, up), lax.ppermute(first, axis, down)


def per_device(state_path, velocity, weights, owners, sources):
    owner_row = owners.reshape(2, 1, COLS)
    source_row = sources.reshape(2, 1, COLS)
    hbm = pl.BlockSpec(memory_space=pltpu.HBM)
    near = pl.BlockSpec(memory_space=pltpu.VMEM)
    struct = lambda *shape: pltpu.HBM(shape, F32)
    scratch = lambda *shape: pltpu.VMEM(shape, F32)
    sems = lambda count: pltpu.SemaphoreType.DMA((count,))
    per_field = lambda count: struct(count, 16, 16, NZ)

    edge_x, edge_y = pltpu.VMEM((5, 4, 16, NZ), F32), pltpu.VMEM((5, 16, 4, NZ), F32)
    request, first_x, last_x, first_y, last_y = call(
        request_kernel,
        (struct(DEV * A_ROWS, 128), edge_x, edge_x, edge_y, edge_y),
        16,
        3,
        in_specs=[hbm] * 5,
        out_specs=(hbm,) + (near,) * 4,
        scratch_shapes=[
            pltpu.VMEM((2, 1, COLS), jnp.int32),
            pltpu.VMEM((2, 1, COLS), jnp.int32),
            pltpu.VMEM((4, 16, 16, NZ), BF16),
            scratch(DEV * A_ROWS, 128),
            scratch(2, 5, 16, 8, NZ),
            scratch(16, 128),
            sems(15),
        ],
    )(owner_row, source_row, weights, state_path, velocity)
    asked = exchange(request.reshape(DEV, A_ROWS, 1, 128))

    halos = neighbours(first_x, last_x, "gx") + neighbours(first_y, last_y, "gy")
    slopes, before, hess, before_parts = call(
        stencil_kernel,
        (struct(2, 3, 16, 16, NZ), struct(16, 16, NZ), per_field(3), pltpu.VMEM((2, COLS, NZ), BF16)),
        24,
        1000,
        in_specs=[hbm] * 6,
        out_specs=(hbm,) * 3 + (near,),
        scratch_shapes=[
            scratch(5, 24, 16, NZ),
            scratch(5, 16, 32, NZ),
            scratch(5, 16, 4, NZ),
            scratch(5, 16, 4, NZ),
            scratch(2, 3, 16, 16, NZ),
            scratch(2, 16, 16, NZ),
            scratch(3, 16, 16, NZ),
            sems(14),
        ],
    )(state_path, velocity, *halos)

    supply = call(
        supply_kernel,
        struct(DEV * V_ROWS, 128),
        8,
        2,
        in_specs=[hbm, near],
        out_specs=hbm,
        scratch_shapes=[scratch(DEV, 128), scratch(DEV * V_ROWS, 128), sems(4)],
    )(asked, before_parts)
    arrived = exchange(supply.reshape(DEV, CAP, 2, 128)).reshape(DEV * V_ROWS, 128)

    normal, taken, weight0, before1, placed, wanted_t = call(
        normal_kernel,
        (
            scratch(4, COLS, NZ),
            pltpu.VMEM((COLS, CAP * DEV), BF16),
            pltpu.VMEM((4, 16, 16, NZ), BF16),
            scratch(COLS, NZ),
            pltpu.HBM((CAP * DEV, COLS), BF16),
            struct(16, 128),
        ),
        20,
        4,
        in_specs=[hbm] * 4,
        out_specs=(near,) * 4 + (hbm,) * 2,
        scratch_shapes=[
            scratch(DEV * A_ROWS, 128),
            scratch(4, CAP * DEV, NZ),
            pltpu.VMEM((1, COLS), jnp.int32),
            scratch(16, 128),
            pltpu.VMEM((CAP * DEV, COLS), BF16),
            sems(5),
        ],
    )(asked.reshape(DEV * A_ROWS, 128), owner_row, weights, before.reshape(COLS, NZ))

    lam, push = call(
        middle_kernel,
        (scratch(COLS, NZ), struct(DEV * V_ROWS, 128)),
        8,
        4,
        in_specs=[near] * 5 + [hbm],
        out_specs=(near, hbm),
        scratch_shapes=[
            pltpu.VMEM((CAP * DEV, COLS), BF16),
            scratch(DEV * V_ROWS, 128),
            pltpu.VMEM((2, COLS, NZ), BF16),
            scratch(16, 128),
            sems(4),
        ],
    )(arrived, normal, taken, weight0, before1, placed)
    returned = exchange(push.reshape(DEV, CAP, 2, 128)).reshape(DEV * V_ROWS, 128)

    hess, slope0, onehot = call(
        blend_kernel,
        (scratch(3, COLS, NZ), scratch(3, COLS, NZ), pltpu.VMEM((COLS, CAP * DEV), BF16)),
        8,
        3,
        in_specs=[near] + [hbm] * 3,
        out_specs=(near,) * 3,
        scratch_shapes=[scratch(16, 128), scratch(3, COLS, NZ), sems(4)],
    )(lam, wanted_t, hess.reshape(3, COLS, NZ), slopes.reshape(2, 3, COLS, NZ))
    out = call(
        final_kernel,
        struct(3, COLS, NZ),
        8,
        2,
        in_specs=[near] * 4,
        out_specs=hbm,
        scratch_shapes=[scratch(3, COLS, NZ), sems(3)],
    )(returned, onehot, hess, slope0)
    return out.reshape(3, 16, 16, NZ)


def solution(mesh):
    return jax.shard_map(
        per_device,
        mesh=mesh,
        in_specs=(
            P(None, "gx", "gy", None),
            P(None, "gx", "gy", None),
            P(None, None, "gx", "gy", None),
            P(None, "gx", "gy", None, None),
            P(None, "gx", "gy", None),
        ),
        out_specs=P(None, "gx", "gy", None),
        check_vma=False,
    )
```

```python
import functools

import jax
import jax.numpy as jnp
from jax import lax
from jax.experimental import pallas as pl
from jax.experimental.pallas import tpu as pltpu
from jax.sharding import PartitionSpec as P

FIRST = (0.8, -0.2, 4.0 / 105.0, -1.0 / 280.0)
SECOND = (-205.0 / 72.0, 1.6, -0.2, 8.0 / 315.0, -1.0 / 560.0)
BETA = 0.05
AXES = ("gx", "gy")
CAP = 6
DEV = 128
COLS = 256
NZ = 256
F32 = jnp.float32
BF16 = jnp.bfloat16
W_ROWS = CAP * 8
A_ROWS = W_ROWS + 1
V_ROWS = CAP * 2
PART = 32


def call(kernel, out_shape, mib, micros, in_specs, **kw):
    run = pl.pallas_call(
        kernel,
        out_shape=out_shape,
        in_specs=in_specs,
        compiler_params=pltpu.CompilerParams(vmem_limit_bytes=mib * 1024 * 1024),
        cost_estimate=pl.CostEstimate(
            flops=int(micros * 1e8), bytes_accessed=int(micros * 2e6), transcendentals=0
        ),
        **kw,
    )

    def placed(*args):
        return run(
            *(
                pltpu.with_memory_space_constraint(x, pltpu.HBM) if spec.memory_space == pltpu.HBM else x
                for spec, x in zip(in_specs, args)
            )
        )

    return placed


def iota(shape, dim):
    return lax.broadcasted_iota(jnp.int32, shape, dim)


def dot(a, b):
    return jnp.dot(a, b, preferred_element_type=F32)


def split(x):
    hi = x.astype(BF16)
    return hi, (x - hi.astype(F32)).astype(BF16)


def select(onehot, parts):
    return sum(dot(onehot, part) for part in parts)


def ones(mask):
    return jnp.where(mask, 1.0, 0.0).astype(BF16)


def masks_by_owner(owner_row, first, count):
    match = iota((count, COLS), 0) + first == owner_row
    before = ones(iota((COLS, COLS), 0) < iota((COLS, COLS), 1))
    slot = dot(ones(match), before)
    return [match & (slot == float(s)) for s in range(CAP)]


def masks_by_column(owner_row):
    spread = jnp.broadcast_to(owner_row.astype(F32), (DEV, COLS)).T
    match = iota((COLS, DEV), 1).astype(F32) == spread
    before = ones(iota((COLS, COLS), 1) < iota((COLS, COLS), 0))
    slot = dot(before, ones(match))
    return [match & (slot == float(s)) for s in range(CAP)]


def put_slots(out_ref, start, values, count):
    for s in range(CAP):
        for half in range(2):
            out_ref[pl.ds(start + s * 2 + half, count, stride=V_ROWS), :] = values[
                s * count : (s + 1) * count, half * 128 : half * 128 + 128
            ]


def start_all(pairs, sems, first=0):
    copies = [
        pltpu.make_async_copy(source, target, sems.at[first + i])
        for i, (source, target) in enumerate(pairs)
    ]
    for copy in copies:
        copy.start()
    return copies


def under_way(tile):
    @pl.loop(0, 2)
    def touch(i):
        tile[pl.ds(i * 8, 8), :] = jnp.zeros((8, 128), F32)


def wait_all(copies):
    for copy in copies:
        copy.wait()


def request_kernel(
    own_hbm, src_hbm, w_hbm, st_hbm, ve_hbm, out_hbm, xlo, xhi, ylo, yhi, own, src, w, out, edges, tile, sems
):
    pairs = [(own_hbm, own), (src_hbm, src), (w_hbm.at[1], w)]
    for x_out, y_out, first, y_first in ((xlo, 0, 0, 0), (xhi, 1, 12, 8)):
        for source, place in ((st_hbm, pl.ds(0, 2)), (ve_hbm, pl.ds(2, 3))):
            pairs.append((source.at[:, pl.ds(first, 4)], x_out.at[place]))
            pairs.append((source.at[:, :, pl.ds(y_first, 8)], edges.at[y_out, place]))
    copies = start_all(pairs, sems)
    under_way(tile)
    wait_all(copies[:2])
    lane = iota((DEV, 128), 1)
    wanted = jnp.zeros((DEV, 128), F32)
    for j in range(2):
        masks = masks_by_owner(own[j], 0, DEV)
        source_row = src[j].astype(F32)
        for s in range(CAP):
            column = jnp.sum(jnp.where(masks[s], source_row, 0.0), axis=1, keepdims=True)
            wanted = jnp.where(lane == 8 * j + s, column, wanted)
    out[pl.ds(W_ROWS, DEV, stride=A_ROWS), :] = wanted
    copies[2].wait()
    sent = []
    for i, first in enumerate(range(0, DEV, PART)):
        onehot = jnp.concatenate([ones(m[first : first + PART]) for m in masks], axis=0)
        for k in range(4):
            placed = dot(onehot, w[k].reshape(COLS, NZ))
            for s in range(CAP):
                for half in range(2):
                    row = first * A_ROWS + s * 8 + k * 2 + half
                    out[pl.ds(row, PART, stride=A_ROWS), :] = placed[
                        s * PART : (s + 1) * PART, half * 128 : half * 128 + 128
                    ]
        block = pl.ds(first * A_ROWS, PART * A_ROWS)
        sent += start_all(((out.at[block], out_hbm.at[block]),), sems, 11 + i)
    wait_all(copies[3:])
    ylo[...] = edges[0, :, :, 0:4]
    yhi[...] = edges[1, :, :, 4:8]
    wait_all(sent)


def fill(sources, halos, xpad, ypad, ylo, yhi, sems, extra=()):
    pairs = list(extra) + [(halos[2], ylo), (halos[3], yhi)]
    pairs += [(halos[0], xpad.at[:, pl.ds(0, 4)]), (halos[1], xpad.at[:, pl.ds(20, 4)])]
    for i, source in enumerate(sources):
        pairs += [(source, xpad.at[i, pl.ds(4, 16)]), (source, ypad.at[i, :, pl.ds(8, 16)])]
    wait_all(start_all(pairs, sems))
    ypad[:, :, 4:8] = ylo[...]
    ypad[:, :, 24:28] = yhi[...]


def differences(xpad, ypad, i, x, rows, coeffs, sign):
    centre = xpad[i, pl.ds(x + 4, rows)]
    parts = [None, None, None]
    for k in range(4):
        d = k + 1
        terms = (
            xpad[i, pl.ds(x + 4 + d, rows)] + sign * xpad[i, pl.ds(x + 4 - d, rows)],
            ypad[i, pl.ds(x, rows), 8 + d : 24 + d, :] + sign * ypad[i, pl.ds(x, rows), 8 - d : 24 - d, :],
            pltpu.roll(centre, NZ - d, 2) + sign * pltpu.roll(centre, d, 2),
        )
        for c in range(3):
            term = coeffs[k] * terms[c]
            parts[c] = term if parts[c] is None else parts[c] + term
    return centre, parts


ROWS = 4


def stencil_kernel(
    st_hbm, ve_hbm, xlo, xhi, ylo, yhi, g_hbm, b_hbm, h_hbm, first_parts, xpad, ypad, ylo_scr, yhi_scr, g, b, h, sems
):
    sources = [st_hbm.at[j] for j in range(2)] + [ve_hbm.at[c] for c in range(3)]
    fill(sources, (xlo, xhi, ylo, yhi), xpad, ypad, ylo_scr, yhi_scr, sems)
    sent = []
    for j in range(2):

        @pl.loop(0, 16, step=ROWS)
        def slope_rows(x):
            here = pl.ds(x, ROWS)
            slope = differences(xpad, ypad, j, x, ROWS, FIRST, -1.0)[1]
            total = None
            for c in range(3):
                g[j, c, here] = slope[c]
                term = xpad[2 + c, pl.ds(x + 4, ROWS)] * slope[c]
                total = term if total is None else total + term
            b[j, here] = -0.5 * total

        sent += start_all(((g.at[j], g_hbm.at[j]),), sems, len(sent))
    for p, part in enumerate(split(b[0].reshape(COLS, NZ))):
        first_parts[p] = part
    sent += start_all(((b.at[1], b_hbm),), sems, len(sent))

    @pl.loop(0, 16, step=ROWS)
    def curve_rows(x):
        for c in range(3):
            centre, parts = differences(xpad, ypad, 2 + c, x, ROWS, SECOND[1:], 1.0)
            total = 3.0 * SECOND[0] * centre + parts[0] + parts[1] + parts[2]
            h[c, pl.ds(x, ROWS)] = -BETA * total

    sent += start_all(((h, h_hbm),), sems, len(sent))
    wait_all(sent)


def supply_kernel(asked_hbm, parts, out_hbm, asked, out, sems):
    wait_all(start_all(((asked_hbm.at[:, W_ROWS, 0], asked),), sems))
    wanted = asked[...]
    place = iota((PART, COLS), 1).astype(F32)
    sent = []
    for i, first in enumerate(range(0, DEV, PART)):
        onehot = jnp.concatenate(
            [ones(wanted[first : first + PART, s : s + 1] == place) for s in range(CAP)], axis=0
        )
        put_slots(out, first * V_ROWS, select(onehot, [parts[p] for p in range(2)]), PART)
        here = pl.ds(first * V_ROWS, PART * V_ROWS)
        sent += start_all(((out.at[here], out_hbm.at[here]),), sems, i)
    wait_all(sent)


def gathered_rows(wanted_t, first):
    place = iota((COLS, DEV), 0).astype(F32)
    return jnp.concatenate(
        [ones(place == wanted_t[first + s : first + s + 1, :]) for s in range(CAP)], axis=1
    )


def normal_kernel(asked_hbm, own_hbm, w_hbm, b_hbm, d, taken, w0, b, placed_hbm, wt_hbm, asked, w, own, wt, placed, sems):
    copies = start_all(((own_hbm.at[0], own), (w_hbm.at[0], w0), (b_hbm, b)), sems)
    wait_all(start_all(((asked_hbm, asked),), sems, 3))
    wanted_t = asked[pl.ds(W_ROWS, DEV, stride=A_ROWS), :].T
    wt[...] = wanted_t[:16]
    sent = start_all(((wt, wt_hbm),), sems, 3)
    onehot_t = gathered_rows(wanted_t, 8)
    for k in range(4):
        for s in range(CAP):
            for half in range(2):
                w[k, s * DEV : (s + 1) * DEV, half * 128 : half * 128 + 128] = asked[
                    pl.ds(s * 8 + k * 2 + half, DEV, stride=A_ROWS), :
                ]
    for m in range(4):
        total = None
        for k in range(4 - m):
            product = w[k] * w[k + m]
            high = product.astype(BF16)
            low = (product - high.astype(F32)).astype(BF16)
            part = dot(onehot_t, high) + dot(onehot_t, low)
            if k != 1:
                part = pltpu.roll(part, (k - 1) % NZ, 1)
            total = part if total is None else total + part
        d[m] = total
    wait_all(copies)
    owner_row = own[...]
    for s, mask in enumerate(masks_by_column(owner_row)):
        taken[:, s * DEV : (s + 1) * DEV] = ones(mask)
    for s, mask in enumerate(masks_by_owner(owner_row, 0, DEV)):
        for i in range(DEV // PART):
            row = i * CAP * PART + s * PART
            placed[row : row + PART] = ones(mask[i * PART : (i + 1) * PART])
    wait_all(sent + start_all(((placed, placed_hbm),), sems, 4))


def read_slots(ref):
    return jnp.concatenate(
        [
            jnp.concatenate(
                [ref[pl.ds(s * 2 + half, DEV, stride=V_ROWS), :] for half in range(2)], axis=1
            )
            for s in range(CAP)
        ],
        axis=0,
    )


def middle_kernel(arr, d, taken, w, b, placed_hbm, lam_out, out_hbm, placed, out, parts, tile, sems):
    copies = start_all(((placed_hbm, placed),), sems)
    under_way(tile)
    received = split(read_slots(arr))
    rows = 128
    for start in range(0, COLS, rows):
        here = slice(start, start + rows)
        mine = select(taken[here], received)
        weights = [
            w[k, start // 16 : (start + rows) // 16].reshape(rows, NZ).astype(F32) for k in range(4)
        ]
        field = b[here]
        for k in range(4):
            field += weights[k] * (mine if k == 1 else pltpu.roll(mine, (1 - k) % NZ, 1))
        lam = d[0, here] * field
        for m in range(1, 4):
            lam += d[m, here] * pltpu.roll(field, NZ - m, 1) + pltpu.roll(d[m, here] * field, m, 1)
        lam_out[here] = lam
        spread = weights[1] * lam
        for k in (0, 2, 3):
            spread += pltpu.roll(weights[k] * lam, (k - 1) % NZ, 1)
        for i, part in enumerate(split(spread)):
            parts[i, here] = part
    wait_all(copies)
    sent = []
    for i, first in enumerate(range(0, DEV, PART)):
        onehot = placed[i * CAP * PART : (i + 1) * CAP * PART]
        put_slots(out, first * V_ROWS, select(onehot, [parts[p] for p in range(2)]), PART)
        here = pl.ds(first * V_ROWS, PART * V_ROWS)
        sent += start_all(((out.at[here], out_hbm.at[here]),), sems, i)
    wait_all(sent)


def blend_kernel(lam, wt_hbm, h_hbm, g_hbm, h, g, onehot, wt, g1, sems):
    copies = start_all(((wt_hbm, wt), (h_hbm, h), (g_hbm.at[0], g), (g_hbm.at[1], g1)), sems)
    copies[0].wait()
    onehot[...] = gathered_rows(wt[...], 0)
    wait_all(copies[1:])
    for c in range(3):
        h[c] = h[c] - 0.5 * (lam[...] * g1[c])


def final_kernel(arr, onehot, h, g, out_hbm, out, sems):
    lam = select(onehot[...], split(read_slots(arr)))
    sent = []
    for c in range(3):
        out[c] = h[c] - 0.5 * (lam * g[c])
        sent += start_all(((out.at[c], out_hbm.at[c]),), sems, c)
    wait_all(sent)


def exchange(value):
    return lax.all_to_all(value, AXES, split_axis=0, concat_axis=0, tiled=True)


def neighbours(first, last, axis):
    count = lax.axis_size(axis)
    up = [(i, (i + 1) % count) for i in range(count)]
    down = [(j, i) for i, j in up]
    return lax.ppermute(last, axis, up), lax.ppermute(first, axis, down)


def per_device(state_path, velocity, weights, owners, sources):
    owner_row = owners.reshape(2, 1, COLS)
    source_row = sources.reshape(2, 1, COLS)
    hbm = pl.BlockSpec(memory_space=pltpu.HBM)
    near = pl.BlockSpec(memory_space=pltpu.VMEM)
    struct = lambda *shape: pltpu.HBM(shape, F32)
    scratch = lambda *shape: pltpu.VMEM(shape, F32)
    sems = lambda count: pltpu.SemaphoreType.DMA((count,))
    per_field = lambda count: struct(count, 16, 16, NZ)

    edge_x, edge_y = pltpu.VMEM((5, 4, 16, NZ), F32), pltpu.VMEM((5, 16, 4, NZ), F32)
    request, first_x, last_x, first_y, last_y = call(
        request_kernel,
        (struct(DEV * A_ROWS, 128), edge_x, edge_x, edge_y, edge_y),
        16,
        3,
        in_specs=[hbm] * 5,
        out_specs=(hbm,) + (near,) * 4,
        scratch_shapes=[
            pltpu.VMEM((2, 1, COLS), jnp.int32),
            pltpu.VMEM((2, 1, COLS), jnp.int32),
            pltpu.VMEM((4, 16, 16, NZ), BF16),
            scratch(DEV * A_ROWS, 128),
            scratch(2, 5, 16, 8, NZ),
            scratch(16, 128),
            sems(15),
        ],
    )(owner_row, source_row, weights, state_path, velocity)
    asked = exchange(request.reshape(DEV, A_ROWS, 1, 128))

    halos = neighbours(first_x, last_x, "gx") + neighbours(first_y, last_y, "gy")
    slopes, before, hess, before_parts = call(
        stencil_kernel,
        (struct(2, 3, 16, 16, NZ), struct(16, 16, NZ), per_field(3), pltpu.VMEM((2, COLS, NZ), BF16)),
        24,
        1000,
        in_specs=[hbm] * 6,
        out_specs=(hbm,) * 3 + (near,),
        scratch_shapes=[
            scratch(5, 24, 16, NZ),
            scratch(5, 16, 32, NZ),
            scratch(5, 16, 4, NZ),
            scratch(5, 16, 4, NZ),
            scratch(2, 3, 16, 16, NZ),
            scratch(2, 16, 16, NZ),
            scratch(3, 16, 16, NZ),
            sems(14),
        ],
    )(state_path, velocity, *halos)

    supply = call(
        supply_kernel,
        struct(DEV * V_ROWS, 128),
        8,
        2,
        in_specs=[hbm, near],
        out_specs=hbm,
        scratch_shapes=[scratch(DEV, 128), scratch(DEV * V_ROWS, 128), sems(4)],
    )(asked, before_parts)
    arrived = exchange(supply.reshape(DEV, CAP, 2, 128)).reshape(DEV * V_ROWS, 128)

    normal, taken, weight0, before1, placed, wanted_t = call(
        normal_kernel,
        (
            scratch(4, COLS, NZ),
            pltpu.VMEM((COLS, CAP * DEV), BF16),
            pltpu.VMEM((4, 16, 16, NZ), BF16),
            scratch(COLS, NZ),
            pltpu.HBM((CAP * DEV, COLS), BF16),
            struct(16, 128),
        ),
        20,
        4,
        in_specs=[hbm] * 4,
        out_specs=(near,) * 4 + (hbm,) * 2,
        scratch_shapes=[
            scratch(DEV * A_ROWS, 128),
            scratch(4, CAP * DEV, NZ),
            pltpu.VMEM((1, COLS), jnp.int32),
            scratch(16, 128),
            pltpu.VMEM((CAP * DEV, COLS), BF16),
            sems(5),
        ],
    )(asked.reshape(DEV * A_ROWS, 128), owner_row, weights, before.reshape(COLS, NZ))

    lam, push = call(
        middle_kernel,
        (scratch(COLS, NZ), struct(DEV * V_ROWS, 128)),
        8,
        4,
        in_specs=[near] * 5 + [hbm],
        out_specs=(near, hbm),
        scratch_shapes=[
            pltpu.VMEM((CAP * DEV, COLS), BF16),
            scratch(DEV * V_ROWS, 128),
            pltpu.VMEM((2, COLS, NZ), BF16),
            scratch(16, 128),
            sems(4),
        ],
    )(arrived, normal, taken, weight0, before1, placed)
    returned = exchange(push.reshape(DEV, CAP, 2, 128)).reshape(DEV * V_ROWS, 128)

    hess, slope0, onehot = call(
        blend_kernel,
        (scratch(3, COLS, NZ), scratch(3, COLS, NZ), pltpu.VMEM((COLS, CAP * DEV), BF16)),
        8,
        3,
        in_specs=[near] + [hbm] * 3,
        out_specs=(near,) * 3,
        scratch_shapes=[scratch(16, 128), scratch(3, COLS, NZ), sems(4)],
    )(lam, wanted_t, hess.reshape(3, COLS, NZ), slopes.reshape(2, 3, COLS, NZ))
    out = call(
        final_kernel,
        struct(3, COLS, NZ),
        8,
        2,
        in_specs=[near] * 4,
        out_specs=hbm,
        scratch_shapes=[scratch(3, COLS, NZ), sems(3)],
    )(returned, onehot, hess, slope0)
    return out.reshape(3, 16, 16, NZ)


def solution(mesh):
    return jax.shard_map(
        per_device,
        mesh=mesh,
        in_specs=(
            P(None, "gx", "gy", None),
            P(None, "gx", "gy", None),
            P(None, None, "gx", "gy", None),
            P(None, "gx", "gy", None, None),
            P(None, "gx", "gy", None),
        ),
        out_specs=P(None, "gx", "gy", None),
        check_vma=False,
    )
```

```python
import functools

import jax
import jax.numpy as jnp
from jax import lax
from jax.experimental import pallas as pl
from jax.experimental.pallas import tpu as pltpu
from jax.sharding import PartitionSpec as P

FIRST = (0.8, -0.2, 4.0 / 105.0, -1.0 / 280.0)
SECOND = (-205.0 / 72.0, 1.6, -0.2, 8.0 / 315.0, -1.0 / 560.0)
BETA = 0.05
AXES = ("gx", "gy")
CAP = 6
DEV = 128
COLS = 256
NZ = 256
F32 = jnp.float32
BF16 = jnp.bfloat16
W_ROWS = CAP * 8
A_ROWS = W_ROWS + 1
V_ROWS = CAP * 2
PART = 32


def call(kernel, out_shape, mib, micros, in_specs, **kw):
    run = pl.pallas_call(
        kernel,
        out_shape=out_shape,
        in_specs=in_specs,
        compiler_params=pltpu.CompilerParams(vmem_limit_bytes=mib * 1024 * 1024),
        cost_estimate=pl.CostEstimate(
            flops=int(micros * 1e8), bytes_accessed=int(micros * 2e6), transcendentals=0
        ),
        **kw,
    )

    def placed(*args):
        return run(
            *(
                pltpu.with_memory_space_constraint(x, pltpu.HBM) if spec.memory_space == pltpu.HBM else x
                for spec, x in zip(in_specs, args)
            )
        )

    return placed


def iota(shape, dim):
    return lax.broadcasted_iota(jnp.int32, shape, dim)


def dot(a, b):
    return jnp.dot(a, b, preferred_element_type=F32)


def split(x):
    hi = x.astype(BF16)
    return hi, (x - hi.astype(F32)).astype(BF16)


def select(onehot, parts):
    return sum(dot(onehot, part) for part in parts)


def ones(mask):
    return jnp.where(mask, 1.0, 0.0).astype(BF16)


def masks_by_owner(owner_row, first, count):
    match = iota((count, COLS), 0) + first == owner_row
    before = ones(iota((COLS, COLS), 0) < iota((COLS, COLS), 1))
    slot = dot(ones(match), before)
    return [match & (slot == float(s)) for s in range(CAP)]


def masks_by_column(owner_row):
    spread = jnp.broadcast_to(owner_row.astype(F32), (DEV, COLS)).T
    match = iota((COLS, DEV), 1).astype(F32) == spread
    before = ones(iota((COLS, COLS), 1) < iota((COLS, COLS), 0))
    slot = dot(before, ones(match))
    return [match & (slot == float(s)) for s in range(CAP)]


def put_slots(out_ref, start, values, count):
    for s in range(CAP):
        for half in range(2):
            out_ref[pl.ds(start + s * 2 + half, count, stride=V_ROWS), :] = values[
                s * count : (s + 1) * count, half * 128 : half * 128 + 128
            ]


def start_all(pairs, sems, first=0):
    copies = [
        pltpu.make_async_copy(source, target, sems.at[first + i])
        for i, (source, target) in enumerate(pairs)
    ]
    for copy in copies:
        copy.start()
    return copies


def under_way(tile):
    @pl.loop(0, 2)
    def touch(i):
        tile[pl.ds(i * 8, 8), :] = jnp.zeros((8, 128), F32)


def odd(axis):
    return lax.rem(lax.axis_index(axis), 2)


def wait_all(copies):
    for copy in copies:
        copy.wait()


def request_kernel(
    own_hbm, src_hbm, w_hbm, st_hbm, ve_hbm, out_hbm, xin, xout, yin, yout, own, src, w, out, edges, tile, sems
):
    pairs = [(own_hbm, own), (src_hbm, src), (w_hbm.at[1], w)]
    odd_x, odd_y = odd("gx"), odd("gy")
    for x_out, y_out, first, y_first in ((xin, 0, 12 - 12 * odd_x, 0), (xout, 1, 12 * odd_x, 8)):
        for source, place in ((st_hbm, pl.ds(0, 2)), (ve_hbm, pl.ds(2, 3))):
            pairs.append((source.at[:, pl.ds(first, 4)], x_out.at[place]))
            pairs.append((source.at[:, :, pl.ds(y_first, 8)], edges.at[y_out, place]))
    copies = start_all(pairs, sems)
    under_way(tile)
    wait_all(copies[:2])
    lane = iota((DEV, 128), 1)
    wanted = jnp.zeros((DEV, 128), F32)
    for j in range(2):
        masks = masks_by_owner(own[j], 0, DEV)
        source_row = src[j].astype(F32)
        for s in range(CAP):
            column = jnp.sum(jnp.where(masks[s], source_row, 0.0), axis=1, keepdims=True)
            wanted = jnp.where(lane == 8 * j + s, column, wanted)
    out[pl.ds(W_ROWS, DEV, stride=A_ROWS), :] = wanted
    copies[2].wait()
    sent = []
    for i, first in enumerate(range(0, DEV, PART)):
        onehot = jnp.concatenate([ones(m[first : first + PART]) for m in masks], axis=0)
        for k in range(4):
            placed = dot(onehot, w[k].reshape(COLS, NZ))
            for s in range(CAP):
                for half in range(2):
                    row = first * A_ROWS + s * 8 + k * 2 + half
                    out[pl.ds(row, PART, stride=A_ROWS), :] = placed[
                        s * PART : (s + 1) * PART, half * 128 : half * 128 + 128
                    ]
        block = pl.ds(first * A_ROWS, PART * A_ROWS)
        sent += start_all(((out.at[block], out_hbm.at[block]),), sems, 11 + i)
    wait_all(copies[3:])
    yin[...] = jnp.where(odd_y == 1, edges[0, :, :, 0:4], edges[1, :, :, 4:8])
    yout[...] = jnp.where(odd_y == 1, edges[1, :, :, 4:8], edges[0, :, :, 0:4])
    wait_all(sent)


def fill(sources, halos, xpad, ypad, yin, yout, sems):
    odd_x, odd_y = odd("gx"), odd("gy")
    pairs = [(halos[2], yin), (halos[3], yout)]
    pairs += [(halos[0], xpad.at[:, pl.ds(20 - 20 * odd_x, 4)]), (halos[1], xpad.at[:, pl.ds(20 * odd_x, 4)])]
    for i, source in enumerate(sources):
        pairs += [(source, xpad.at[i, pl.ds(4, 16)]), (source, ypad.at[i, :, pl.ds(8, 16)])]
    wait_all(start_all(pairs, sems))
    ypad[:, :, 4:8] = jnp.where(odd_y == 1, yin[...], yout[...])
    ypad[:, :, 24:28] = jnp.where(odd_y == 1, yout[...], yin[...])


def differences(xpad, ypad, i, x, rows, coeffs, sign):
    centre = xpad[i, pl.ds(x + 4, rows)]
    parts = [None, None, None]
    for k in range(4):
        d = k + 1
        terms = (
            xpad[i, pl.ds(x + 4 + d, rows)] + sign * xpad[i, pl.ds(x + 4 - d, rows)],
            ypad[i, pl.ds(x, rows), 8 + d : 24 + d, :] + sign * ypad[i, pl.ds(x, rows), 8 - d : 24 - d, :],
            pltpu.roll(centre, NZ - d, 2) + sign * pltpu.roll(centre, d, 2),
        )
        for c in range(3):
            term = coeffs[k] * terms[c]
            parts[c] = term if parts[c] is None else parts[c] + term
    return centre, parts


ROWS = 4


def stencil_kernel(
    st_hbm, ve_hbm, yout, yin, xout, xin, g_hbm, b_hbm, h_hbm, first_parts, xpad, ypad, yin_scr, yout_scr, g, b, h, sems
):
    sources = [st_hbm.at[j] for j in range(2)] + [ve_hbm.at[c] for c in range(3)]
    fill(sources, (xin, xout, yin, yout), xpad, ypad, yin_scr, yout_scr, sems)
    sent = []
    for j in range(2):

        @pl.loop(0, 16, step=ROWS)
        def slope_rows(x):
            here = pl.ds(x, ROWS)
            slope = differences(xpad, ypad, j, x, ROWS, FIRST, -1.0)[1]
            total = None
            for c in range(3):
                g[j, c, here] = slope[c]
                term = xpad[2 + c, pl.ds(x + 4, ROWS)] * slope[c]
                total = term if total is None else total + term
            b[j, here] = -0.5 * total

        sent += start_all(((g.at[j], g_hbm.at[j]),), sems, len(sent))
    for p, part in enumerate(split(b[0].reshape(COLS, NZ))):
        first_parts[p] = part
    sent += start_all(((b.at[1], b_hbm),), sems, len(sent))

    @pl.loop(0, 16, step=ROWS)
    def curve_rows(x):
        for c in range(3):
            centre, parts = differences(xpad, ypad, 2 + c, x, ROWS, SECOND[1:], 1.0)
            total = 3.0 * SECOND[0] * centre + parts[0] + parts[1] + parts[2]
            h[c, pl.ds(x, ROWS)] = -BETA * total

    sent += start_all(((h, h_hbm),), sems, len(sent))
    wait_all(sent)


def supply_kernel(asked_hbm, parts, out_hbm, asked, out, sems):
    wait_all(start_all(((asked_hbm.at[:, W_ROWS, 0], asked),), sems))
    wanted = asked[...]
    place = iota((PART, COLS), 1).astype(F32)
    sent = []
    for i, first in enumerate(range(0, DEV, PART)):
        onehot = jnp.concatenate(
            [ones(wanted[first : first + PART, s : s + 1] == place) for s in range(CAP)], axis=0
        )
        put_slots(out, first * V_ROWS, select(onehot, [parts[p] for p in range(2)]), PART)
        here = pl.ds(first * V_ROWS, PART * V_ROWS)
        sent += start_all(((out.at[here], out_hbm.at[here]),), sems, i)
    wait_all(sent)


def gathered_rows(wanted_t, first):
    place = iota((COLS, DEV), 0).astype(F32)
    return jnp.concatenate(
        [ones(place == wanted_t[first + s : first + s + 1, :]) for s in range(CAP)], axis=1
    )


def normal_kernel(asked_hbm, own_hbm, w_hbm, b_hbm, d, taken, w0, b, placed_hbm, wt_hbm, asked, w, own, wt, placed, sems):
    copies = start_all(((own_hbm.at[0], own), (w_hbm.at[0], w0), (b_hbm, b)), sems)
    wait_all(start_all(((asked_hbm, asked),), sems, 3))
    wanted_t = asked[pl.ds(W_ROWS, DEV, stride=A_ROWS), :].T
    wt[...] = wanted_t[:16]
    sent = start_all(((wt, wt_hbm),), sems, 3)
    onehot_t = gathered_rows(wanted_t, 8)
    for k in range(4):
        for s in range(CAP):
            for half in range(2):
                w[k, s * DEV : (s + 1) * DEV, half * 128 : half * 128 + 128] = asked[
                    pl.ds(s * 8 + k * 2 + half, DEV, stride=A_ROWS), :
                ]
    for m in range(4):
        total = None
        for k in range(4 - m):
            product = w[k] * w[k + m]
            high = product.astype(BF16)
            low = (product - high.astype(F32)).astype(BF16)
            part = dot(onehot_t, high) + dot(onehot_t, low)
            if k != 1:
                part = pltpu.roll(part, (k - 1) % NZ, 1)
            total = part if total is None else total + part
        d[m] = total
    wait_all(copies)
    owner_row = own[...]
    for s, mask in enumerate(masks_by_column(owner_row)):
        taken[:, s * DEV : (s + 1) * DEV] = ones(mask)
    for s, mask in enumerate(masks_by_owner(owner_row, 0, DEV)):
        for i in range(DEV // PART):
            row = i * CAP * PART + s * PART
            placed[row : row + PART] = ones(mask[i * PART : (i + 1) * PART])
    wait_all(sent + start_all(((placed, placed_hbm),), sems, 4))


def read_slots(ref):
    return jnp.concatenate(
        [
            jnp.concatenate(
                [ref[pl.ds(s * 2 + half, DEV, stride=V_ROWS), :] for half in range(2)], axis=1
            )
            for s in range(CAP)
        ],
        axis=0,
    )


def middle_kernel(arr, d, taken, w, b, placed_hbm, lam_out, out_hbm, placed, out, parts, tile, sems):
    copies = start_all(((placed_hbm, placed),), sems)
    under_way(tile)
    received = split(read_slots(arr))
    rows = 128
    for start in range(0, COLS, rows):
        here = slice(start, start + rows)
        mine = select(taken[here], received)
        weights = [
            w[k, start // 16 : (start + rows) // 16].reshape(rows, NZ).astype(F32) for k in range(4)
        ]
        field = b[here]
        for k in range(4):
            field += weights[k] * (mine if k == 1 else pltpu.roll(mine, (1 - k) % NZ, 1))
        lam = d[0, here] * field
        for m in range(1, 4):
            lam += d[m, here] * pltpu.roll(field, NZ - m, 1) + pltpu.roll(d[m, here] * field, m, 1)
        lam_out[here] = lam
        spread = weights[1] * lam
        for k in (0, 2, 3):
            spread += pltpu.roll(weights[k] * lam, (k - 1) % NZ, 1)
        for i, part in enumerate(split(spread)):
            parts[i, here] = part
    wait_all(copies)
    sent = []
    for i, first in enumerate(range(0, DEV, PART)):
        onehot = placed[i * CAP * PART : (i + 1) * CAP * PART]
        put_slots(out, first * V_ROWS, select(onehot, [parts[p] for p in range(2)]), PART)
        here = pl.ds(first * V_ROWS, PART * V_ROWS)
        sent += start_all(((out.at[here], out_hbm.at[here]),), sems, i)
    wait_all(sent)


def blend_kernel(lam, wt_hbm, h_hbm, g_hbm, h, g, onehot, wt, g1, sems):
    copies = start_all(((wt_hbm, wt), (h_hbm, h), (g_hbm.at[0], g), (g_hbm.at[1], g1)), sems)
    copies[0].wait()
    onehot[...] = gathered_rows(wt[...], 0)
    wait_all(copies[1:])
    for c in range(3):
        h[c] = h[c] - 0.5 * (lam[...] * g1[c])


def final_kernel(arr, onehot, h, g, out_hbm, out, sems):
    lam = select(onehot[...], split(read_slots(arr)))
    sent = []
    for c in range(3):
        out[c] = h[c] - 0.5 * (lam * g[c])
        sent += start_all(((out.at[c], out_hbm.at[c]),), sems, c)
    wait_all(sent)


def exchange(value):
    return lax.all_to_all(value, AXES, split_axis=0, concat_axis=0, tiled=True)


def swapped(inner, outer, axis):
    count = lax.axis_size(axis)
    within = [(i, i ^ 1) for i in range(count)]
    across = [(i, (i + 1) % count if i % 2 else (i - 1) % count) for i in range(count)]
    far = lax.ppermute(outer, axis, across)
    return lax.ppermute(inner, axis, within), far


def per_device(state_path, velocity, weights, owners, sources):
    owner_row = owners.reshape(2, 1, COLS)
    source_row = sources.reshape(2, 1, COLS)
    hbm = pl.BlockSpec(memory_space=pltpu.HBM)
    near = pl.BlockSpec(memory_space=pltpu.VMEM)
    struct = lambda *shape: pltpu.HBM(shape, F32)
    scratch = lambda *shape: pltpu.VMEM(shape, F32)
    sems = lambda count: pltpu.SemaphoreType.DMA((count,))
    per_field = lambda count: struct(count, 16, 16, NZ)

    edge_x, edge_y = pltpu.VMEM((5, 4, 16, NZ), F32), pltpu.VMEM((5, 16, 4, NZ), F32)
    request, inner_x, outer_x, inner_y, outer_y = call(
        request_kernel,
        (struct(DEV * A_ROWS, 128), edge_x, edge_x, edge_y, edge_y),
        16,
        3,
        in_specs=[hbm] * 5,
        out_specs=(hbm,) + (near,) * 4,
        scratch_shapes=[
            pltpu.VMEM((2, 1, COLS), jnp.int32),
            pltpu.VMEM((2, 1, COLS), jnp.int32),
            pltpu.VMEM((4, 16, 16, NZ), BF16),
            scratch(DEV * A_ROWS, 128),
            scratch(2, 5, 16, 8, NZ),
            scratch(16, 128),
            sems(15),
        ],
    )(owner_row, source_row, weights, state_path, velocity)
    asked = exchange(request.reshape(DEV, A_ROWS, 1, 128))

    in_x, out_x = swapped(inner_x, outer_x, "gx")
    in_y, out_y = swapped(inner_y, outer_y, "gy")
    halos = out_y, in_y, out_x, in_x
    slopes, before, hess, before_parts = call(
        stencil_kernel,
        (struct(2, 3, 16, 16, NZ), struct(16, 16, NZ), per_field(3), pltpu.VMEM((2, COLS, NZ), BF16)),
        24,
        1000,
        in_specs=[hbm] * 6,
        out_specs=(hbm,) * 3 + (near,),
        scratch_shapes=[
            scratch(5, 24, 16, NZ),
            scratch(5, 16, 32, NZ),
            scratch(5, 16, 4, NZ),
            scratch(5, 16, 4, NZ),
            scratch(2, 3, 16, 16, NZ),
            scratch(2, 16, 16, NZ),
            scratch(3, 16, 16, NZ),
            sems(14),
        ],
    )(state_path, velocity, *halos)

    supply = call(
        supply_kernel,
        struct(DEV * V_ROWS, 128),
        8,
        2,
        in_specs=[hbm, near],
        out_specs=hbm,
        scratch_shapes=[scratch(DEV, 128), scratch(DEV * V_ROWS, 128), sems(4)],
    )(asked, before_parts)
    arrived = exchange(supply.reshape(DEV, CAP, 2, 128)).reshape(DEV * V_ROWS, 128)

    normal, taken, weight0, before1, placed, wanted_t = call(
        normal_kernel,
        (
            scratch(4, COLS, NZ),
            pltpu.VMEM((COLS, CAP * DEV), BF16),
            pltpu.VMEM((4, 16, 16, NZ), BF16),
            scratch(COLS, NZ),
            pltpu.HBM((CAP * DEV, COLS), BF16),
            struct(16, 128),
        ),
        20,
        4,
        in_specs=[hbm] * 4,
        out_specs=(near,) * 4 + (hbm,) * 2,
        scratch_shapes=[
            scratch(DEV * A_ROWS, 128),
            scratch(4, CAP * DEV, NZ),
            pltpu.VMEM((1, COLS), jnp.int32),
            scratch(16, 128),
            pltpu.VMEM((CAP * DEV, COLS), BF16),
            sems(5),
        ],
    )(asked.reshape(DEV * A_ROWS, 128), owner_row, weights, before.reshape(COLS, NZ))

    lam, push = call(
        middle_kernel,
        (scratch(COLS, NZ), struct(DEV * V_ROWS, 128)),
        8,
        4,
        in_specs=[near] * 5 + [hbm],
        out_specs=(near, hbm),
        scratch_shapes=[
            pltpu.VMEM((CAP * DEV, COLS), BF16),
            scratch(DEV * V_ROWS, 128),
            pltpu.VMEM((2, COLS, NZ), BF16),
            scratch(16, 128),
            sems(4),
        ],
    )(arrived, normal, taken, weight0, before1, placed)
    returned = exchange(push.reshape(DEV, CAP, 2, 128)).reshape(DEV * V_ROWS, 128)

    hess, slope0, onehot = call(
        blend_kernel,
        (scratch(3, COLS, NZ), scratch(3, COLS, NZ), pltpu.VMEM((COLS, CAP * DEV), BF16)),
        8,
        3,
        in_specs=[near] + [hbm] * 3,
        out_specs=(near,) * 3,
        scratch_shapes=[scratch(16, 128), scratch(3, COLS, NZ), sems(4)],
    )(lam, wanted_t, hess.reshape(3, COLS, NZ), slopes.reshape(2, 3, COLS, NZ))
    out = call(
        final_kernel,
        struct(3, COLS, NZ),
        8,
        2,
        in_specs=[near] * 4,
        out_specs=hbm,
        scratch_shapes=[scratch(3, COLS, NZ), sems(3)],
    )(returned, onehot, hess, slope0)
    return out.reshape(3, 16, 16, NZ)


def solution(mesh):
    return jax.shard_map(
        per_device,
        mesh=mesh,
        in_specs=(
            P(None, "gx", "gy", None),
            P(None, "gx", "gy", None),
            P(None, None, "gx", "gy", None),
            P(None, "gx", "gy", None, None),
            P(None, "gx", "gy", None),
        ),
        out_specs=P(None, "gx", "gy", None),
        check_vma=False,
    )
```

```python
import functools

import jax
import jax.numpy as jnp
from jax import lax
from jax.experimental import pallas as pl
from jax.experimental.pallas import tpu as pltpu
from jax.sharding import PartitionSpec as P

FIRST = (0.8, -0.2, 4.0 / 105.0, -1.0 / 280.0)
SECOND = (-205.0 / 72.0, 1.6, -0.2, 8.0 / 315.0, -1.0 / 560.0)
BETA = 0.05
AXES = ("gx", "gy")
CAP = 6
DEV = 128
COLS = 256
NZ = 256
F32 = jnp.float32
BF16 = jnp.bfloat16
W_ROWS = CAP * 8
A_ROWS = W_ROWS + 1
V_ROWS = CAP * 2
PART = 32


def call(kernel, out_shape, mib, micros, in_specs, **kw):
    run = pl.pallas_call(
        kernel,
        out_shape=out_shape,
        in_specs=in_specs,
        compiler_params=pltpu.CompilerParams(vmem_limit_bytes=mib * 1024 * 1024),
        cost_estimate=pl.CostEstimate(
            flops=int(micros * 1e8), bytes_accessed=int(micros * 2e6), transcendentals=0
        ),
        **kw,
    )

    def placed(*args):
        return run(
            *(
                pltpu.with_memory_space_constraint(x, pltpu.HBM) if spec.memory_space == pltpu.HBM else x
                for spec, x in zip(in_specs, args)
            )
        )

    return placed


def iota(shape, dim):
    return lax.broadcasted_iota(jnp.int32, shape, dim)


def dot(a, b):
    return jnp.dot(a, b, preferred_element_type=F32)


def split(x):
    hi = x.astype(BF16)
    return hi, (x - hi.astype(F32)).astype(BF16)


def select(onehot, parts):
    return sum(dot(onehot, part) for part in parts)


def ones(mask):
    return jnp.where(mask, 1.0, 0.0).astype(BF16)


def masks_by_owner(owner_row, first, count):
    match = iota((count, COLS), 0) + first == owner_row
    before = ones(iota((COLS, COLS), 0) < iota((COLS, COLS), 1))
    slot = dot(ones(match), before)
    return [match & (slot == float(s)) for s in range(CAP)]


def masks_by_column(owner_row):
    spread = jnp.broadcast_to(owner_row.astype(F32), (DEV, COLS)).T
    match = iota((COLS, DEV), 1).astype(F32) == spread
    before = ones(iota((COLS, COLS), 1) < iota((COLS, COLS), 0))
    slot = dot(before, ones(match))
    return [match & (slot == float(s)) for s in range(CAP)]


def put_slots(out_ref, start, values, count):
    for s in range(CAP):
        for half in range(2):
            out_ref[pl.ds(start + s * 2 + half, count, stride=V_ROWS), :] = values[
                s * count : (s + 1) * count, half * 128 : half * 128 + 128
            ]


def start_all(pairs, sems, first=0):
    copies = [
        pltpu.make_async_copy(source, target, sems.at[first + i])
        for i, (source, target) in enumerate(pairs)
    ]
    for copy in copies:
        copy.start()
    return copies


def under_way(tile):
    @pl.loop(0, 2)
    def touch(i):
        tile[pl.ds(i * 8, 8), :] = jnp.zeros((8, 128), F32)


def odd(axis):
    return lax.rem(lax.axis_index(axis), 2)


def wait_all(copies):
    for copy in copies:
        copy.wait()


def request_kernel(
    own_hbm, src_hbm, w_hbm, st_hbm, ve_hbm, out_hbm, xin, xout, ylo, yhi, own, src, w, out, edges, tile, sems
):
    pairs = [(own_hbm, own), (src_hbm, src), (w_hbm.at[1], w)]
    odd_x = odd("gx")
    for x_out, y_out, first, y_first in ((xin, 0, 12 - 12 * odd_x, 0), (xout, 1, 12 * odd_x, 8)):
        for source, place in ((st_hbm, pl.ds(0, 2)), (ve_hbm, pl.ds(2, 3))):
            pairs.append((source.at[:, pl.ds(first, 4)], x_out.at[place]))
            pairs.append((source.at[:, :, pl.ds(y_first, 8)], edges.at[y_out, place]))
    copies = start_all(pairs, sems)
    under_way(tile)
    wait_all(copies[:2])
    lane = iota((DEV, 128), 1)
    wanted = jnp.zeros((DEV, 128), F32)
    for j in range(2):
        masks = masks_by_owner(own[j], 0, DEV)
        source_row = src[j].astype(F32)
        for s in range(CAP):
            column = jnp.sum(jnp.where(masks[s], source_row, 0.0), axis=1, keepdims=True)
            wanted = jnp.where(lane == 8 * j + s, column, wanted)
    out[pl.ds(W_ROWS, DEV, stride=A_ROWS), :] = wanted
    copies[2].wait()
    sent = []
    for i, first in enumerate(range(0, DEV, PART)):
        onehot = jnp.concatenate([ones(m[first : first + PART]) for m in masks], axis=0)
        for k in range(4):
            placed = dot(onehot, w[k].reshape(COLS, NZ))
            for s in range(CAP):
                for half in range(2):
                    row = first * A_ROWS + s * 8 + k * 2 + half
                    out[pl.ds(row, PART, stride=A_ROWS), :] = placed[
                        s * PART : (s + 1) * PART, half * 128 : half * 128 + 128
                    ]
        block = pl.ds(first * A_ROWS, PART * A_ROWS)
        sent += start_all(((out.at[block], out_hbm.at[block]),), sems, 11 + i)
    wait_all(copies[3:])
    ylo[...] = edges[0, :, :, 0:4]
    yhi[...] = edges[1, :, :, 4:8]
    wait_all(sent)


def fill(sources, halos, xpad, ypad, ylo, yhi, sems, extra=()):
    odd_x = odd("gx")
    pairs = list(extra) + [(halos[2], ylo), (halos[3], yhi)]
    pairs += [(halos[0], xpad.at[:, pl.ds(20 - 20 * odd_x, 4)]), (halos[1], xpad.at[:, pl.ds(20 * odd_x, 4)])]
    for i, source in enumerate(sources):
        pairs += [(source, xpad.at[i, pl.ds(4, 16)]), (source, ypad.at[i, :, pl.ds(8, 16)])]
    wait_all(start_all(pairs, sems))
    ypad[:, :, 4:8] = ylo[...]
    ypad[:, :, 24:28] = yhi[...]


def differences(xpad, ypad, i, x, rows, coeffs, sign):
    centre = xpad[i, pl.ds(x + 4, rows)]
    parts = [None, None, None]
    for k in range(4):
        d = k + 1
        terms = (
            xpad[i, pl.ds(x + 4 + d, rows)] + sign * xpad[i, pl.ds(x + 4 - d, rows)],
            ypad[i, pl.ds(x, rows), 8 + d : 24 + d, :] + sign * ypad[i, pl.ds(x, rows), 8 - d : 24 - d, :],
            pltpu.roll(centre, NZ - d, 2) + sign * pltpu.roll(centre, d, 2),
        )
        for c in range(3):
            term = coeffs[k] * terms[c]
            parts[c] = term if parts[c] is None else parts[c] + term
    return centre, parts


ROWS = 4


def stencil_kernel(
    st_hbm, ve_hbm, xin, xout, ylo, yhi, g_hbm, b_hbm, h_hbm, first_parts, xpad, ypad, ylo_scr, yhi_scr, g, b, h, sems
):
    sources = [st_hbm.at[j] for j in range(2)] + [ve_hbm.at[c] for c in range(3)]
    fill(sources, (xin, xout, ylo, yhi), xpad, ypad, ylo_scr, yhi_scr, sems)
    sent = []
    for j in range(2):

        @pl.loop(0, 16, step=ROWS)
        def slope_rows(x):
            here = pl.ds(x, ROWS)
            slope = differences(xpad, ypad, j, x, ROWS, FIRST, -1.0)[1]
            total = None
            for c in range(3):
                g[j, c, here] = slope[c]
                term = xpad[2 + c, pl.ds(x + 4, ROWS)] * slope[c]
                total = term if total is None else total + term
            b[j, here] = -0.5 * total

        sent += start_all(((g.at[j], g_hbm.at[j]),), sems, len(sent))
    for p, part in enumerate(split(b[0].reshape(COLS, NZ))):
        first_parts[p] = part
    sent += start_all(((b.at[1], b_hbm),), sems, len(sent))

    @pl.loop(0, 16, step=ROWS)
    def curve_rows(x):
        for c in range(3):
            centre, parts = differences(xpad, ypad, 2 + c, x, ROWS, SECOND[1:], 1.0)
            total = 3.0 * SECOND[0] * centre + parts[0] + parts[1] + parts[2]
            h[c, pl.ds(x, ROWS)] = -BETA * total

    sent += start_all(((h, h_hbm),), sems, len(sent))
    wait_all(sent)


def supply_kernel(asked_hbm, parts, out_hbm, asked, out, sems):
    wait_all(start_all(((asked_hbm.at[:, W_ROWS, 0], asked),), sems))
    wanted = asked[...]
    place = iota((PART, COLS), 1).astype(F32)
    sent = []
    for i, first in enumerate(range(0, DEV, PART)):
        onehot = jnp.concatenate(
            [ones(wanted[first : first + PART, s : s + 1] == place) for s in range(CAP)], axis=0
        )
        put_slots(out, first * V_ROWS, select(onehot, [parts[p] for p in range(2)]), PART)
        here = pl.ds(first * V_ROWS, PART * V_ROWS)
        sent += start_all(((out.at[here], out_hbm.at[here]),), sems, i)
    wait_all(sent)


def gathered_rows(wanted_t, first):
    place = iota((COLS, DEV), 0).astype(F32)
    return jnp.concatenate(
        [ones(place == wanted_t[first + s : first + s + 1, :]) for s in range(CAP)], axis=1
    )


def normal_kernel(asked_hbm, own_hbm, w_hbm, b_hbm, d, taken, w0, b, placed_hbm, wt_hbm, asked, w, own, wt, placed, sems):
    copies = start_all(((own_hbm.at[0], own), (w_hbm.at[0], w0), (b_hbm, b)), sems)
    wait_all(start_all(((asked_hbm, asked),), sems, 3))
    wanted_t = asked[pl.ds(W_ROWS, DEV, stride=A_ROWS), :].T
    wt[...] = wanted_t[:16]
    sent = start_all(((wt, wt_hbm),), sems, 3)
    onehot_t = gathered_rows(wanted_t, 8)
    for k in range(4):
        for s in range(CAP):
            for half in range(2):
                w[k, s * DEV : (s + 1) * DEV, half * 128 : half * 128 + 128] = asked[
                    pl.ds(s * 8 + k * 2 + half, DEV, stride=A_ROWS), :
                ]
    for m in range(4):
        total = None
        for k in range(4 - m):
            product = w[k] * w[k + m]
            high = product.astype(BF16)
            low = (product - high.astype(F32)).astype(BF16)
            part = dot(onehot_t, high) + dot(onehot_t, low)
            if k != 1:
                part = pltpu.roll(part, (k - 1) % NZ, 1)
            total = part if total is None else total + part
        d[m] = total
    wait_all(copies)
    owner_row = own[...]
    for s, mask in enumerate(masks_by_column(owner_row)):
        taken[:, s * DEV : (s + 1) * DEV] = ones(mask)
    for s, mask in enumerate(masks_by_owner(owner_row, 0, DEV)):
        for i in range(DEV // PART):
            row = i * CAP * PART + s * PART
            placed[row : row + PART] = ones(mask[i * PART : (i + 1) * PART])
    wait_all(sent + start_all(((placed, placed_hbm),), sems, 4))


def read_slots(ref):
    return jnp.concatenate(
        [
            jnp.concatenate(
                [ref[pl.ds(s * 2 + half, DEV, stride=V_ROWS), :] for half in range(2)], axis=1
            )
            for s in range(CAP)
        ],
        axis=0,
    )


def middle_kernel(arr, d, taken, w, b, placed_hbm, lam_out, out_hbm, placed, out, parts, tile, sems):
    copies = start_all(((placed_hbm, placed),), sems)
    under_way(tile)
    mine_all = select(taken[...], split(read_slots(arr)))
    rows = 128
    for start in range(0, COLS, rows):
        here = slice(start, start + rows)
        mine = mine_all[here]
        weights = [
            w[k, start // 16 : (start + rows) // 16].reshape(rows, NZ).astype(F32) for k in range(4)
        ]
        field = b[here]
        for k in range(4):
            field += weights[k] * (mine if k == 1 else pltpu.roll(mine, (1 - k) % NZ, 1))
        lam = d[0, here] * field
        for m in range(1, 4):
            lam += d[m, here] * pltpu.roll(field, NZ - m, 1) + pltpu.roll(d[m, here] * field, m, 1)
        lam_out[here] = lam
        spread = weights[1] * lam
        for k in (0, 2, 3):
            spread += pltpu.roll(weights[k] * lam, (k - 1) % NZ, 1)
        for i, part in enumerate(split(spread)):
            parts[i, here] = part
    wait_all(copies)
    sent = []
    for i, first in enumerate(range(0, DEV, PART)):
        onehot = placed[i * CAP * PART : (i + 1) * CAP * PART]
        put_slots(out, first * V_ROWS, select(onehot, [parts[p] for p in range(2)]), PART)
        here = pl.ds(first * V_ROWS, PART * V_ROWS)
        sent += start_all(((out.at[here], out_hbm.at[here]),), sems, i)
    wait_all(sent)


def blend_kernel(lam, wt_hbm, h_hbm, g_hbm, h, g, onehot, wt, g1, sems):
    copies = start_all(((wt_hbm, wt), (h_hbm, h), (g_hbm.at[0], g), (g_hbm.at[1], g1)), sems)
    copies[0].wait()
    onehot[...] = gathered_rows(wt[...], 0)
    wait_all(copies[1:])
    for c in range(3):
        h[c] = h[c] - 0.5 * (lam[...] * g1[c])


def final_kernel(arr, onehot, h, g, out_hbm, out, sems):
    lam = select(onehot[...], split(read_slots(arr)))
    sent = []
    for c in range(3):
        out[c] = h[c] - 0.5 * (lam * g[c])
        sent += start_all(((out.at[c], out_hbm.at[c]),), sems, c)
    wait_all(sent)


def exchange(value):
    return lax.all_to_all(value, AXES, split_axis=0, concat_axis=0, tiled=True)


def swapped(inner, outer, axis):
    count = lax.axis_size(axis)
    within = [(i, i ^ 1) for i in range(count)]
    across = [(i, (i + 1) % count if i % 2 else (i - 1) % count) for i in range(count)]
    return lax.ppermute(inner, axis, within), lax.ppermute(outer, axis, across)


def neighbours(first, last, axis):
    count = lax.axis_size(axis)
    up = [(i, (i + 1) % count) for i in range(count)]
    down = [(j, i) for i, j in up]
    return lax.ppermute(last, axis, up), lax.ppermute(first, axis, down)


def per_device(state_path, velocity, weights, owners, sources):
    owner_row = owners.reshape(2, 1, COLS)
    source_row = sources.reshape(2, 1, COLS)
    hbm = pl.BlockSpec(memory_space=pltpu.HBM)
    near = pl.BlockSpec(memory_space=pltpu.VMEM)
    struct = lambda *shape: pltpu.HBM(shape, F32)
    scratch = lambda *shape: pltpu.VMEM(shape, F32)
    sems = lambda count: pltpu.SemaphoreType.DMA((count,))
    per_field = lambda count: struct(count, 16, 16, NZ)

    edge_x, edge_y = pltpu.VMEM((5, 4, 16, NZ), F32), pltpu.VMEM((5, 16, 4, NZ), F32)
    request, inner_x, outer_x, first_y, last_y = call(
        request_kernel,
        (struct(DEV * A_ROWS, 128), edge_x, edge_x, edge_y, edge_y),
        16,
        3,
        in_specs=[hbm] * 5,
        out_specs=(hbm,) + (near,) * 4,
        scratch_shapes=[
            pltpu.VMEM((2, 1, COLS), jnp.int32),
            pltpu.VMEM((2, 1, COLS), jnp.int32),
            pltpu.VMEM((4, 16, 16, NZ), BF16),
            scratch(DEV * A_ROWS, 128),
            scratch(2, 5, 16, 8, NZ),
            scratch(16, 128),
            sems(15),
        ],
    )(owner_row, source_row, weights, state_path, velocity)
    asked = exchange(request.reshape(DEV, A_ROWS, 1, 128))

    halos = swapped(inner_x, outer_x, "gx") + neighbours(first_y, last_y, "gy")
    slopes, before, hess, before_parts = call(
        stencil_kernel,
        (struct(2, 3, 16, 16, NZ), struct(16, 16, NZ), per_field(3), pltpu.VMEM((2, COLS, NZ), BF16)),
        24,
        1000,
        in_specs=[hbm] * 6,
        out_specs=(hbm,) * 3 + (near,),
        scratch_shapes=[
            scratch(5, 24, 16, NZ),
            scratch(5, 16, 32, NZ),
            scratch(5, 16, 4, NZ),
            scratch(5, 16, 4, NZ),
            scratch(2, 3, 16, 16, NZ),
            scratch(2, 16, 16, NZ),
            scratch(3, 16, 16, NZ),
            sems(14),
        ],
    )(state_path, velocity, *halos)

    supply = call(
        supply_kernel,
        struct(DEV * V_ROWS, 128),
        8,
        2,
        in_specs=[hbm, near],
        out_specs=hbm,
        scratch_shapes=[scratch(DEV, 128), scratch(DEV * V_ROWS, 128), sems(4)],
    )(asked, before_parts)
    arrived = exchange(supply.reshape(DEV, CAP, 2, 128)).reshape(DEV * V_ROWS, 128)

    normal, taken, weight0, before1, placed, wanted_t = call(
        normal_kernel,
        (
            scratch(4, COLS, NZ),
            pltpu.VMEM((COLS, CAP * DEV), BF16),
            pltpu.VMEM((4, 16, 16, NZ), BF16),
            scratch(COLS, NZ),
            pltpu.HBM((CAP * DEV, COLS), BF16),
            struct(16, 128),
        ),
        20,
        4,
        in_specs=[hbm] * 4,
        out_specs=(near,) * 4 + (hbm,) * 2,
        scratch_shapes=[
            scratch(DEV * A_ROWS, 128),
            scratch(4, CAP * DEV, NZ),
            pltpu.VMEM((1, COLS), jnp.int32),
            scratch(16, 128),
            pltpu.VMEM((CAP * DEV, COLS), BF16),
            sems(5),
        ],
    )(asked.reshape(DEV * A_ROWS, 128), owner_row, weights, before.reshape(COLS, NZ))

    lam, push = call(
        middle_kernel,
        (scratch(COLS, NZ), struct(DEV * V_ROWS, 128)),
        8,
        4,
        in_specs=[near] * 5 + [hbm],
        out_specs=(near, hbm),
        scratch_shapes=[
            pltpu.VMEM((CAP * DEV, COLS), BF16),
            scratch(DEV * V_ROWS, 128),
            pltpu.VMEM((2, COLS, NZ), BF16),
            scratch(16, 128),
            sems(4),
        ],
    )(arrived, normal, taken, weight0, before1, placed)
    returned = exchange(push.reshape(DEV, CAP, 2, 128)).reshape(DEV * V_ROWS, 128)

    hess, slope0, onehot = call(
        blend_kernel,
        (scratch(3, COLS, NZ), scratch(3, COLS, NZ), pltpu.VMEM((COLS, CAP * DEV), BF16)),
        8,
        3,
        in_specs=[near] + [hbm] * 3,
        out_specs=(near,) * 3,
        scratch_shapes=[scratch(16, 128), scratch(3, COLS, NZ), sems(4)],
    )(lam, wanted_t, hess.reshape(3, COLS, NZ), slopes.reshape(2, 3, COLS, NZ))
    out = call(
        final_kernel,
        struct(3, COLS, NZ),
        8,
        2,
        in_specs=[near] * 4,
        out_specs=hbm,
        scratch_shapes=[scratch(3, COLS, NZ), sems(3)],
    )(returned, onehot, hess, slope0)
    return out.reshape(3, 16, 16, NZ)


def solution(mesh):
    return jax.shard_map(
        per_device,
        mesh=mesh,
        in_specs=(
            P(None, "gx", "gy", None),
            P(None, "gx", "gy", None),
            P(None, None, "gx", "gy", None),
            P(None, "gx", "gy", None, None),
            P(None, "gx", "gy", None),
        ),
        out_specs=P(None, "gx", "gy", None),
        check_vma=False,
    )
```

```python
import functools

import jax
import jax.numpy as jnp
from jax import lax
from jax.experimental import pallas as pl
from jax.experimental.pallas import tpu as pltpu
from jax.sharding import PartitionSpec as P

FIRST = (0.8, -0.2, 4.0 / 105.0, -1.0 / 280.0)
SECOND = (-205.0 / 72.0, 1.6, -0.2, 8.0 / 315.0, -1.0 / 560.0)
BETA = 0.05
AXES = ("gx", "gy")
CAP = 6
DEV = 128
COLS = 256
NZ = 256
F32 = jnp.float32
BF16 = jnp.bfloat16
W_ROWS = CAP * 8
A_ROWS = W_ROWS + 1
V_ROWS = CAP * 2
PART = 32
FIRST_PART = 16


def call(kernel, out_shape, mib, micros, in_specs, **kw):
    run = pl.pallas_call(
        kernel,
        out_shape=out_shape,
        in_specs=in_specs,
        compiler_params=pltpu.CompilerParams(vmem_limit_bytes=mib * 1024 * 1024),
        cost_estimate=pl.CostEstimate(
            flops=int(micros * 1e8), bytes_accessed=int(micros * 2e6), transcendentals=0
        ),
        **kw,
    )

    def placed(*args):
        return run(
            *(
                pltpu.with_memory_space_constraint(x, pltpu.HBM) if spec.memory_space == pltpu.HBM else x
                for spec, x in zip(in_specs, args)
            )
        )

    return placed


def iota(shape, dim):
    return lax.broadcasted_iota(jnp.int32, shape, dim)


def dot(a, b):
    return jnp.dot(a, b, preferred_element_type=F32)


def split(x):
    hi = x.astype(BF16)
    return hi, (x - hi.astype(F32)).astype(BF16)


def select(onehot, parts):
    return sum(dot(onehot, part) for part in parts)


def ones(mask):
    return jnp.where(mask, 1.0, 0.0).astype(BF16)


def masks_by_owner(owner_row, first, count):
    match = iota((count, COLS), 0) + first == owner_row
    before = ones(iota((COLS, COLS), 0) < iota((COLS, COLS), 1))
    slot = dot(ones(match), before)
    return [match & (slot == float(s)) for s in range(CAP)]


def masks_by_column(owner_row):
    spread = jnp.broadcast_to(owner_row.astype(F32), (DEV, COLS)).T
    match = iota((COLS, DEV), 1).astype(F32) == spread
    before = ones(iota((COLS, COLS), 1) < iota((COLS, COLS), 0))
    slot = dot(before, ones(match))
    return [match & (slot == float(s)) for s in range(CAP)]


def put_slots(out_ref, start, values, count):
    for s in range(CAP):
        for half in range(2):
            out_ref[pl.ds(start + s * 2 + half, count, stride=V_ROWS), :] = values[
                s * count : (s + 1) * count, half * 128 : half * 128 + 128
            ]


def start_all(pairs, sems, first=0):
    copies = [
        pltpu.make_async_copy(source, target, sems.at[first + i])
        for i, (source, target) in enumerate(pairs)
    ]
    for copy in copies:
        copy.start()
    return copies


def under_way(tile):
    @pl.loop(0, 2)
    def touch(i):
        tile[pl.ds(i * 8, 8), :] = jnp.zeros((8, 128), F32)


def wait_all(copies):
    for copy in copies:
        copy.wait()


def request_kernel(
    own_hbm, src_hbm, w_hbm, st_hbm, ve_hbm, out_hbm, xlo, xhi, ylo, yhi, own, src, w, out, edges, sems
):
    pairs = [(own_hbm, own), (src_hbm, src), (w_hbm.at[1], w)]
    for x_out, y_out, first, y_first in ((xlo, 0, 0, 0), (xhi, 1, 12, 8)):
        for source, place in ((st_hbm, pl.ds(0, 2)), (ve_hbm, pl.ds(2, 3))):
            pairs.append((source.at[:, pl.ds(first, 4)], x_out.at[place]))
            pairs.append((source.at[:, :, pl.ds(y_first, 8)], edges.at[y_out, place]))
    copies = start_all(pairs, sems)
    wait_all(copies[:2])
    lane = iota((DEV, 128), 1)
    wanted = jnp.zeros((DEV, 128), F32)
    for j in range(2):
        masks = masks_by_owner(own[j], 0, DEV)
        source_row = src[j].astype(F32)
        for s in range(CAP):
            column = jnp.sum(jnp.where(masks[s], source_row, 0.0), axis=1, keepdims=True)
            wanted = jnp.where(lane == 8 * j + s, column, wanted)
    out[pl.ds(W_ROWS, DEV, stride=A_ROWS), :] = wanted
    copies[2].wait()
    sent = []
    for i, first in enumerate(range(0, DEV, FIRST_PART)):
        onehot = jnp.concatenate([ones(m[first : first + FIRST_PART]) for m in masks], axis=0)
        for k in range(4):
            placed = dot(onehot, w[k].reshape(COLS, NZ))
            for s in range(CAP):
                for half in range(2):
                    row = first * A_ROWS + s * 8 + k * 2 + half
                    out[pl.ds(row, FIRST_PART, stride=A_ROWS), :] = placed[
                        s * FIRST_PART : (s + 1) * FIRST_PART, half * 128 : half * 128 + 128
                    ]
        block = pl.ds(first * A_ROWS, FIRST_PART * A_ROWS)
        sent += start_all(((out.at[block], out_hbm.at[block]),), sems, 11 + i)
    wait_all(copies[3:])
    ylo[...] = edges[0, :, :, 0:4]
    yhi[...] = edges[1, :, :, 4:8]
    wait_all(sent)


def fill(sources, halos, xpad, ypad, ylo, yhi, sems, extra=()):
    pairs = list(extra) + [(halos[2], ylo), (halos[3], yhi)]
    pairs += [(halos[0], xpad.at[:, pl.ds(0, 4)]), (halos[1], xpad.at[:, pl.ds(20, 4)])]
    for i, source in enumerate(sources):
        pairs += [(source, xpad.at[i, pl.ds(4, 16)]), (source, ypad.at[i, :, pl.ds(8, 16)])]
    wait_all(start_all(pairs, sems))
    ypad[:, :, 4:8] = ylo[...]
    ypad[:, :, 24:28] = yhi[...]


def differences(xpad, ypad, i, x, rows, coeffs, sign):
    centre = xpad[i, pl.ds(x + 4, rows)]
    parts = [None, None, None]
    for k in range(4):
        d = k + 1
        terms = (
            xpad[i, pl.ds(x + 4 + d, rows)] + sign * xpad[i, pl.ds(x + 4 - d, rows)],
            ypad[i, pl.ds(x, rows), 8 + d : 24 + d, :] + sign * ypad[i, pl.ds(x, rows), 8 - d : 24 - d, :],
            pltpu.roll(centre, NZ - d, 2) + sign * pltpu.roll(centre, d, 2),
        )
        for c in range(3):
            term = coeffs[k] * terms[c]
            parts[c] = term if parts[c] is None else parts[c] + term
    return centre, parts


ROWS = 4


def stencil_kernel(
    st_hbm, ve_hbm, xlo, xhi, ylo, yhi, g_hbm, b_hbm, h_hbm, first_parts, xpad, ypad, ylo_scr, yhi_scr, g, b, h, sems
):
    sources = [st_hbm.at[j] for j in range(2)] + [ve_hbm.at[c] for c in range(3)]
    fill(sources, (xlo, xhi, ylo, yhi), xpad, ypad, ylo_scr, yhi_scr, sems)
    sent = []
    for j in range(2):

        @pl.loop(0, 16, step=ROWS)
        def slope_rows(x):
            here = pl.ds(x, ROWS)
            slope = differences(xpad, ypad, j, x, ROWS, FIRST, -1.0)[1]
            total = None
            for c in range(3):
                g[j, c, here] = slope[c]
                term = xpad[2 + c, pl.ds(x + 4, ROWS)] * slope[c]
                total = term if total is None else total + term
            b[j, here] = -0.5 * total

        sent += start_all(((g.at[j], g_hbm.at[j]),), sems, len(sent))
    for p, part in enumerate(split(b[0].reshape(COLS, NZ))):
        first_parts[p] = part
    sent += start_all(((b.at[1], b_hbm),), sems, len(sent))

    @pl.loop(0, 16, step=ROWS)
    def curve_rows(x):
        for c in range(3):
            centre, parts = differences(xpad, ypad, 2 + c, x, ROWS, SECOND[1:], 1.0)
            total = 3.0 * SECOND[0] * centre + parts[0] + parts[1] + parts[2]
            h[c, pl.ds(x, ROWS)] = -BETA * total

    sent += start_all(((h, h_hbm),), sems, len(sent))
    wait_all(sent)


def supply_kernel(asked_hbm, parts, out_hbm, asked, out, sems):
    wait_all(start_all(((asked_hbm.at[:, W_ROWS, 0], asked),), sems))
    wanted = asked[...]
    place = iota((PART, COLS), 1).astype(F32)
    sent = []
    for i, first in enumerate(range(0, DEV, PART)):
        onehot = jnp.concatenate(
            [ones(wanted[first : first + PART, s : s + 1] == place) for s in range(CAP)], axis=0
        )
        put_slots(out, first * V_ROWS, select(onehot, [parts[p] for p in range(2)]), PART)
        here = pl.ds(first * V_ROWS, PART * V_ROWS)
        sent += start_all(((out.at[here], out_hbm.at[here]),), sems, i)
    wait_all(sent)


def gathered_rows(wanted_t, first):
    place = iota((COLS, DEV), 0).astype(F32)
    return jnp.concatenate(
        [ones(place == wanted_t[first + s : first + s + 1, :]) for s in range(CAP)], axis=1
    )


def normal_kernel(asked_hbm, own_hbm, w_hbm, b_hbm, d, taken, w0, b, placed_hbm, wt_hbm, asked, w, own, wt, placed, sems):
    copies = start_all(((own_hbm.at[0], own), (w_hbm.at[0], w0), (b_hbm, b)), sems)
    wait_all(start_all(((asked_hbm, asked),), sems, 3))
    wanted_t = asked[pl.ds(W_ROWS, DEV, stride=A_ROWS), :].T
    wt[...] = wanted_t[:16]
    sent = start_all(((wt, wt_hbm),), sems, 3)
    onehot_t = gathered_rows(wanted_t, 8)
    for k in range(4):
        for s in range(CAP):
            for half in range(2):
                w[k, s * DEV : (s + 1) * DEV, half * 128 : half * 128 + 128] = asked[
                    pl.ds(s * 8 + k * 2 + half, DEV, stride=A_ROWS), :
                ]
    for m in range(4):
        total = None
        for k in range(4 - m):
            product = w[k] * w[k + m]
            high = product.astype(BF16)
            low = (product - high.astype(F32)).astype(BF16)
            part = dot(onehot_t, high) + dot(onehot_t, low)
            if k != 1:
                part = pltpu.roll(part, (k - 1) % NZ, 1)
            total = part if total is None else total + part
        d[m] = total
    wait_all(copies)
    owner_row = own[...]
    for s, mask in enumerate(masks_by_column(owner_row)):
        taken[:, s * DEV : (s + 1) * DEV] = ones(mask)
    for s, mask in enumerate(masks_by_owner(owner_row, 0, DEV)):
        for i in range(DEV // PART):
            row = i * CAP * PART + s * PART
            placed[row : row + PART] = ones(mask[i * PART : (i + 1) * PART])
    wait_all(sent + start_all(((placed, placed_hbm),), sems, 4))


def read_slots(ref):
    return jnp.concatenate(
        [
            jnp.concatenate(
                [ref[pl.ds(s * 2 + half, DEV, stride=V_ROWS), :] for half in range(2)], axis=1
            )
            for s in range(CAP)
        ],
        axis=0,
    )


def middle_kernel(arr, d, taken, w, b, placed_hbm, lam_out, out_hbm, placed, out, parts, tile, sems):
    copies = start_all(((placed_hbm, placed),), sems)
    under_way(tile)
    received = split(read_slots(arr))
    rows = 128
    for start in range(0, COLS, rows):
        here = slice(start, start + rows)
        mine = select(taken[here], received)
        weights = [
            w[k, start // 16 : (start + rows) // 16].reshape(rows, NZ).astype(F32) for k in range(4)
        ]
        field = b[here]
        for k in range(4):
            field += weights[k] * (mine if k == 1 else pltpu.roll(mine, (1 - k) % NZ, 1))
        lam = d[0, here] * field
        for m in range(1, 4):
            lam += d[m, here] * pltpu.roll(field, NZ - m, 1) + pltpu.roll(d[m, here] * field, m, 1)
        lam_out[here] = lam
        spread = weights[1] * lam
        for k in (0, 2, 3):
            spread += pltpu.roll(weights[k] * lam, (k - 1) % NZ, 1)
        for i, part in enumerate(split(spread)):
            parts[i, here] = part
    wait_all(copies)
    sent = []
    for i, first in enumerate(range(0, DEV, PART)):
        onehot = placed[i * CAP * PART : (i + 1) * CAP * PART]
        put_slots(out, first * V_ROWS, select(onehot, [parts[p] for p in range(2)]), PART)
        here = pl.ds(first * V_ROWS, PART * V_ROWS)
        sent += start_all(((out.at[here], out_hbm.at[here]),), sems, i)
    wait_all(sent)


def blend_kernel(lam, wt_hbm, h_hbm, g_hbm, h, g, onehot, wt, g1, sems):
    copies = start_all(((wt_hbm, wt), (h_hbm, h), (g_hbm.at[0], g), (g_hbm.at[1], g1)), sems)
    copies[0].wait()
    onehot[...] = gathered_rows(wt[...], 0)
    wait_all(copies[1:])
    for c in range(3):
        h[c] = h[c] - 0.5 * (lam[...] * g1[c])
        g[c] = 0.5 * g[c]


def final_kernel(arr, onehot, h, g, out_hbm, out, sems):
    lam = select(onehot[...], split(read_slots(arr)))
    sent = []
    for c in range(3):
        out[c] = h[c] - lam * g[c]
        sent += start_all(((out.at[c], out_hbm.at[c]),), sems, c)
    wait_all(sent)


def exchange(value):
    return lax.all_to_all(value, AXES, split_axis=0, concat_axis=0, tiled=True)


def neighbours(first, last, axis):
    count = lax.axis_size(axis)
    up = [(i, (i + 1) % count) for i in range(count)]
    down = [(j, i) for i, j in up]
    return lax.ppermute(last, axis, up), lax.ppermute(first, axis, down)


def per_device(state_path, velocity, weights, owners, sources):
    owner_row = owners.reshape(2, 1, COLS)
    source_row = sources.reshape(2, 1, COLS)
    hbm = pl.BlockSpec(memory_space=pltpu.HBM)
    near = pl.BlockSpec(memory_space=pltpu.VMEM)
    struct = lambda *shape: pltpu.HBM(shape, F32)
    scratch = lambda *shape: pltpu.VMEM(shape, F32)
    sems = lambda count: pltpu.SemaphoreType.DMA((count,))
    per_field = lambda count: struct(count, 16, 16, NZ)

    edge_x, edge_y = pltpu.VMEM((5, 4, 16, NZ), F32), pltpu.VMEM((5, 16, 4, NZ), F32)
    request, first_x, last_x, first_y, last_y = call(
        request_kernel,
        (struct(DEV * A_ROWS, 128), edge_x, edge_x, edge_y, edge_y),
        16,
        3,
        in_specs=[hbm] * 5,
        out_specs=(hbm,) + (near,) * 4,
        scratch_shapes=[
            pltpu.VMEM((2, 1, COLS), jnp.int32),
            pltpu.VMEM((2, 1, COLS), jnp.int32),
            pltpu.VMEM((4, 16, 16, NZ), BF16),
            scratch(DEV * A_ROWS, 128),
            scratch(2, 5, 16, 8, NZ),
            sems(19),
        ],
    )(owner_row, source_row, weights, state_path, velocity)
    asked = exchange(request.reshape(DEV, A_ROWS, 1, 128))

    halos = neighbours(first_x, last_x, "gx") + neighbours(first_y, last_y, "gy")
    slopes, before, hess, before_parts = call(
        stencil_kernel,
        (struct(2, 3, 16, 16, NZ), struct(16, 16, NZ), per_field(3), pltpu.VMEM((2, COLS, NZ), BF16)),
        24,
        1000,
        in_specs=[hbm] * 6,
        out_specs=(hbm,) * 3 + (near,),
        scratch_shapes=[
            scratch(5, 24, 16, NZ),
            scratch(5, 16, 32, NZ),
            scratch(5, 16, 4, NZ),
            scratch(5, 16, 4, NZ),
            scratch(2, 3, 16, 16, NZ),
            scratch(2, 16, 16, NZ),
            scratch(3, 16, 16, NZ),
            sems(14),
        ],
    )(state_path, velocity, *halos)

    supply = call(
        supply_kernel,
        struct(DEV * V_ROWS, 128),
        8,
        2,
        in_specs=[hbm, near],
        out_specs=hbm,
        scratch_shapes=[scratch(DEV, 128), scratch(DEV * V_ROWS, 128), sems(4)],
    )(asked, before_parts)
    arrived = exchange(supply.reshape(DEV, CAP, 2, 128)).reshape(DEV * V_ROWS, 128)

    normal, taken, weight0, before1, placed, wanted_t = call(
        normal_kernel,
        (
            scratch(4, COLS, NZ),
            pltpu.VMEM((COLS, CAP * DEV), BF16),
            pltpu.VMEM((4, 16, 16, NZ), BF16),
            scratch(COLS, NZ),
            pltpu.HBM((CAP * DEV, COLS), BF16),
            struct(16, 128),
        ),
        20,
        4,
        in_specs=[hbm] * 4,
        out_specs=(near,) * 4 + (hbm,) * 2,
        scratch_shapes=[
            scratch(DEV * A_ROWS, 128),
            scratch(4, CAP * DEV, NZ),
            pltpu.VMEM((1, COLS), jnp.int32),
            scratch(16, 128),
            pltpu.VMEM((CAP * DEV, COLS), BF16),
            sems(5),
        ],
    )(asked.reshape(DEV * A_ROWS, 128), owner_row, weights, before.reshape(COLS, NZ))

    lam, push = call(
        middle_kernel,
        (scratch(COLS, NZ), struct(DEV * V_ROWS, 128)),
        8,
        4,
        in_specs=[near] * 5 + [hbm],
        out_specs=(near, hbm),
        scratch_shapes=[
            pltpu.VMEM((CAP * DEV, COLS), BF16),
            scratch(DEV * V_ROWS, 128),
            pltpu.VMEM((2, COLS, NZ), BF16),
            scratch(16, 128),
            sems(4),
        ],
    )(arrived, normal, taken, weight0, before1, placed)
    returned = exchange(push.reshape(DEV, CAP, 2, 128)).reshape(DEV * V_ROWS, 128)

    hess, slope0, onehot = call(
        blend_kernel,
        (scratch(3, COLS, NZ), scratch(3, COLS, NZ), pltpu.VMEM((COLS, CAP * DEV), BF16)),
        8,
        3,
        in_specs=[near] + [hbm] * 3,
        out_specs=(near,) * 3,
        scratch_shapes=[scratch(16, 128), scratch(3, COLS, NZ), sems(4)],
    )(lam, wanted_t, hess.reshape(3, COLS, NZ), slopes.reshape(2, 3, COLS, NZ))
    out = call(
        final_kernel,
        struct(3, COLS, NZ),
        8,
        2,
        in_specs=[near] * 4,
        out_specs=hbm,
        scratch_shapes=[scratch(3, COLS, NZ), sems(3)],
    )(returned, onehot, hess, slope0)
    return out.reshape(3, 16, 16, NZ)


def solution(mesh):
    return jax.shard_map(
        per_device,
        mesh=mesh,
        in_specs=(
            P(None, "gx", "gy", None),
            P(None, "gx", "gy", None),
            P(None, None, "gx", "gy", None),
            P(None, "gx", "gy", None, None),
            P(None, "gx", "gy", None),
        ),
        out_specs=P(None, "gx", "gy", None),
        check_vma=False,
    )
```

```python
import functools

import jax
import jax.numpy as jnp
from jax import lax
from jax.experimental import pallas as pl
from jax.experimental.pallas import tpu as pltpu
from jax.sharding import PartitionSpec as P

FIRST = (0.8, -0.2, 4.0 / 105.0, -1.0 / 280.0)
SECOND = (-205.0 / 72.0, 1.6, -0.2, 8.0 / 315.0, -1.0 / 560.0)
BETA = 0.05
AXES = ("gx", "gy")
CAP = 6
DEV = 128
COLS = 256
NZ = 256
F32 = jnp.float32
BF16 = jnp.bfloat16
W_ROWS = CAP * 8
A_ROWS = W_ROWS + 1
V_ROWS = CAP * 2
PART = 32
FIRST_PART = 16


def call(kernel, out_shape, mib, micros, in_specs, **kw):
    run = pl.pallas_call(
        kernel,
        out_shape=out_shape,
        in_specs=in_specs,
        compiler_params=pltpu.CompilerParams(vmem_limit_bytes=mib * 1024 * 1024),
        cost_estimate=pl.CostEstimate(
            flops=int(micros * 1e8), bytes_accessed=int(micros * 2e6), transcendentals=0
        ),
        **kw,
    )

    def placed(*args):
        return run(
            *(
                pltpu.with_memory_space_constraint(x, pltpu.HBM) if spec.memory_space == pltpu.HBM else x
                for spec, x in zip(in_specs, args)
            )
        )

    return placed


def iota(shape, dim):
    return lax.broadcasted_iota(jnp.int32, shape, dim)


def dot(a, b):
    return jnp.dot(a, b, preferred_element_type=F32)


def split(x):
    hi = x.astype(BF16)
    return hi, (x - hi.astype(F32)).astype(BF16)


def select(onehot, parts):
    return sum(dot(onehot, part) for part in parts)


def ones(mask):
    return jnp.where(mask, 1.0, 0.0).astype(BF16)


def masks_by_owner(owner_row, first, count):
    match = iota((count, COLS), 0) + first == owner_row
    before = ones(iota((COLS, COLS), 0) < iota((COLS, COLS), 1))
    slot = dot(ones(match), before)
    return [match & (slot == float(s)) for s in range(CAP)]


def masks_by_column(owner_row):
    spread = jnp.broadcast_to(owner_row.astype(F32), (DEV, COLS)).T
    match = iota((COLS, DEV), 1).astype(F32) == spread
    before = ones(iota((COLS, COLS), 1) < iota((COLS, COLS), 0))
    slot = dot(before, ones(match))
    return [match & (slot == float(s)) for s in range(CAP)]


def put_slots(out_ref, start, values, count):
    for s in range(CAP):
        for half in range(2):
            out_ref[pl.ds(start + s * 2 + half, count, stride=V_ROWS), :] = values[
                s * count : (s + 1) * count, half * 128 : half * 128 + 128
            ]


def start_all(pairs, sems, first=0):
    copies = [
        pltpu.make_async_copy(source, target, sems.at[first + i])
        for i, (source, target) in enumerate(pairs)
    ]
    for copy in copies:
        copy.start()
    return copies


def under_way(tile):
    @pl.loop(0, 2)
    def touch(i):
        tile[pl.ds(i * 8, 8), :] = jnp.zeros((8, 128), F32)


def wait_all(copies):
    for copy in copies:
        copy.wait()


def request_kernel(
    own_hbm, src_hbm, w_hbm, st_hbm, ve_hbm, out_hbm, xlo, xhi, ylo, yhi, own, src, w, out, edges, sems
):
    pairs = [(own_hbm, own), (src_hbm, src), (w_hbm.at[1], w)]
    for x_out, y_out, first, y_first in ((xlo, 0, 0, 0), (xhi, 1, 12, 8)):
        for source, place in ((st_hbm, pl.ds(0, 2)), (ve_hbm, pl.ds(2, 3))):
            pairs.append((source.at[:, pl.ds(first, 4)], x_out.at[place]))
            pairs.append((source.at[:, :, pl.ds(y_first, 8)], edges.at[y_out, place]))
    copies = start_all(pairs, sems)
    wait_all(copies[:2])
    lane = iota((DEV, 128), 1)
    wanted = jnp.zeros((DEV, 128), F32)
    for j in range(2):
        masks = masks_by_owner(own[j], 0, DEV)
        source_row = src[j].astype(F32)
        for s in range(CAP):
            column = jnp.sum(jnp.where(masks[s], source_row, 0.0), axis=1, keepdims=True)
            wanted = jnp.where(lane == 8 * j + s, column, wanted)
    out[pl.ds(W_ROWS, DEV, stride=A_ROWS), :] = wanted
    copies[2].wait()
    sent = []
    for i, first in enumerate(range(0, DEV, FIRST_PART)):
        onehot = jnp.concatenate([ones(m[first : first + FIRST_PART]) for m in masks], axis=0)
        for k in range(4):
            placed = dot(onehot, w[k].reshape(COLS, NZ))
            for s in range(CAP):
                for half in range(2):
                    row = first * A_ROWS + s * 8 + k * 2 + half
                    out[pl.ds(row, FIRST_PART, stride=A_ROWS), :] = placed[
                        s * FIRST_PART : (s + 1) * FIRST_PART, half * 128 : half * 128 + 128
                    ]
        block = pl.ds(first * A_ROWS, FIRST_PART * A_ROWS)
        sent += start_all(((out.at[block], out_hbm.at[block]),), sems, 11 + i)
    wait_all(copies[3:])
    ylo[...] = edges[0, :, :, 0:4]
    yhi[...] = edges[1, :, :, 4:8]
    wait_all(sent)


def fill(sources, halos, xpad, ypad, ylo, yhi, sems, extra=()):
    pairs = list(extra) + [(halos[2], ylo), (halos[3], yhi)]
    pairs += [(halos[0], xpad.at[:, pl.ds(0, 4)]), (halos[1], xpad.at[:, pl.ds(20, 4)])]
    for i, source in enumerate(sources):
        pairs += [(source, xpad.at[i, pl.ds(4, 16)]), (source, ypad.at[i, :, pl.ds(8, 16)])]
    wait_all(start_all(pairs, sems))
    ypad[:, :, 4:8] = ylo[...]
    ypad[:, :, 24:28] = yhi[...]


def differences(xpad, ypad, i, x, rows, coeffs, sign):
    centre = xpad[i, pl.ds(x + 4, rows)]
    parts = [None, None, None]
    for k in range(4):
        d = k + 1
        terms = (
            xpad[i, pl.ds(x + 4 + d, rows)] + sign * xpad[i, pl.ds(x + 4 - d, rows)],
            ypad[i, pl.ds(x, rows), 8 + d : 24 + d, :] + sign * ypad[i, pl.ds(x, rows), 8 - d : 24 - d, :],
            pltpu.roll(centre, NZ - d, 2) + sign * pltpu.roll(centre, d, 2),
        )
        for c in range(3):
            term = coeffs[k] * terms[c]
            parts[c] = term if parts[c] is None else parts[c] + term
    return centre, parts


ROWS = 4


def stencil_kernel(
    st_hbm, ve_hbm, ylo, yhi, xlo, xhi, g_hbm, b_hbm, h_hbm, first_parts, xpad, ypad, ylo_scr, yhi_scr, g, b, h, sems
):
    sources = [st_hbm.at[j] for j in range(2)] + [ve_hbm.at[c] for c in range(3)]
    fill(sources, (xlo, xhi, ylo, yhi), xpad, ypad, ylo_scr, yhi_scr, sems)
    sent = []
    for j in range(2):

        @pl.loop(0, 16, step=ROWS)
        def slope_rows(x):
            here = pl.ds(x, ROWS)
            slope = differences(xpad, ypad, j, x, ROWS, FIRST, -1.0)[1]
            total = None
            for c in range(3):
                g[j, c, here] = slope[c]
                term = xpad[2 + c, pl.ds(x + 4, ROWS)] * slope[c]
                total = term if total is None else total + term
            b[j, here] = -0.5 * total

        sent += start_all(((g.at[j], g_hbm.at[j]),), sems, len(sent))
    for p, part in enumerate(split(b[0].reshape(COLS, NZ))):
        first_parts[p] = part
    sent += start_all(((b.at[1], b_hbm),), sems, len(sent))

    @pl.loop(0, 16, step=ROWS)
    def curve_rows(x):
        for c in range(3):
            centre, parts = differences(xpad, ypad, 2 + c, x, ROWS, SECOND[1:], 1.0)
            total = 3.0 * SECOND[0] * centre + parts[0] + parts[1] + parts[2]
            h[c, pl.ds(x, ROWS)] = -BETA * total

    sent += start_all(((h, h_hbm),), sems, len(sent))
    wait_all(sent)


def supply_kernel(asked_hbm, parts, out_hbm, asked, out, sems):
    wait_all(start_all(((asked_hbm.at[:, W_ROWS, 0], asked),), sems))
    wanted = asked[...]
    place = iota((PART, COLS), 1).astype(F32)
    sent = []
    for i, first in enumerate(range(0, DEV, PART)):
        onehot = jnp.concatenate(
            [ones(wanted[first : first + PART, s : s + 1] == place) for s in range(CAP)], axis=0
        )
        put_slots(out, first * V_ROWS, select(onehot, [parts[p] for p in range(2)]), PART)
        here = pl.ds(first * V_ROWS, PART * V_ROWS)
        sent += start_all(((out.at[here], out_hbm.at[here]),), sems, i)
    wait_all(sent)


def gathered_rows(wanted_t, first):
    place = iota((COLS, DEV), 0).astype(F32)
    return jnp.concatenate(
        [ones(place == wanted_t[first + s : first + s + 1, :]) for s in range(CAP)], axis=1
    )


def normal_kernel(asked_hbm, own_hbm, w_hbm, b_hbm, d, taken, w0, b, placed_hbm, wt_hbm, asked, w, own, wt, placed, sems):
    copies = start_all(((own_hbm.at[0], own), (w_hbm.at[0], w0), (b_hbm, b)), sems)
    wait_all(start_all(((asked_hbm, asked),), sems, 3))
    wanted_t = asked[pl.ds(W_ROWS, DEV, stride=A_ROWS), :].T
    wt[...] = wanted_t[:16]
    sent = start_all(((wt, wt_hbm),), sems, 3)
    onehot_t = gathered_rows(wanted_t, 8)
    for k in range(4):
        for s in range(CAP):
            for half in range(2):
                w[k, s * DEV : (s + 1) * DEV, half * 128 : half * 128 + 128] = asked[
                    pl.ds(s * 8 + k * 2 + half, DEV, stride=A_ROWS), :
                ]
    for m in range(4):
        total = None
        for k in range(4 - m):
            product = w[k] * w[k + m]
            high = product.astype(BF16)
            low = (product - high.astype(F32)).astype(BF16)
            part = dot(onehot_t, high) + dot(onehot_t, low)
            if k != 1:
                part = pltpu.roll(part, (k - 1) % NZ, 1)
            total = part if total is None else total + part
        d[m] = total
    wait_all(copies)
    owner_row = own[...]
    for s, mask in enumerate(masks_by_column(owner_row)):
        taken[:, s * DEV : (s + 1) * DEV] = ones(mask)
    for s, mask in enumerate(masks_by_owner(owner_row, 0, DEV)):
        for i in range(DEV // PART):
            row = i * CAP * PART + s * PART
            placed[row : row + PART] = ones(mask[i * PART : (i + 1) * PART])
    wait_all(sent + start_all(((placed, placed_hbm),), sems, 4))


def read_slots(ref):
    return jnp.concatenate(
        [
            jnp.concatenate(
                [ref[pl.ds(s * 2 + half, DEV, stride=V_ROWS), :] for half in range(2)], axis=1
            )
            for s in range(CAP)
        ],
        axis=0,
    )


def middle_kernel(arr, d, taken, w, b, placed_hbm, lam_out, out_hbm, placed, out, parts, tile, sems):
    copies = start_all(((placed_hbm, placed),), sems)
    under_way(tile)
    received = split(read_slots(arr))
    rows = 128
    for start in range(0, COLS, rows):
        here = slice(start, start + rows)
        mine = select(taken[here], received)
        weights = [
            w[k, start // 16 : (start + rows) // 16].reshape(rows, NZ).astype(F32) for k in range(4)
        ]
        field = b[here]
        for k in range(4):
            field += weights[k] * (mine if k == 1 else pltpu.roll(mine, (1 - k) % NZ, 1))
        lam = d[0, here] * field
        for m in range(1, 4):
            lam += d[m, here] * pltpu.roll(field, NZ - m, 1) + pltpu.roll(d[m, here] * field, m, 1)
        lam_out[here] = lam
        spread = weights[1] * lam
        for k in (0, 2, 3):
            spread += pltpu.roll(weights[k] * lam, (k - 1) % NZ, 1)
        for i, part in enumerate(split(spread)):
            parts[i, here] = part
    wait_all(copies)
    sent = []
    for i, first in enumerate(range(0, DEV, PART)):
        onehot = placed[i * CAP * PART : (i + 1) * CAP * PART]
        put_slots(out, first * V_ROWS, select(onehot, [parts[p] for p in range(2)]), PART)
        here = pl.ds(first * V_ROWS, PART * V_ROWS)
        sent += start_all(((out.at[here], out_hbm.at[here]),), sems, i)
    wait_all(sent)


def blend_kernel(lam, wt_hbm, h_hbm, g_hbm, h, g, onehot, wt, g1, sems):
    copies = start_all(((wt_hbm, wt), (h_hbm, h), (g_hbm.at[0], g), (g_hbm.at[1], g1)), sems)
    copies[0].wait()
    onehot[...] = gathered_rows(wt[...], 0)
    wait_all(copies[1:])
    for c in range(3):
        h[c] = h[c] - 0.5 * (lam[...] * g1[c])
        g[c] = 0.5 * g[c]


def final_kernel(arr, onehot, h, g, out_hbm, out, sems):
    lam = select(onehot[...], split(read_slots(arr)))
    sent = []
    for c in range(3):
        out[c] = h[c] - lam * g[c]
        sent += start_all(((out.at[c], out_hbm.at[c]),), sems, c)
    wait_all(sent)


def exchange(value):
    return lax.all_to_all(value, AXES, split_axis=0, concat_axis=0, tiled=True)


def neighbours(first, last, axis):
    count = lax.axis_size(axis)
    up = [(i, (i + 1) % count) for i in range(count)]
    down = [(j, i) for i, j in up]
    return lax.ppermute(last, axis, up), lax.ppermute(first, axis, down)


def per_device(state_path, velocity, weights, owners, sources):
    owner_row = owners.reshape(2, 1, COLS)
    source_row = sources.reshape(2, 1, COLS)
    hbm = pl.BlockSpec(memory_space=pltpu.HBM)
    near = pl.BlockSpec(memory_space=pltpu.VMEM)
    struct = lambda *shape: pltpu.HBM(shape, F32)
    scratch = lambda *shape: pltpu.VMEM(shape, F32)
    sems = lambda count: pltpu.SemaphoreType.DMA((count,))
    per_field = lambda count: struct(count, 16, 16, NZ)

    edge_x, edge_y = pltpu.VMEM((5, 4, 16, NZ), F32), pltpu.VMEM((5, 16, 4, NZ), F32)
    request, first_x, last_x, first_y, last_y = call(
        request_kernel,
        (struct(DEV * A_ROWS, 128), edge_x, edge_x, edge_y, edge_y),
        16,
        3,
        in_specs=[hbm] * 5,
        out_specs=(hbm,) + (near,) * 4,
        scratch_shapes=[
            pltpu.VMEM((2, 1, COLS), jnp.int32),
            pltpu.VMEM((2, 1, COLS), jnp.int32),
            pltpu.VMEM((4, 16, 16, NZ), BF16),
            scratch(DEV * A_ROWS, 128),
            scratch(2, 5, 16, 8, NZ),
            sems(19),
        ],
    )(owner_row, source_row, weights, state_path, velocity)
    asked = exchange(request.reshape(DEV, A_ROWS, 1, 128))

    halos = neighbours(first_y, last_y, "gy") + neighbours(first_x, last_x, "gx")
    slopes, before, hess, before_parts = call(
        stencil_kernel,
        (struct(2, 3, 16, 16, NZ), struct(16, 16, NZ), per_field(3), pltpu.VMEM((2, COLS, NZ), BF16)),
        24,
        1000,
        in_specs=[hbm] * 6,
        out_specs=(hbm,) * 3 + (near,),
        scratch_shapes=[
            scratch(5, 24, 16, NZ),
            scratch(5, 16, 32, NZ),
            scratch(5, 16, 4, NZ),
            scratch(5, 16, 4, NZ),
            scratch(2, 3, 16, 16, NZ),
            scratch(2, 16, 16, NZ),
            scratch(3, 16, 16, NZ),
            sems(14),
        ],
    )(state_path, velocity, *halos)

    supply = call(
        supply_kernel,
        struct(DEV * V_ROWS, 128),
        8,
        2,
        in_specs=[hbm, near],
        out_specs=hbm,
        scratch_shapes=[scratch(DEV, 128), scratch(DEV * V_ROWS, 128), sems(4)],
    )(asked, before_parts)
    arrived = exchange(supply.reshape(DEV, CAP, 2, 128)).reshape(DEV * V_ROWS, 128)

    normal, taken, weight0, before1, placed, wanted_t = call(
        normal_kernel,
        (
            scratch(4, COLS, NZ),
            pltpu.VMEM((COLS, CAP * DEV), BF16),
            pltpu.VMEM((4, 16, 16, NZ), BF16),
            scratch(COLS, NZ),
            pltpu.HBM((CAP * DEV, COLS), BF16),
            struct(16, 128),
        ),
        20,
        4,
        in_specs=[hbm] * 4,
        out_specs=(near,) * 4 + (hbm,) * 2,
        scratch_shapes=[
            scratch(DEV * A_ROWS, 128),
            scratch(4, CAP * DEV, NZ),
            pltpu.VMEM((1, COLS), jnp.int32),
            scratch(16, 128),
            pltpu.VMEM((CAP * DEV, COLS), BF16),
            sems(5),
        ],
    )(asked.reshape(DEV * A_ROWS, 128), owner_row, weights, before.reshape(COLS, NZ))

    lam, push = call(
        middle_kernel,
        (scratch(COLS, NZ), struct(DEV * V_ROWS, 128)),
        8,
        4,
        in_specs=[near] * 5 + [hbm],
        out_specs=(near, hbm),
        scratch_shapes=[
            pltpu.VMEM((CAP * DEV, COLS), BF16),
            scratch(DEV * V_ROWS, 128),
            pltpu.VMEM((2, COLS, NZ), BF16),
            scratch(16, 128),
            sems(4),
        ],
    )(arrived, normal, taken, weight0, before1, placed)
    returned = exchange(push.reshape(DEV, CAP, 2, 128)).reshape(DEV * V_ROWS, 128)

    hess, slope0, onehot = call(
        blend_kernel,
        (scratch(3, COLS, NZ), scratch(3, COLS, NZ), pltpu.VMEM((COLS, CAP * DEV), BF16)),
        8,
        3,
        in_specs=[near] + [hbm] * 3,
        out_specs=(near,) * 3,
        scratch_shapes=[scratch(16, 128), scratch(3, COLS, NZ), sems(4)],
    )(lam, wanted_t, hess.reshape(3, COLS, NZ), slopes.reshape(2, 3, COLS, NZ))
    out = call(
        final_kernel,
        struct(3, COLS, NZ),
        8,
        2,
        in_specs=[near] * 4,
        out_specs=hbm,
        scratch_shapes=[scratch(3, COLS, NZ), sems(3)],
    )(returned, onehot, hess, slope0)
    return out.reshape(3, 16, 16, NZ)


def solution(mesh):
    return jax.shard_map(
        per_device,
        mesh=mesh,
        in_specs=(
            P(None, "gx", "gy", None),
            P(None, "gx", "gy", None),
            P(None, None, "gx", "gy", None),
            P(None, "gx", "gy", None, None),
            P(None, "gx", "gy", None),
        ),
        out_specs=P(None, "gx", "gy", None),
        check_vma=False,
    )
```
